32 devices in a mesh: dp: 4 (over x, core), fsdp: 8 (over z, y).
Axes of the slice: x: 2, y: 2, z: 4, core: 2. Of those that a mesh axis runs over, the one named last changes fastest.
Arguments:
- text_in: bfloat16 [512, 64, 768], P(('dp', 'fsdp')), may hold values from -6 to 6
- text_segments: int32 [512, 64], P(('dp', 'fsdp')), may hold values from 0 to 8, never falling along the last dimension, each value on 1 to 32 neighbouring positions
- text_cotangent: bfloat16 [512, 64, 768], P(('dp', 'fsdp')), may hold values from -6 to 6
- image_in: bfloat16 [128, 50, 768], P(('dp', 'fsdp')), may hold values from -6 to 6
- ln1_gain: bfloat16 [768], P('fsdp'), may hold values from 0.25 to 1.75
- ln1_bias: bfloat16 [768], P('fsdp'), may hold values from -4 to 4
- w_qkv: bfloat16 [768, 2304], P('fsdp'), may hold values from -0.21875 to 0.21875
- q_bias: bfloat16 [768], P('fsdp'), may hold values from -4 to 4
- v_bias: bfloat16 [768], P('fsdp'), may hold values from -4 to 4
- w_out: bfloat16 [768, 768], P('fsdp'), may hold values from -0.625 to 0.625
- out_bias: bfloat16 [768], P('fsdp'), may hold values from -4 to 4
- ln2_gain: bfloat16 [768], P('fsdp'), may hold values from 0.25 to 1.75
- ln2_bias: bfloat16 [768], P('fsdp'), may hold values from -4 to 4
- w_fc1: bfloat16 [768, 3072], P('fsdp'), may hold values from -0.21875 to 0.21875
- fc1_bias: bfloat16 [3072], P('fsdp'), may hold values from -4 to 4
- w_fc2: bfloat16 [3072, 768], P('fsdp'), may hold values from -0.109375 to 0.109375
- fc2_bias: bfloat16 [768], P('fsdp'), may hold values from -4 to 4
- image_norms: bfloat16 [2, 768], P(None, 'fsdp'), may hold values from 0.25 to 1.75
- image_qkv: bfloat16 [768, 2304], P('fsdp'), may hold values from -0.21875 to 0.21875
- image_proj: bfloat16 [768, 768], P('fsdp'), may hold values from -0.625 to 0.625
- image_fc1: bfloat16 [768, 3072], P('fsdp'), may hold values from -0.21875 to 0.21875
- image_fc2: bfloat16 [3072, 768], P('fsdp'), may hold values from -0.109375 to 0.109375
Outputs:
- text_out: bfloat16 [512, 64, 768], P(('dp', 'fsdp'))
- image_out: bfloat16 [128, 50, 768], P(('dp', 'fsdp'))
- text_grad: float32 [512, 64, 768], P(('dp', 'fsdp'))
- grad_ln1_gain: float32 [768], P('fsdp')
- grad_ln1_bias: float32 [768], P('fsdp')
- grad_qkv: float32 [768, 2304], P('fsdp')
- grad_q_bias: float32 [768], P('fsdp')
- grad_v_bias: float32 [768], P('fsdp')
- grad_w_out: float32 [768, 768], P('fsdp')
- grad_out_bias: float32 [768], P('fsdp')
- grad_ln2_gain: float32 [768], P('fsdp')
- grad_ln2_bias: float32 [768], P('fsdp')
- grad_fc1: float32 [768, 3072], P('fsdp')
- grad_fc1_bias: float32 [3072], P('fsdp')
- grad_fc2: float32 [3072, 768], P('fsdp')
- grad_fc2_bias: float32 [768], P('fsdp')
The draws below stay inside these ranges and needn't reach their ends.
Inputs may be any that keep to these rules, and one draw needn't show every extreme that they name: `text_segments`: along each row ids never fall; each id covers 1 to 32 positions and every id from 0 to 8 appears in every row.
All inputs are finite; a program needn't handle non-finite values.
Results may differ from the reference program's by a relative error of at most 0.015.
Values may be sent and summed in bfloat16 or wider, within the bound.
No kernel may reach another device: no remote copies, remote signals or barrier semaphores. Data moves between devices by JAX's collectives and lax.ppermute only.
A program may use at most 256 MiB of HBM per device.

```python
import math
import jax
import jax.numpy as jnp
import numpy as np
from jax import lax

D = 768
HEADS = 12
HEAD_DIM = 64
FF = 3072
SEQ = 64
IMG_TOK = 50
TXT = 512
IMG = 128


def steps_of(key, extent, split, smallest, largest):
    factor_of = 1.0
    for position, blocks in split:
        draws = jax.random.uniform(jax.random.fold_in(jax.random.fold_in(key, 6), position), (blocks,), jnp.float32, smallest / len(split), largest / len(split))
        factor_of = factor_of * jnp.repeat(jnp.exp(draws), extent[position] // blocks).reshape((-1,) + (1,) * (len(extent) - 1 - position))
    return factor_of


def profile(count, total, limit, slope):
    weights = [(1 << 20) // math.isqrt(grade ** slope) + 1 for grade in range(2, count + 1)]
    rest, counts = total - limit - (count - 1), [1] * (count - 1)
    while rest > 0:
        free = [i for i in range(count - 1) if counts[i] < limit]
        whole, budget = sum([weights[i] for i in free]), rest
        for i in free:
            addition = min(limit - counts[i], max(1, budget * weights[i] // whole), rest)
            counts[i] = counts[i] + addition
            rest = rest - addition
    return np.array([limit] + counts)


def ragged(stream_key, number_of, total, bound, slope):
    if number_of == 2:
        one = jax.random.randint(stream_key, (), max(1, total - bound), min(bound, total - 1) + 1)
        return jnp.stack([one, total - one])
    sizes = jnp.asarray(profile(number_of, total, bound, slope), jnp.int32)
    twos = (number_of - 1) // 2
    source_of, receiver = sizes[1:1 + 2 * twos:2], sizes[2:2 + 2 * twos:2]
    slack = jnp.minimum(source_of - 1, bound - receiver)
    shifted = jax.random.randint(jax.random.fold_in(stream_key, 1), (twos,), 0, 1 << 20) % (slack + 1)
    sizes = sizes.at[1:1 + 2 * twos:2].set(source_of - shifted).at[2:2 + 2 * twos:2].set(receiver + shifted)
    return sizes[jax.random.permutation(jax.random.fold_in(stream_key, 2), number_of)]


def noise(stream_key, shape, width, reach, shards=(), dtype=jnp.bfloat16):
    factor_of = steps_of(stream_key, shape, shards, -0.22, 0.18) if shards else 1.0
    drawn = jax.random.normal(stream_key, shape, jnp.float32) * width * factor_of
    return jnp.minimum(jnp.maximum(drawn, -reach), reach).astype(dtype)


def setup_inputs(seed: int = 0) -> dict:
    keys = jax.random.split(jax.random.key(seed), 23)
    text_in = noise(keys[0], (TXT, SEQ, D), 1.0, 6.0, ((0, 32),))
    text_segments = jax.vmap(lambda own: jnp.searchsorted(jnp.cumsum(ragged(own, SEQ // 8 + 1, SEQ, SEQ // 2, 0)), jnp.arange(SEQ), side="right"))(jax.random.split(keys[1], TXT)).reshape((TXT, SEQ)).astype(jnp.int32)
    text_cotangent = noise(keys[2], (TXT, SEQ, D), 1.0, 6.0, ((0, 32),))
    image_in = noise(keys[3], (IMG, IMG_TOK, D), 1.0, 6.0, ((0, 32),))
    ln1_gain = jnp.clip(1.0 + 0.15 * jax.random.normal(keys[4], (D,), jnp.float32), 0.25, 1.75).astype(jnp.bfloat16)
    ln1_bias = noise(keys[5], (D,), 0.3, 4.0, ((0, 8),))
    w_qkv = noise(keys[6], (D, 3 * D), D ** -0.5, 0.21875, ((0, 8),))
    q_bias = noise(keys[7], (D,), 0.5, 4.0, ((0, 8),))
    v_bias = noise(keys[8], (D,), 0.3, 4.0, ((0, 8),))
    w_out = noise(keys[9], (D, D), (D // 8) ** -0.5, 0.625, ((0, 8),))
    out_bias = noise(keys[10], (D,), 0.3, 4.0, ((0, 8),))
    ln2_gain = jnp.clip(1.0 + 0.15 * jax.random.normal(keys[11], (D,), jnp.float32), 0.25, 1.75).astype(jnp.bfloat16)
    ln2_bias = noise(keys[12], (D,), 0.3, 4.0, ((0, 8),))
    w_fc1 = noise(keys[13], (D, FF), D ** -0.5, 0.21875, ((0, 8),))
    fc1_bias = noise(keys[14], (FF,), 0.3, 4.0, ((0, 8),))
    w_fc2 = noise(keys[15], (FF, D), FF ** -0.5, 0.109375, ((0, 8),))
    fc2_bias = noise(keys[16], (D,), 0.3, 4.0, ((0, 8),))
    image_norms = jnp.clip(1.0 + 0.15 * jax.random.normal(keys[17], (2, D), jnp.float32), 0.25, 1.75).astype(jnp.bfloat16)
    image_qkv = noise(keys[18], (D, 3 * D), D ** -0.5, 0.21875, ((0, 8),))
    image_proj = noise(keys[19], (D, D), (D // 8) ** -0.5, 0.625, ((0, 8),))
    image_fc1 = noise(keys[20], (D, FF), D ** -0.5, 0.21875, ((0, 8),))
    image_fc2 = noise(keys[21], (FF, D), FF ** -0.5, 0.109375, ((0, 8),))
    return dict(text_in=text_in, text_segments=text_segments, text_cotangent=text_cotangent, image_in=image_in, ln1_gain=ln1_gain, ln1_bias=ln1_bias, w_qkv=w_qkv, q_bias=q_bias, v_bias=v_bias, w_out=w_out, out_bias=out_bias, ln2_gain=ln2_gain, ln2_bias=ln2_bias, w_fc1=w_fc1, fc1_bias=fc1_bias, w_fc2=w_fc2, fc2_bias=fc2_bias, image_norms=image_norms, image_qkv=image_qkv, image_proj=image_proj, image_fc1=image_fc1, image_fc2=image_fc2)


@jax.custom_vjp
def low(v):
    return lax.optimization_barrier(v.astype(jnp.bfloat16)).astype(jnp.float32)

@jax.custom_vjp
def low_back(v):
    return v

def low_keep(v):
    return (low(v), None)

def low_pass(kept, grad):
    return (grad,)

def back_keep(v):
    return (v, None)

def back_low(kept, grad):
    return (low(grad),)
low.defvjp(low_keep, low_pass)
low_back.defvjp(back_keep, back_low)
highest = lax.Precision.HIGHEST
epsilon = 1e-06
group_rows = 32

def normed(values, scale_by, shift_by):
    centre = values - lax.optimization_barrier(jnp.mean(values, axis=-1, keepdims=True))
    spread = lax.rsqrt(lax.optimization_barrier(jnp.mean(centre * centre, axis=-1, keepdims=True)) + epsilon)
    return centre * spread * scale_by + shift_by

def block(inputs, allowed, norms, w_qkv, qkv_bias, w_out, out_bias, w_fc1, fc1_bias, w_fc2, fc2_bias):
    batch_rows, length, model_width = inputs.shape
    norm_one = low(normed(inputs, norms[0], norms[1]))
    joined = low(low_back(jnp.einsum('rsd,df->rsf', norm_one, w_qkv, precision=highest) + qkv_bias))
    parted = joined.reshape(batch_rows, length, 3, HEADS, HEAD_DIM)
    scores = low_back(jnp.einsum('rqhe,rkhe->rhqk', parted[:, :, 0], parted[:, :, 1], precision=highest) * HEAD_DIM ** (-0.5))
    if allowed is not None:
        scores = jnp.where(allowed[:, None], scores, -1e+30)
    attend = low(jax.nn.softmax(scores, axis=-1))
    mixed_heads = jnp.einsum('rhqk,rkhe->rqhe', attend, parted[:, :, 2], precision=highest)
    mixed_heads = low(low_back(mixed_heads.reshape(batch_rows, length, model_width)))
    hidden = inputs + low_back(jnp.einsum('rsd,de->rse', mixed_heads, w_out, precision=highest) + out_bias)
    norm_two = low(normed(hidden, norms[2], norms[3]))
    pre_act = low_back(jnp.einsum('rsd,df->rsf', norm_two, w_fc1, precision=highest) + fc1_bias)
    active = low(jax.nn.gelu(pre_act, approximate=False))
    return hidden + low_back(jnp.einsum('rsf,fd->rsd', active, w_fc2, precision=highest) + fc2_bias)

def text_block(inputs, segment_ids, weights):
    zeros_mid = jnp.zeros_like(weights[3])
    allowed = segment_ids[:, :, None] == segment_ids[:, None, :]
    qkv_bias = jnp.concatenate([weights[3], zeros_mid, weights[4]])
    norms = (weights[0], weights[1], weights[7], weights[8])
    return block(inputs, allowed, norms, weights[2], qkv_bias, weights[5], weights[6], weights[9], weights[10], weights[11], weights[12])

def reference(text_in, text_segments, text_cotangent, image_in, ln1_gain, ln1_bias, w_qkv, q_bias, v_bias, w_out, out_bias, ln2_gain, ln2_bias, w_fc1, fc1_bias, w_fc2, fc2_bias, image_norms, image_qkv, image_proj, image_fc1, image_fc2):
    params = tuple((item.astype(jnp.float32) for item in (ln1_gain, ln1_bias, w_qkv, q_bias, v_bias, w_out, out_bias, ln2_gain, ln2_bias, w_fc1, fc1_bias, w_fc2, fc2_bias)))
    groups = TXT // group_rows
    input_groups = text_in.reshape(groups, group_rows, SEQ, D)
    id_groups = text_segments.reshape(groups, group_rows, SEQ)
    cot_groups = text_cotangent.reshape(groups, group_rows, SEQ, D)

    def one_group(carry, pieces):
        group_in, group_ids, group_cot = pieces
        result, pullback = jax.vjp(lambda values, weights: text_block(values, group_ids, weights), group_in.astype(jnp.float32), params)
        grad_in, grad_weights = pullback(group_cot.astype(jnp.float32))
        carry = tuple((total_part + added_part for total_part, added_part in zip(carry, grad_weights)))
        return (carry, (result.astype(jnp.bfloat16), grad_in))
    start = tuple((jnp.zeros_like(item) for item in params))
    sums, (text_out, text_grad) = lax.scan(one_group, start, (input_groups, id_groups, cot_groups))
    image_norm_f = image_norms.astype(jnp.float32)
    image_mats = tuple((item.astype(jnp.float32) for item in (image_qkv, image_proj, image_fc1, image_fc2)))

    def image_group(group_in):
        norms = (image_norm_f[0], 0.0, image_norm_f[1], 0.0)
        result = block(group_in.astype(jnp.float32), None, norms, image_mats[0], 0.0, image_mats[1], 0.0, image_mats[2], 0.0, image_mats[3], 0.0)
        return result.astype(jnp.bfloat16)
    image_out = lax.map(image_group, image_in.reshape(IMG // group_rows, group_rows, IMG_TOK, D)).reshape(IMG, IMG_TOK, D)
    return (text_out.reshape(TXT, SEQ, D), image_out, text_grad.reshape(TXT, SEQ, D), sums[0], sums[1], sums[2], sums[3], sums[4], sums[5], sums[6], sums[7], sums[8], sums[9], sums[10], sums[11], sums[12])
```

```python
from functools import partial

import jax
import jax.numpy as jnp
from jax import lax
from jax.experimental import pallas as pl
from jax.experimental.pallas import tpu as pltpu
from jax.sharding import PartitionSpec as P

HEADS = 12
EPSILON = 1e-06
LANES = 128
TILE = 256
MIB = 1024 * 1024
F32 = jnp.float32
BF16 = jnp.bfloat16

LN1_GAIN, LN1_BIAS, Q_BIAS, V_BIAS, OUT_BIAS, LN2_GAIN, LN2_BIAS, FC2_BIAS = range(8)
IMAGE_GAIN_ONE, IMAGE_GAIN_TWO, FC1_BIAS = 8, 9, 10
VECTOR_ROWS = 16


def dot_nn(a, b):
    return lax.dot_general(a, b, (((1,), (0,)), ((), ())), preferred_element_type=F32)


def dot_nt(a, b):
    return lax.dot_general(a, b, (((1,), (1,)), ((), ())), preferred_element_type=F32)


def dot_tn(a, b):
    return lax.dot_general(a, b, (((0,), (0,)), ((), ())), preferred_element_type=F32)


def call(body, name, flops, moved, **kwargs):
    return pl.pallas_call(
        body,
        name=name,
        compiler_params=pltpu.CompilerParams(vmem_limit_bytes=60 * MIB),
        cost_estimate=pl.CostEstimate(
            flops=int(flops), bytes_accessed=int(moved), transcendentals=0
        ),
        **kwargs,
    )


class Part:
    def __init__(self, name, start, width, folds):
        self.name, self.start, self.width, self.folds = name, start, width, folds


def pack_parts(shapes, n_fsdp):
    parts, at = {}, 0
    for name, (rows, columns), model in shapes:
        folds = rows // model
        parts[name] = Part(name, at, columns // 2, folds)
        at += folds * (columns // 2)
    return parts, at


def own_piece(matrix, folds, x, core):
    rows, columns = matrix.shape
    half = rows // 2
    piece = lax.dynamic_slice(matrix, (x * half, core * (columns // 2)), (half, columns // 2))
    if folds > 1:
        step = half // folds
        piece = jnp.concatenate([piece[k * step : (k + 1) * step] for k in range(folds)], axis=1)
    return piece


class Whole:
    def __init__(self, arrays):
        self.arrays = arrays

    def operands(self, names):
        return [self.arrays[name] for name in names]

    def start(self, refs, place, names, targets, semaphores):
        for ref, name in zip(refs, names):
            pltpu.make_async_copy(ref, targets[name], semaphores[name]).start()


def start_piece(source, parts, names, targets, semaphores, f, x, core):
    for name in names:
        part = parts[name]
        height = source.shape[0]
        first = f * (2 * part.folds * height) + x * (part.folds * height)
        for fold in range(part.folds):
            columns = part.start + fold * part.width
            pltpu.make_async_copy(
                source.at[:, pl.ds(columns, part.width)],
                targets[name].at[
                    pl.ds(pl.multiple_of(first + fold * height, 16), height),
                    pl.ds(pl.multiple_of(core * part.width, LANES), part.width),
                ],
                semaphores[name],
            ).start()


class Relative:
    def __init__(self, parts, buffers):
        self.parts, self.buffers = parts, buffers

    def operands(self, names):
        return [array for array, _ in self.buffers]

    def start(self, refs, place, names, targets, semaphores):
        f, x, core = place
        for ref, (_, (high, dy, dx, dc)) in zip(refs, self.buffers):
            for low in range(2):
                start_piece(
                    ref.at[low],
                    self.parts,
                    names,
                    targets,
                    semaphores,
                    f ^ (dy + 2 * (2 * high + low)),
                    x ^ dx,
                    core ^ dc,
                )


class Listed:
    def __init__(self, parts, array):
        self.parts, self.array = parts, array

    def operands(self, names):
        return [self.array]

    def start(self, refs, place, names, targets, semaphores):
        (ref,) = refs

        def step(i, carry):
            start_piece(
                ref.at[i], self.parts, names, targets, semaphores, i // 4, (i // 2) % 2, i % 2
            )
            return carry

        lax.fori_loop(0, ref.shape[0], step, 0)


class Loader:
    def __init__(self, wanted, shapes):
        self.wanted, self.shapes = wanted, shapes
        self.names = [name for _, names in wanted for name in names]
        self.arrays = [a for source, names in wanted for a in source.operands(names)]
        self.specs = [pl.BlockSpec(memory_space=pl.ANY)] * len(self.arrays)
        self.scratch = [pltpu.VMEM(shapes[name], BF16) for name in self.names] + [
            pltpu.SemaphoreType.DMA((len(self.names),))
        ]
        self.bytes = sum(2 * shapes[name][0] * shapes[name][1] for name in self.names)

    def bind(self, refs, scratch, place_ref):
        self.refs = refs
        self.targets = dict(zip(self.names, scratch))
        self.semaphores = {name: scratch[-1].at[i] for i, name in enumerate(self.names)}
        self.place = (place_ref[0], place_ref[1], place_ref[2])
        return self

    def start(self):
        at = 0
        for source, names in self.wanted:
            count = len(source.operands(names))
            source.start(
                self.refs[at : at + count], self.place, names, self.targets, self.semaphores
            )
            at += count

    def wait(self, name):
        target = self.targets[name]
        pltpu.make_async_copy(target, target, self.semaphores[name]).wait()


def normed(values, gain, shift):
    centre = values - jnp.mean(values, axis=-1, keepdims=True)
    spread = lax.rsqrt(jnp.mean(centre * centre, axis=-1, keepdims=True) + EPSILON)
    return centre * spread * gain + shift


def norm_back(values, gain, grad):
    centre = values - jnp.mean(values, axis=-1, keepdims=True)
    spread = lax.rsqrt(jnp.mean(centre * centre, axis=-1, keepdims=True) + EPSILON)
    scaled = centre * spread
    grad_gain = jnp.sum(grad * scaled, axis=0, keepdims=True)
    grad_shift = jnp.sum(grad, axis=0, keepdims=True)
    inner = grad * gain
    inner = inner - jnp.mean(inner, axis=-1, keepdims=True) - scaled * jnp.mean(
        inner * scaled, axis=-1, keepdims=True
    )
    return inner * spread, grad_gain, grad_shift


def lane_sides(scale=1.0):
    lane = lax.broadcasted_iota(jnp.int32, (LANES, LANES), 1)
    left = jnp.where(lane < LANES // 2, scale, 0.0)
    return left.astype(BF16), (scale - left).astype(BF16)


def by_head(values, sides):
    return jnp.concatenate([values * sides[0], values * sides[1]], axis=0)


def attention(queries, keys, values, allowed, sides, key_sides):
    scores = dot_nt(queries, by_head(keys, key_sides))
    weights = []
    for head in range(2):
        own = jnp.where(allowed, scores[:, head * LANES : (head + 1) * LANES], -1e30)
        raised = jnp.exp(own - jnp.max(own, axis=-1, keepdims=True))
        weights.append(raised / jnp.sum(raised, axis=-1, keepdims=True))
    weights = jnp.concatenate(weights, axis=1).astype(BF16)
    return weights, dot_nn(weights, by_head(values, sides))


def gelu_both(values):
    below = 0.5 + 0.5 * lax.erf(values * 0.7071067811865476)
    bell = jnp.exp(values * values * -0.5) * 0.3989422804014327
    return values * below, below + values * bell


def text_attend_body(loader, n_sources, width, place, x_ref, ids_ref, vec_ref, *rest):
    sources, rest = rest[:n_sources], rest[n_sources:]
    normed_ref, joined_ref, mixed_ref, weights_ref = rest[:4]
    load = loader.bind(sources, rest[4:], place)

    @pl.when(pl.program_id(0) == 0)
    def _():
        load.start()
        load.wait("qkv")

    w_qkv = load.targets["qkv"]
    values = x_ref[...].astype(F32)
    norm_one = normed(
        values, vec_ref[LN1_GAIN : LN1_GAIN + 1, :], vec_ref[LN1_BIAS : LN1_BIAS + 1, :]
    ).astype(BF16)
    normed_ref[...] = norm_one
    for third, bias in enumerate((Q_BIAS, None, V_BIAS)):
        columns = slice(third * width, (third + 1) * width)
        product = dot_nn(norm_one, w_qkv[:, columns])
        if bias is not None:
            product = product + vec_ref[bias : bias + 1, :]
        joined_ref[:, columns] = product.astype(BF16)
    sides, key_sides = lane_sides(), lane_sides((width // HEADS) ** -0.5)
    for part in range(x_ref.shape[0] // LANES):
        rows = slice(part * LANES, (part + 1) * LANES)
        ids = jnp.broadcast_to(ids_ref[part], (LANES, LANES))
        allowed = ids == ids.T
        for pair in range(width // LANES):
            one = slice(pair * LANES, (pair + 1) * LANES)
            two = slice(width + pair * LANES, width + (pair + 1) * LANES)
            three = slice(2 * width + pair * LANES, 2 * width + (pair + 1) * LANES)
            weights, mixed = attention(
                joined_ref[rows, one],
                joined_ref[rows, two],
                joined_ref[rows, three],
                allowed,
                sides,
                key_sides,
            )
            weights_ref[part, pair] = weights
            mixed_ref[rows, one] = mixed.astype(BF16)


def text_hidden_body(loader, n_sources, place, x_ref, mixed_ref, vec_ref, fc1_bias_ref, *rest):
    sources, rest = rest[:n_sources], rest[n_sources:]
    hidden_ref, norm_two_ref, active_ref, slope_ref = rest[:4]
    load = loader.bind(sources, rest[4:], place)

    @pl.when(pl.program_id(0) == 0)
    def _():
        load.start()
        load.wait("out")
        load.wait("fc1")

    w_out, w_fc1 = load.targets["out"], load.targets["fc1"]
    hidden = (
        x_ref[...].astype(F32)
        + dot_nn(mixed_ref[...], w_out[...])
        + vec_ref[OUT_BIAS : OUT_BIAS + 1, :]
    )
    hidden_ref[...] = hidden
    norm_two = normed(
        hidden, vec_ref[LN2_GAIN : LN2_GAIN + 1, :], vec_ref[LN2_BIAS : LN2_BIAS + 1, :]
    ).astype(BF16)
    norm_two_ref[...] = norm_two
    step = hidden.shape[1]
    for k in range(w_fc1.shape[1] // step):
        columns = slice(k * step, (k + 1) * step)
        pre_act = dot_nn(norm_two, w_fc1[:, columns]) + fc1_bias_ref[:, columns]
        active, slope = gelu_both(pre_act)
        active_ref[:, columns] = active.astype(BF16)
        slope_ref[:, columns] = slope.astype(BF16)


def text_back_body(loader, n_sources, place, g_ref, hidden_ref, active_ref, slope_ref, vec_ref, *rest):
    sources, rest = rest[:n_sources], rest[n_sources:]
    out_ref, pre_ref, d_hidden_ref, dy1_ref, d_mixed_ref, sums_ref, wide_ref = rest[:7]
    load = loader.bind(sources, rest[7:], place)
    first = pl.program_id(0) == 0

    @pl.when(first)
    def _():
        load.start()
        for name in load.names:
            load.wait(name)
        sums_ref[...] = jnp.zeros_like(sums_ref)
        wide_ref[...] = jnp.zeros_like(wide_ref)

    w_out, w_fc1, w_fc2 = (load.targets[name] for name in ("out", "fc1", "fc2"))
    g = g_ref[...]
    hidden = hidden_ref[...]
    out_ref[...] = (
        hidden + dot_nn(active_ref[...], w_fc2[...]) + vec_ref[FC2_BIAS : FC2_BIAS + 1, :]
    ).astype(BF16)
    step = hidden.shape[1]
    d_norm = jnp.zeros(hidden.shape, F32)
    for k in range(w_fc1.shape[1] // step):
        columns = slice(k * step, (k + 1) * step)
        d_pre = dot_nt(g, w_fc2[columns, :]) * slope_ref[:, columns].astype(F32)
        low = d_pre.astype(BF16)
        pre_ref[:, columns] = low
        wide_ref[0:1, columns] += jnp.sum(low.astype(F32), axis=0, keepdims=True)
        d_norm = d_norm + dot_nt(low, w_fc1[:, columns])
    part, gain, shift = norm_back(hidden, vec_ref[LN2_GAIN : LN2_GAIN + 1, :], d_norm)
    d_hidden = g.astype(F32) + part
    d_hidden_ref[...] = d_hidden
    dy1 = d_hidden.astype(BF16)
    dy1_ref[...] = dy1
    d_mixed_ref[...] = dot_nt(dy1, w_out[...]).astype(BF16)
    sums_ref[LN2_GAIN : LN2_GAIN + 1, :] += gain
    sums_ref[LN2_BIAS : LN2_BIAS + 1, :] += shift
    sums_ref[OUT_BIAS : OUT_BIAS + 1, :] += jnp.sum(dy1.astype(F32), axis=0, keepdims=True)
    sums_ref[FC2_BIAS : FC2_BIAS + 1, :] += jnp.sum(g.astype(F32), axis=0, keepdims=True)


def text_unjoin_body(
    loader, n_sources, width, place, x_ref, joined_ref, weights_ref, d_mixed_ref, d_hidden_ref, vec_ref, *rest
):
    sources, rest = rest[:n_sources], rest[n_sources:]
    d_joined_ref, grad_ref, sums_ref = rest[:3]
    load = loader.bind(sources, rest[3:], place)

    @pl.when(pl.program_id(0) == 0)
    def _():
        load.start()
        load.wait("qkv")
        sums_ref[...] = jnp.zeros_like(sums_ref)

    w_qkv = load.targets["qkv"]
    scale = (width // HEADS) ** -0.5
    sides, key_sides = lane_sides(), lane_sides(scale)
    left = lax.broadcasted_iota(jnp.int32, (LANES, LANES), 1) < LANES // 2
    for part in range(x_ref.shape[0] // LANES):
        rows = slice(part * LANES, (part + 1) * LANES)
        for pair in range(width // LANES):
            one = slice(pair * LANES, (pair + 1) * LANES)
            two = slice(width + pair * LANES, width + (pair + 1) * LANES)
            three = slice(2 * width + pair * LANES, 2 * width + (pair + 1) * LANES)
            low = weights_ref[part, pair]
            d_mixed = d_mixed_ref[rows, one]
            d_weights = dot_nt(d_mixed, by_head(joined_ref[rows, three], sides))
            d_scores = []
            for head in range(2):
                lanes = slice(head * LANES, (head + 1) * LANES)
                own, grad = low[:, lanes].astype(F32), d_weights[:, lanes]
                total = jnp.sum(grad * own, axis=-1, keepdims=True)
                total = total / jnp.sum(own, axis=-1, keepdims=True)
                d_scores.append(own * (grad - total))
            d_scores = jnp.concatenate(d_scores, axis=1).astype(BF16)
            d_joined_ref[rows, one] = dot_nn(
                d_scores, by_head(joined_ref[rows, two], key_sides)
            ).astype(BF16)
            d_keys = dot_tn(d_scores, joined_ref[rows, one]) * scale
            d_joined_ref[rows, two] = jnp.where(left, d_keys[:LANES], d_keys[LANES:]).astype(BF16)
            d_values = dot_tn(low, d_mixed)
            d_joined_ref[rows, three] = jnp.where(
                left, d_values[:LANES], d_values[LANES:]
            ).astype(BF16)
    d_joined = d_joined_ref[...]
    d_norm = dot_nt(d_joined, w_qkv[...])
    part, gain, shift = norm_back(
        x_ref[...].astype(F32), vec_ref[LN1_GAIN : LN1_GAIN + 1, :], d_norm
    )
    grad_ref[...] = d_hidden_ref[...] + part
    sums_ref[LN1_GAIN : LN1_GAIN + 1, :] += gain
    sums_ref[LN1_BIAS : LN1_BIAS + 1, :] += shift
    for row, third in ((Q_BIAS, 0), (V_BIAS, 2)):
        columns = d_joined_ref[:, third * width : (third + 1) * width].astype(F32)
        sums_ref[row : row + 1, :] += jnp.sum(columns, axis=0, keepdims=True)


def image_body(loader, n_sources, width, tokens, padded, place, x_ref, vec_ref, *rest):
    sources, rest = rest[:n_sources], rest[n_sources:]
    out_ref, joined_ref, mixed_ref, hidden_ref = rest[:4]
    load = loader.bind(sources, rest[4:], place)
    load.start()
    values = x_ref[...].astype(F32)
    norm_one = normed(values, vec_ref[IMAGE_GAIN_ONE : IMAGE_GAIN_ONE + 1, :], 0.0).astype(BF16)
    load.wait("qkv")
    w_qkv = load.targets["qkv"]
    for third in range(3):
        columns = slice(third * width, (third + 1) * width)
        joined_ref[:, columns] = dot_nn(norm_one, w_qkv[:, columns]).astype(BF16)
    sides, key_sides = lane_sides(), lane_sides((width // HEADS) ** -0.5)
    row = lax.broadcasted_iota(jnp.int32, (LANES, LANES), 0)
    column = lax.broadcasted_iota(jnp.int32, (LANES, LANES), 1)
    allowed = (row // padded == column // padded) & (column % padded < tokens)
    for part in range(x_ref.shape[0] // LANES):
        rows = slice(part * LANES, (part + 1) * LANES)
        for pair in range(width // LANES):
            one = slice(pair * LANES, (pair + 1) * LANES)
            two = slice(width + pair * LANES, width + (pair + 1) * LANES)
            three = slice(2 * width + pair * LANES, 2 * width + (pair + 1) * LANES)
            _, mixed = attention(
                joined_ref[rows, one],
                joined_ref[rows, two],
                joined_ref[rows, three],
                allowed,
                sides,
                key_sides,
            )
            mixed_ref[rows, one] = mixed.astype(BF16)
    load.wait("out")
    hidden = values + dot_nn(mixed_ref[...], load.targets["out"][...])
    norm_two = normed(hidden, vec_ref[IMAGE_GAIN_TWO : IMAGE_GAIN_TWO + 1, :], 0.0).astype(BF16)
    hidden_ref[...] = hidden
    load.wait("fc1")
    load.wait("fc2")
    w_fc1, w_fc2 = load.targets["fc1"], load.targets["fc2"]
    for k in range(w_fc1.shape[1] // width):
        columns = slice(k * width, (k + 1) * width)
        pre_act = dot_nn(norm_two, w_fc1[:, columns])
        active = (pre_act * (0.5 + 0.5 * lax.erf(pre_act * 0.7071067811865476))).astype(BF16)
        hidden_ref[...] += dot_nn(active, w_fc2[columns, :])
    out_ref[...] = hidden_ref[...].astype(BF16)


SLOTS = 16


def slot_place(slot, f, x):
    dy, dx, dz = slot // 8, (slot // 4) % 2, slot % 4
    return f ^ (dy + 2 * dz), x ^ dx


def grad_columns_body(place, left_ref, own_in, other_in, own_out, other_out, turned, total):
    @pl.when(pl.program_id(0) == 0)
    def _():
        turned[...] = left_ref[...].T

    height = own_out.shape[1]
    for right, out in ((other_in, other_out), (own_in, own_out)):
        total[...] = dot_nn(turned[...], right[...])
        for slot in range(SLOTS):
            f, x = slot_place(slot, place[0], place[1])
            rows = pl.ds(pl.multiple_of((f * 2 + x) * height, 16), height)
            out[slot] = total[rows, :].astype(BF16)


def grad_columns(place, left, right, name):
    tokens, model = left.shape
    columns = right.shape[1]
    width = columns // 2
    steps = width // 384
    block = width // steps
    height = model // SLOTS

    def own_block(j, place):
        return (0, place[2] * steps + j)

    def other_block(j, place):
        return (0, (1 - place[2]) * steps + j)

    out = jax.ShapeDtypeStruct((SLOTS, height, width), BF16)
    return call(
        grad_columns_body,
        name,
        2 * tokens * model * columns,
        2 * tokens * (model + columns) + 2 * model * columns,
        grid_spec=pltpu.PrefetchScalarGridSpec(
            num_scalar_prefetch=1,
            grid=(steps,),
            in_specs=[
                pl.BlockSpec((tokens, model), lambda j, place: (0, 0)),
                pl.BlockSpec((tokens, block), own_block),
                pl.BlockSpec((tokens, block), other_block),
            ],
            out_specs=[pl.BlockSpec((SLOTS, height, block), lambda j, place: (0, 0, j))] * 2,
            scratch_shapes=[pltpu.VMEM((model, tokens), BF16), pltpu.VMEM((model, block), F32)],
        ),
        out_shape=(out, out),
    )(place, left, right, right)


def grad_rows_body(place, left_ref, right_ref, own_out, other_out):
    total = dot_tn(left_ref[...], right_ref[...])
    half_rows, half_columns = total.shape[0] // 2, total.shape[1] // 2
    height = own_out.shape[3]
    first_x, first_core = place[1] == 0, place[2] == 0
    sides = (total[:, :half_columns], total[:, half_columns:])
    own = jnp.where(first_core, sides[0], sides[1]).astype(BF16)
    other = jnp.where(first_core, sides[1], sides[0]).astype(BF16)
    for value, out in ((other, other_out), (own, own_out)):
        ends = (value[:half_rows], value[half_rows:])
        for dx in range(2):
            rows = jnp.where(first_x, ends[dx], ends[1 - dx])
            for fold in range(half_rows // height):
                out[0, dx, 0, :, fold * half_columns : (fold + 1) * half_columns] = rows[
                    fold * height : (fold + 1) * height
                ]


def grad_rows(place, left, right, n_fsdp, name):
    tokens, columns = right.shape
    rows = left.shape[1] // n_fsdp
    folds = left.shape[1] // columns
    height, width = rows // (2 * folds), folds * columns // 2

    def left_block(i, place):
        return (0, place[0] ^ (i // 4 + 2 * (i % 4)))

    out = jax.ShapeDtypeStruct((2, 2, 4, height, width), BF16)
    own, other = call(
        grad_rows_body,
        name,
        2 * tokens * left.shape[1] * columns,
        2 * tokens * (left.shape[1] + columns) + 2 * left.shape[1] * columns,
        grid_spec=pltpu.PrefetchScalarGridSpec(
            num_scalar_prefetch=1,
            grid=(n_fsdp,),
            in_specs=[
                pl.BlockSpec((tokens, rows), left_block),
                pl.BlockSpec((tokens, columns), lambda i, place: (0, 0)),
            ],
            out_specs=[
                pl.BlockSpec((1, 2, 1, height, width), lambda i, place: (i // 4, 0, i % 4, 0, 0))
            ]
            * 2,
        ),
        out_shape=(out, out),
    )(place, left, right)
    return own.reshape(SLOTS, height, width), other.reshape(SLOTS, height, width)


def add_pairs_body(n_pairs, *refs):
    ins, outs = refs[: 2 * n_pairs], refs[2 * n_pairs :]
    at = 0
    for own, came in zip(ins[0::2], ins[1::2]):
        width = own.shape[2]
        value = (own[...].astype(F32) + came[...].astype(F32)).astype(BF16)
        for i, out in enumerate(outs):

            @pl.when(pl.program_id(0) == i)
            def _():
                out[:, :, at : at + width] = value

        at += width


def add_pairs(pairs, name):
    slots, height, _ = pairs[0][0].shape
    steps = slots // 2
    width = sum(own.shape[2] for own, _ in pairs)
    out = jax.ShapeDtypeStruct((2, height, width), BF16)
    return call(
        partial(add_pairs_body, len(pairs)),
        name,
        slots * height * width,
        6 * slots * height * width,
        grid=(steps,),
        in_specs=[
            pl.BlockSpec((2, height, array.shape[2]), lambda i: (i, 0, 0))
            for pair in pairs
            for array in pair
        ],
        out_specs=[pl.BlockSpec((2, height, width), lambda i: (0, 0, 0))] * steps,
        out_shape=[out] * steps,
    )(*[array for pair in pairs for array in pair])


def swap(value, axis, bit):
    size = lax.axis_size(axis)
    return lax.ppermute(value, axis, [(i, i ^ bit) for i in range(size)])


def gather_pieces(own):
    s0 = jnp.stack([own, swap(own, "fsdp", 2)])
    s1 = swap(s0, "fsdp", 4)
    y0, x0 = swap(s0, "fsdp", 1), swap(s0, "dp", 2)
    y1, x1 = swap(s1, "fsdp", 1), swap(s1, "dp", 2)
    d0, d1 = swap(y0, "dp", 2), swap(x1, "fsdp", 1)
    here = [
        (s0, (0, 0, 0)),
        (s1, (1, 0, 0)),
        (y0, (0, 1, 0)),
        (y1, (1, 1, 0)),
        (x0, (0, 0, 1)),
        (x1, (1, 0, 1)),
        (d0, (0, 1, 1)),
        (d1, (1, 1, 1)),
    ]
    return [(a, at + (0,)) for a, at in here] + [(swap(a, "dp", 1), at + (1,)) for a, at in here]


def plus(a, b):
    return (a.astype(F32) + b.astype(F32)).astype(a.dtype)


def reduce_pieces(pairs, name):
    came = [(own, swap(other, "dp", 1)) for own, other in pairs]
    s0, s1, x0, x1, y0, y1, d0, d1 = add_pairs(came, name)
    y0 = plus(y0, swap(d0, "dp", 2))
    x1 = plus(x1, swap(d1, "fsdp", 1))
    x0, y1 = swap(x0, "dp", 2), swap(y1, "fsdp", 1)
    x1, y0 = swap(x1, "dp", 2), swap(y0, "fsdp", 1)
    s1 = (s1.astype(F32) + x1.astype(F32) + y1.astype(F32)).astype(BF16)
    s0 = s0.astype(F32) + x0.astype(F32) + y0.astype(F32)
    came = swap(s1, "fsdp", 4)
    send = (s0[1] + came[1].astype(F32)).astype(BF16)
    keep = s0[0] + came[0].astype(F32)
    total = (keep + swap(send, "fsdp", 2).astype(F32)).astype(BF16)
    both = jnp.stack([total, swap(total, "dp", 2)])
    return both, swap(both, "dp", 1)


def unpack(both, other, x, core, start, width, folds):
    def rows(pieces):
        pieces = pieces[:, :, start : start + folds * width]
        pieces = jnp.where(x == 0, pieces, pieces[::-1])
        height = pieces.shape[1]
        pieces = pieces.reshape(2, height, folds, width).transpose(0, 2, 1, 3)
        return pieces.reshape(2 * folds * height, width)

    one, two = rows(both).astype(F32), rows(other).astype(F32)
    first = core == 0
    return jnp.concatenate([jnp.where(first, one, two), jnp.where(first, two, one)], axis=1)


def gather_vectors(own, f):
    bits = lax.axis_size("fsdp").bit_length() - 1
    order = [2, 4, 1] if bits == 3 else [1 << b for b in range(bits)]
    held = own
    for bit in order:
        held = jnp.stack([held, swap(held, "fsdp", bit)])
    for axis, bit in enumerate(reversed(order)):
        held = jnp.where((f & bit) != 0, jnp.flip(held, axis), held)
    wanted = sorted(range(bits), key=lambda axis: -order[::-1][axis])
    held = held.transpose(bits, *wanted, bits + 1)
    return held.reshape(own.shape[0], -1)


def reduce_vectors(sums, f):
    n = lax.axis_size("fsdp")
    rows = sums.shape[0]
    held = sums.reshape(rows, n, -1).transpose(1, 0, 2)
    bit = n // 2
    while bit:
        halves = held.reshape(2, bit, *held.shape[1:])
        upper = (f & bit) != 0
        send = jnp.where(upper, halves[0], halves[1])
        keep = jnp.where(upper, halves[1], halves[0])
        held = keep + swap(send, "fsdp", bit)
        bit //= 2
    held = held[0]
    bit = 1
    while bit < lax.axis_size("dp"):
        held = held + swap(held, "dp", bit)
        bit *= 2
    return held


def per_device(
    text_in,
    text_segments,
    text_cotangent,
    image_in,
    ln1_gain,
    ln1_bias,
    w_qkv,
    q_bias,
    v_bias,
    w_out,
    out_bias,
    ln2_gain,
    ln2_bias,
    w_fc1,
    fc1_bias,
    w_fc2,
    fc2_bias,
    image_norms,
    image_qkv,
    image_proj,
    image_fc1,
    image_fc2,
):
    n_fsdp, n_dp = lax.axis_size("fsdp"), lax.axis_size("dp")
    batch_rows, length, model = text_in.shape
    hidden_units = w_fc1.shape[1]
    tokens = batch_rows * length
    folds = hidden_units // model
    f, replica = lax.axis_index("fsdp"), lax.axis_index("dp")
    x, core = replica // 2, replica % 2
    place = jnp.stack([f, x, core]).astype(jnp.int32)
    shard = model // n_fsdp
    by_pieces = n_fsdp == 8 and n_dp == 4 and shard % 32 == 0

    shapes = {
        "qkv": (model, 3 * model),
        "out": (model, model),
        "fc1": (model, hidden_units),
        "fc2": (hidden_units, model),
    }
    text = {"qkv": w_qkv, "out": w_out, "fc1": w_fc1, "fc2": w_fc2}
    image = {"qkv": image_qkv, "out": image_proj, "fc1": image_fc1, "fc2": image_fc2}

    def packed(matrices, names):
        parts, _ = pack_parts([(name, shapes[name], model) for name in names], n_fsdp)
        return parts, jnp.concatenate(
            [own_piece(matrices[name], parts[name].folds, x, core) for name in names], axis=1
        )

    vectors = jnp.concatenate(
        [
            jnp.stack(
                [ln1_gain, ln1_bias, q_bias, v_bias, out_bias, ln2_gain, ln2_bias, fc2_bias]
            ),
            image_norms,
            fc1_bias.reshape(folds, shard),
        ]
    )
    vectors = jnp.pad(vectors, ((0, VECTOR_ROWS - vectors.shape[0]), (0, 0)))
    if by_pieces:
        parts, own = packed(text, ("qkv",))
        text_first = Relative(parts, gather_pieces(own))
        vectors = gather_vectors(vectors, f).astype(F32)
        parts, own = packed(text, ("out", "fc1", "fc2"))
        text_rest = Listed(parts, lax.all_gather(own, ("fsdp", "dp")))
        parts, own = packed(image, ("qkv", "out", "fc1", "fc2"))
        image_source = Listed(parts, lax.all_gather(own, ("fsdp", "dp")))
    else:
        vectors = lax.all_gather(vectors, "fsdp", axis=1, tiled=True).astype(F32)
        gathered = {n: lax.all_gather(a, "fsdp", axis=0, tiled=True) for n, a in text.items()}
        text_first = text_rest = Whole(gathered)
        image_source = Whole(
            {n: lax.all_gather(a, "fsdp", axis=0, tiled=True) for n, a in image.items()}
        )
    fc1_vector = vectors[FC1_BIAS : FC1_BIAS + folds].reshape(folds, n_fsdp, shard)
    fc1_vector = fc1_vector.transpose(1, 0, 2).reshape(1, hidden_units)

    inflow = text_in.reshape(tokens, model)
    cotangent = text_cotangent.reshape(tokens, model)
    ids = text_segments + 16 * (lax.broadcasted_iota(jnp.int32, text_segments.shape, 0) % (LANES // length))
    ids = ids.astype(F32).reshape(tokens // LANES, 1, LANES)
    steps = tokens // TILE
    groups = TILE // LANES
    pairs = model // LANES

    def rows_of(width):
        return pl.BlockSpec((TILE, width), lambda i, place: (i, 0))

    def fixed(*shape):
        return pl.BlockSpec(shape, lambda i, place: (0,) * len(shape))

    def array(*shape, dtype=BF16):
        return jax.ShapeDtypeStruct(shape, dtype)

    weights_spec = pl.BlockSpec((groups, pairs, LANES, 2 * LANES), lambda i, place: (i, 0, 0, 0))
    vec_spec = fixed(VECTOR_ROWS, model)

    def run(body, loader, name, flops, moved, in_specs, out_specs, out_shape, operands, grid=(steps,), extra=()):
        return call(
            body,
            name,
            flops,
            moved + loader.bytes,
            grid_spec=pltpu.PrefetchScalarGridSpec(
                num_scalar_prefetch=1,
                grid=grid,
                in_specs=list(in_specs) + loader.specs,
                out_specs=out_specs,
                scratch_shapes=list(extra) + loader.scratch,
            ),
            out_shape=out_shape,
        )(place, *operands, *loader.arrays)

    square = 2 * tokens * model * model
    loader = Loader([(text_first, ["qkv"])], shapes)
    norm_one, joined, mixed, weights = run(
        partial(text_attend_body, loader, len(loader.arrays), model),
        loader,
        "text_attend",
        4 * square,
        tokens * model * 20,
        [rows_of(model), pl.BlockSpec((groups, 1, LANES), lambda i, place: (i, 0, 0)), vec_spec],
        [rows_of(model), rows_of(3 * model), rows_of(model), weights_spec],
        [
            array(tokens, model),
            array(tokens, 3 * model),
            array(tokens, model),
            array(tokens // LANES, pairs, LANES, 2 * LANES),
        ],
        (inflow, ids, vectors),
    )

    loader = Loader([(text_rest, ["out", "fc1"])], shapes)
    hidden, norm_two, active, slope = run(
        partial(text_hidden_body, loader, len(loader.arrays)),
        loader,
        "text_hidden",
        (1 + folds) * square,
        tokens * model * (10 + 4 * folds),
        [rows_of(model), rows_of(model), vec_spec, fixed(1, hidden_units)],
        [rows_of(model), rows_of(model), rows_of(hidden_units), rows_of(hidden_units)],
        [
            array(tokens, model, dtype=F32),
            array(tokens, model),
            array(tokens, hidden_units),
            array(tokens, hidden_units),
        ],
        (inflow, mixed, vectors, fc1_vector),
    )

    loader = Loader([(text_rest, ["out", "fc1", "fc2"])], shapes)
    text_out, d_pre, d_hidden, dy1, d_mixed, sums_two, sums_wide = run(
        partial(text_back_body, loader, len(loader.arrays)),
        loader,
        "text_back",
        (1 + 3 * folds) * square,
        tokens * model * (16 + 6 * folds),
        [rows_of(model), rows_of(model), rows_of(hidden_units), rows_of(hidden_units), vec_spec],
        [
            rows_of(model),
            rows_of(hidden_units),
            rows_of(model),
            rows_of(model),
            rows_of(model),
            fixed(8, model),
            fixed(8, hidden_units),
        ],
        [
            array(tokens, model),
            array(tokens, hidden_units),
            array(tokens, model, dtype=F32),
            array(tokens, model),
            array(tokens, model),
            array(8, model, dtype=F32),
            array(8, hidden_units, dtype=F32),
        ],
        (cotangent, hidden, active, slope, vectors),
    )

    loader = Loader([(text_first, ["qkv"])], shapes)
    d_joined, text_grad, sums_one = run(
        partial(text_unjoin_body, loader, len(loader.arrays), model),
        loader,
        "text_unjoin",
        5 * square,
        tokens * model * 28,
        [
            rows_of(model),
            rows_of(3 * model),
            weights_spec,
            rows_of(model),
            rows_of(model),
            vec_spec,
        ],
        [rows_of(3 * model), rows_of(model), fixed(8, model)],
        [
            array(tokens, 3 * model),
            array(tokens, model, dtype=F32),
            array(8, model, dtype=F32),
        ],
        (inflow, joined, weights, d_mixed, d_hidden, vectors),
    )

    images, image_tokens, _ = image_in.shape
    padded = -(-image_tokens // 64) * 64
    image_rows = jnp.pad(image_in, ((0, 0), (0, padded - image_tokens), (0, 0)))
    image_rows = image_rows.reshape(images * padded, model)
    loader = Loader([(image_source, ["qkv", "out", "fc1", "fc2"])], shapes)
    held = images * padded
    image_out = run(
        partial(image_body, loader, len(loader.arrays), model, image_tokens, padded),
        loader,
        "image_block",
        2 * held * model * model * (4 + 2 * folds),
        4 * held * model,
        [fixed(held, model), vec_spec],
        fixed(held, model),
        array(held, model),
        (image_rows, vectors),
        grid=(1,),
        extra=[
            pltpu.VMEM((held, 3 * model), BF16),
            pltpu.VMEM((held, model), BF16),
            pltpu.VMEM((held, model), F32),
        ],
    )
    image_out = image_out.reshape(images, padded, model)[:, :image_tokens]

    if by_pieces:
        two = grad_rows(place, active, cotangent, n_fsdp, "grad_fc2")
        got = reduce_pieces([two], "add_fc2")
        grad_fc2 = unpack(*got, x, core, 0, model // 2, folds)
        one = grad_columns(place, norm_two, d_pre, "grad_fc1")
        out = grad_columns(place, mixed, dy1, "grad_out")
        got = reduce_pieces([one, out], "add_fc1")
        grad_fc1 = unpack(*got, x, core, 0, hidden_units // 2, 1)
        grad_out = unpack(*got, x, core, hidden_units // 2, model // 2, 1)
        got = reduce_pieces([grad_columns(place, norm_one, d_joined, "grad_qkv")], "add_qkv")
        grad_qkv = unpack(*got, x, core, 0, 3 * model // 2, 1)
    else:

        def product(left, right):
            total = lax.psum_scatter(dot_tn(left, right), "fsdp", scatter_dimension=0, tiled=True)
            return lax.psum(total, "dp")

        grad_fc2 = product(active, cotangent)
        grad_fc1 = product(norm_two, d_pre)
        grad_out = product(mixed, dy1)
        grad_qkv = product(norm_one, d_joined)

    wide = sums_wide[0].reshape(n_fsdp, folds, shard).transpose(1, 0, 2).reshape(folds, model)
    sums = jnp.concatenate([sums_one + sums_two, wide])
    sums = reduce_vectors(sums, f)
    return (
        text_out.reshape(text_in.shape),
        image_out,
        text_grad.reshape(text_in.shape),
        sums[LN1_GAIN],
        sums[LN1_BIAS],
        grad_qkv,
        sums[Q_BIAS],
        sums[V_BIAS],
        grad_out,
        sums[OUT_BIAS],
        sums[LN2_GAIN],
        sums[LN2_BIAS],
        grad_fc1,
        sums[8 : 8 + folds].reshape(-1),
        grad_fc2,
        sums[FC2_BIAS],
    )


def solution(mesh):
    rows = P(("dp", "fsdp"), None, None)
    vector, matrix = P("fsdp"), P("fsdp", None)
    in_specs = (
        rows,
        P(("dp", "fsdp"), None),
        rows,
        rows,
        vector,
        vector,
        matrix,
        vector,
        vector,
        matrix,
        vector,
        vector,
        vector,
        matrix,
        vector,
        matrix,
        vector,
        P(None, "fsdp"),
        matrix,
        matrix,
        matrix,
        matrix,
    )
    out_specs = (
        rows,
        rows,
        rows,
        vector,
        vector,
        matrix,
        vector,
        vector,
        matrix,
        vector,
        vector,
        vector,
        matrix,
        vector,
        matrix,
        vector,
    )
    return jax.shard_map(
        per_device, mesh=mesh, in_specs=in_specs, out_specs=out_specs, check_vma=False
    )
```

```python
from functools import partial

import jax
import jax.numpy as jnp
from jax import lax
from jax.experimental import pallas as pl
from jax.experimental.pallas import tpu as pltpu
from jax.sharding import PartitionSpec as P

HEADS = 12
EPSILON = 1e-06
LANES = 128
TILE = 256
MIB = 1024 * 1024
F32 = jnp.float32
BF16 = jnp.bfloat16

LN1_GAIN, LN1_BIAS, Q_BIAS, V_BIAS, OUT_BIAS, LN2_GAIN, LN2_BIAS, FC2_BIAS = range(8)
IMAGE_GAIN_ONE, IMAGE_GAIN_TWO, FC1_BIAS = 8, 9, 10
VECTOR_ROWS = 16


def dot_nn(a, b):
    return lax.dot_general(a, b, (((1,), (0,)), ((), ())), preferred_element_type=F32)


def dot_nt(a, b):
    return lax.dot_general(a, b, (((1,), (1,)), ((), ())), preferred_element_type=F32)


def dot_tn(a, b):
    return lax.dot_general(a, b, (((0,), (0,)), ((), ())), preferred_element_type=F32)


def call(body, name, flops, moved, operands, after=(), num_prefetch=0, weight=100, **kwargs):
    grid_spec = kwargs.pop("grid_spec")
    first = num_prefetch + len(grid_spec["in_specs"])

    def ordered(*refs):
        return body(*refs[:first], *refs[first + len(after) :])

    grid_spec["in_specs"] = list(grid_spec["in_specs"]) + [
        pl.BlockSpec(memory_space=pltpu.HBM)
    ] * len(after)
    return pl.pallas_call(
        ordered,
        name=name,
        grid_spec=pltpu.PrefetchScalarGridSpec(num_scalar_prefetch=num_prefetch, **grid_spec),
        compiler_params=pltpu.CompilerParams(vmem_limit_bytes=63 * MIB),
        cost_estimate=pl.CostEstimate(
            flops=int(flops) * weight, bytes_accessed=int(moved), transcendentals=0
        ),
        **kwargs,
    )(*operands, *after)


class Part:
    def __init__(self, name, start, width, folds):
        self.name, self.start, self.width, self.folds = name, start, width, folds


def pack_parts(shapes):
    parts, at = {}, 0
    for name, (rows, columns), model in shapes:
        folds = rows // model
        parts[name] = Part(name, at, columns // 2, folds)
        at += folds * (columns // 2)
    return parts, at


def cut_body(plan, at, place, *refs):
    vectors, refs = (refs[0], refs[1:]) if at is not None else (None, refs)
    sources, outs = refs[: len(plan)], refs[len(plan) :]
    for source, (target, part) in zip(sources, plan):
        step = source.shape[0] // part.folds
        for fold in range(part.folds):
            left = part.start + fold * part.width
            outs[target][:, left : left + part.width] = source[fold * step : (fold + 1) * step, :]
    if vectors is None:
        return
    block = jnp.zeros((outs[0].shape[0], LANES), BF16)
    outs[0][:, at : at + LANES] = block
    outs[0][: vectors.shape[0], at : at + LANES] = vectors[...]


def cut_pieces(place, vectors, packs):
    plan, sources, shapes, specs = [], [], [], []
    for target, (parts, width, matrices) in enumerate(packs):
        for name, part in parts.items():
            plan.append((target, part))
            sources.append(matrices[name])
            rows = matrices[name].shape[0] // 2
            specs.append(pl.BlockSpec((rows, part.width), lambda i, place: (place[1], place[2])))
        width += LANES if vectors is not None else 0
        shapes.append(jax.ShapeDtypeStruct((rows // part.folds, width), BF16))
    return call(
        partial(cut_body, plan, None if vectors is None else packs[0][1]),
        "cut_pieces",
        0,
        sum(a.size for a in sources),
        (place, *([] if vectors is None else [vectors]), *sources),
        weight=1,
        num_prefetch=1,
        grid_spec=dict(
            grid=(1,),
            in_specs=(
                []
                if vectors is None
                else [pl.BlockSpec(vectors.shape, lambda i, place: (0, 0))]
            )
            + specs,
            out_specs=[pl.BlockSpec(a.shape, lambda i, place: (0, 0)) for a in shapes],
        ),
        out_shape=shapes,
    )


class Whole:
    def __init__(self, arrays):
        self.arrays = arrays

    def operands(self, names):
        return [self.arrays[name] for name in names]

    def start(self, refs, place, names, targets, semaphores):
        for ref, name in zip(refs, names):
            pltpu.make_async_copy(ref, targets[name], semaphores[name]).start()


def start_piece(source, parts, names, targets, semaphores, f, x, core):
    for name in names:
        part = parts[name]
        height = source.shape[0]
        first = f * (2 * part.folds * height) + x * (part.folds * height)
        for fold in range(part.folds):
            columns = part.start + fold * part.width
            pltpu.make_async_copy(
                source.at[:, pl.ds(columns, part.width)],
                targets[name].at[
                    pl.ds(pl.multiple_of(first + fold * height, 16), height),
                    pl.ds(pl.multiple_of(core * part.width, LANES), part.width),
                ],
                semaphores[name],
            ).start()


class Relative:
    def __init__(self, parts, buffers):
        self.parts, self.buffers = parts, buffers

    def operands(self, names):
        return [array for array, _ in self.buffers]

    def start(self, refs, place, names, targets, semaphores):
        f, x, core = place
        for ref, (_, (dy, dx, dc)) in zip(refs, self.buffers):
            for dz in range(ref.shape[0]):
                start_piece(
                    ref.at[dz],
                    self.parts,
                    names,
                    targets,
                    semaphores,
                    f ^ (dy + 2 * dz),
                    x ^ dx,
                    core ^ dc,
                )


class Listed:
    def __init__(self, parts, array):
        self.parts, self.array = parts, array

    def operands(self, names):
        return [self.array]

    def start(self, refs, place, names, targets, semaphores):
        (ref,) = refs

        def step(i, carry):
            start_piece(
                ref.at[i], self.parts, names, targets, semaphores, i // 4, (i // 2) % 2, i % 2
            )
            return carry

        lax.fori_loop(0, ref.shape[0], step, 0)


class Loader:
    def __init__(self, wanted, shapes):
        self.wanted, self.shapes = wanted, shapes
        self.names = [name for _, names in wanted for name in names]
        self.arrays = [a for source, names in wanted for a in source.operands(names)]
        self.specs = [pl.BlockSpec(memory_space=pltpu.HBM)] * len(self.arrays)
        self.scratch = [pltpu.VMEM(shapes[name], BF16) for name in self.names] + [
            pltpu.SemaphoreType.DMA((len(self.names),))
        ]
        self.bytes = sum(2 * shapes[name][0] * shapes[name][1] for name in self.names)

    def bind(self, refs, scratch, place_ref):
        self.refs = refs
        self.targets = dict(zip(self.names, scratch))
        self.semaphores = {name: scratch[-1].at[i] for i, name in enumerate(self.names)}
        self.place = (place_ref[0], place_ref[1], place_ref[2])
        return self

    def start(self):
        at = 0
        for source, names in self.wanted:
            count = len(source.operands(names))
            source.start(
                self.refs[at : at + count], self.place, names, self.targets, self.semaphores
            )
            at += count

    def wait(self, name):
        target = self.targets[name]
        pltpu.make_async_copy(target, target, self.semaphores[name]).wait()


def normed(values, gain, shift):
    centre = values - jnp.mean(values, axis=-1, keepdims=True)
    spread = lax.rsqrt(jnp.mean(centre * centre, axis=-1, keepdims=True) + EPSILON)
    return centre * spread * gain + shift


def norm_back(values, gain, grad):
    centre = values - jnp.mean(values, axis=-1, keepdims=True)
    spread = lax.rsqrt(jnp.mean(centre * centre, axis=-1, keepdims=True) + EPSILON)
    scaled = centre * spread
    grad_gain = jnp.sum(grad * scaled, axis=0, keepdims=True)
    grad_shift = jnp.sum(grad, axis=0, keepdims=True)
    inner = grad * gain
    inner = inner - jnp.mean(inner, axis=-1, keepdims=True) - scaled * jnp.mean(
        inner * scaled, axis=-1, keepdims=True
    )
    return inner * spread, grad_gain, grad_shift


def lane_sides(scale=1.0):
    lane = lax.broadcasted_iota(jnp.int32, (LANES, LANES), 1)
    left = jnp.where(lane < LANES // 2, scale, 0.0)
    return left.astype(BF16), (scale - left).astype(BF16)


def by_head(values, sides):
    return jnp.concatenate([values * sides[0], values * sides[1]], axis=0)


def pair_columns(width, pair):
    return [slice(third * width + pair * LANES, third * width + (pair + 1) * LANES) for third in range(3)]


def head_ones():
    row = lax.broadcasted_iota(jnp.int32, (2 * LANES, LANES), 0)
    lane = lax.broadcasted_iota(jnp.int32, (2 * LANES, LANES), 1)
    return jnp.where((row < LANES) == (lane < LANES // 2), 1.0, 0.0).astype(BF16)


def spread_ones():
    row = lax.broadcasted_iota(jnp.int32, (2 * LANES, 2 * LANES), 0)
    lane = lax.broadcasted_iota(jnp.int32, (2 * LANES, 2 * LANES), 1)
    return jnp.where((row % LANES < LANES // 2) == (lane < LANES), 1.0, 0.0).astype(BF16)


def attention(joined_ref, rows, width, allowed, store):
    sides, key_sides = lane_sides(), lane_sides((width // HEADS) ** -0.5)
    places = [pair_columns(width, pair) for pair in range(width // LANES)]
    scores = [
        dot_nt(joined_ref[rows, one], by_head(joined_ref[rows, two], key_sides))
        for one, two, _ in places
    ]
    weights = []
    for both in scores:
        parts = []
        for head in range(2):
            own = jnp.where(allowed, both[:, head * LANES : (head + 1) * LANES], -1e30)
            raised = jnp.exp(own - jnp.max(own, axis=-1, keepdims=True))
            parts.append(raised * (1.0 / jnp.sum(raised, axis=-1, keepdims=True)))
        weights.append(jnp.concatenate(parts, axis=1).astype(BF16))
    for pair, (low, (_, _, three)) in enumerate(zip(weights, places)):
        store(pair, low, by_head(joined_ref[rows, three], sides))


def gelu_both(values):
    below = 0.5 + 0.5 * lax.erf(values * 0.7071067811865476)
    bell = jnp.exp(values * values * -0.5) * 0.3989422804014327
    return values * below, below + values * bell


def text_attend_body(loader, n_sources, width, place, x_ref, ids_ref, vec_ref, *rest):
    sources, rest = rest[:n_sources], rest[n_sources:]
    normed_ref, joined_ref, mixed_ref, weights_ref, exact_ref = rest[:5]
    load = loader.bind(sources, rest[5:], place)

    @pl.when(pl.program_id(0) == 0)
    def _():
        load.start()
        load.wait("qkv")

    w_qkv = load.targets["qkv"]
    values = x_ref[...].astype(F32)
    norm_one = normed(
        values, vec_ref[LN1_GAIN : LN1_GAIN + 1, :], vec_ref[LN1_BIAS : LN1_BIAS + 1, :]
    ).astype(BF16)
    normed_ref[...] = norm_one
    for third, bias in enumerate((Q_BIAS, None, V_BIAS)):
        columns = slice(third * width, (third + 1) * width)
        product = dot_nn(norm_one, w_qkv[:, columns])
        if bias is not None:
            product = product + vec_ref[bias : bias + 1, :]
        joined_ref[:, columns] = product.astype(BF16)
    ones = head_ones()
    for part in range(x_ref.shape[0] // LANES):
        rows = slice(part * LANES, (part + 1) * LANES)
        ids = jnp.broadcast_to(ids_ref[part], (LANES, LANES))

        def store(pair, low, values):
            lanes = slice(pair * LANES, (pair + 1) * LANES)
            weights_ref[part, pair] = low
            both = dot_nn(low, jnp.concatenate([values, ones], axis=1))
            mixed_ref[rows, lanes] = both[:, :LANES].astype(BF16)
            exact_ref[rows, lanes] = both[:, :LANES] / both[:, LANES:]

        attention(joined_ref, rows, width, ids == ids.T, store)


def text_forward_body(loader, n_sources, place, x_ref, mixed_ref, vec_ref, fc1_bias_ref, *rest):
    sources, rest = rest[:n_sources], rest[n_sources:]
    hidden_ref, norm_two_ref, active_ref, slope_ref = rest[:4]
    load = loader.bind(sources, rest[4:], place)
    first = pl.program_id(0) == 0

    @pl.when(first)
    def _():
        load.start()
        load.wait("out")

    hidden = (
        x_ref[...].astype(F32)
        + dot_nn(mixed_ref[...], load.targets["out"][...])
        + vec_ref[OUT_BIAS : OUT_BIAS + 1, :]
    )
    hidden_ref[...] = hidden
    norm_two = normed(
        hidden, vec_ref[LN2_GAIN : LN2_GAIN + 1, :], vec_ref[LN2_BIAS : LN2_BIAS + 1, :]
    ).astype(BF16)
    norm_two_ref[...] = norm_two

    @pl.when(first)
    def _():
        load.wait("fc1")

    w_fc1 = load.targets["fc1"]
    step = hidden.shape[1]
    for k in range(w_fc1.shape[1] // step):
        columns = slice(k * step, (k + 1) * step)
        pre_act = dot_nn(norm_two, w_fc1[:, columns]) + fc1_bias_ref[:, columns]
        active, slope = gelu_both(pre_act)
        active_ref[:, columns] = active.astype(BF16)
        slope_ref[:, columns] = slope.astype(BF16)


def text_back_body(loader, n_sources, place, g_ref, hidden_ref, slope_ref, vec_ref, *rest):
    sources, rest = rest[:n_sources], rest[n_sources:]
    pre_ref, d_hidden_ref, dy1_ref, d_mixed_ref, sums_ref, wide_ref = rest[:6]
    load = loader.bind(sources, rest[6:], place)
    first = pl.program_id(0) == 0

    @pl.when(first)
    def _():
        load.start()
        load.wait("fc2")
        sums_ref[...] = jnp.zeros_like(sums_ref)
        wide_ref[...] = jnp.zeros_like(wide_ref)

    g = g_ref[...]
    w_fc2 = load.targets["fc2"]
    step = g.shape[1]
    for k in range(slope_ref.shape[1] // step):
        columns = slice(k * step, (k + 1) * step)
        low = (dot_nt(g, w_fc2[columns, :]) * slope_ref[:, columns].astype(F32)).astype(BF16)
        pre_ref[:, columns] = low
        wide_ref[0:1, columns] += jnp.sum(low.astype(F32), axis=0, keepdims=True)

    @pl.when(first)
    def _():
        load.wait("fc1")
        load.wait("out")

    d_norm = dot_nt(pre_ref[...], load.targets["fc1"][...])
    part, gain, shift = norm_back(
        hidden_ref[...], vec_ref[LN2_GAIN : LN2_GAIN + 1, :], d_norm
    )
    d_hidden = g.astype(F32) + part
    d_hidden_ref[...] = d_hidden
    dy1 = d_hidden.astype(BF16)
    dy1_ref[...] = dy1
    d_mixed_ref[...] = dot_nt(dy1, load.targets["out"][...]).astype(BF16)
    sums_ref[LN2_GAIN : LN2_GAIN + 1, :] += gain
    sums_ref[LN2_BIAS : LN2_BIAS + 1, :] += shift
    sums_ref[OUT_BIAS : OUT_BIAS + 1, :] += jnp.sum(dy1.astype(F32), axis=0, keepdims=True)
    sums_ref[FC2_BIAS : FC2_BIAS + 1, :] += jnp.sum(g.astype(F32), axis=0, keepdims=True)


def text_out_body(loader, n_sources, place, hidden_ref, active_ref, vec_ref, *rest):
    sources, rest = rest[:n_sources], rest[n_sources:]
    (out_ref,) = rest[:1]
    load = loader.bind(sources, rest[1:], place)

    @pl.when(pl.program_id(0) == 0)
    def _():
        load.start()
        load.wait("fc2")

    out_ref[...] = (
        hidden_ref[...]
        + dot_nn(active_ref[...], load.targets["fc2"][...])
        + vec_ref[FC2_BIAS : FC2_BIAS + 1, :]
    ).astype(BF16)


def text_unjoin_body(
    loader,
    n_sources,
    width,
    place,
    joined_ref,
    weights_ref,
    d_mixed_ref,
    exact_ref,
    x_ref,
    d_hidden_ref,
    vec_ref,
    *rest,
):
    sources, rest = rest[:n_sources], rest[n_sources:]
    d_joined_ref, grad_ref, sums_ref = rest[:3]
    load = loader.bind(sources, rest[3:], place)
    start = pl.program_id(0) == 0

    @pl.when(start)
    def _():
        load.start()
        sums_ref[...] = jnp.zeros_like(sums_ref)

    scale = (width // HEADS) ** -0.5
    sides, key_sides = lane_sides(), lane_sides(scale)
    left = lax.broadcasted_iota(jnp.int32, (LANES, LANES), 1) < LANES // 2
    ones = spread_ones()
    places = [pair_columns(width, pair) for pair in range(width // LANES)]
    for part in range(joined_ref.shape[0] // LANES):
        rows = slice(part * LANES, (part + 1) * LANES)
        d_weights = [
            dot_nt(d_mixed_ref[rows, one], by_head(joined_ref[rows, three], sides))
            for one, _, three in places
        ]
        d_scores = []
        for pair, (one, _, _) in enumerate(places):
            product = d_mixed_ref[rows, one].astype(F32) * exact_ref[rows, one]
            high = product.astype(BF16)
            low = (product - high.astype(F32)).astype(BF16)
            total = dot_nn(jnp.concatenate([high, low], axis=1), ones)
            d_scores.append(
                (weights_ref[part, pair].astype(F32) * (d_weights[pair] - total)).astype(BF16)
            )
        for pair, (one, two, three) in enumerate(places):
            d_joined_ref[rows, one] = dot_nn(
                d_scores[pair], by_head(joined_ref[rows, two], key_sides)
            ).astype(BF16)
            d_keys = dot_tn(d_scores[pair], joined_ref[rows, one]) * scale
            d_joined_ref[rows, two] = jnp.where(left, d_keys[:LANES], d_keys[LANES:]).astype(BF16)
            d_values = dot_tn(weights_ref[part, pair], d_mixed_ref[rows, one])
            d_joined_ref[rows, three] = jnp.where(
                left, d_values[:LANES], d_values[LANES:]
            ).astype(BF16)
    for row, third in ((Q_BIAS, 0), (V_BIAS, 2)):
        columns = d_joined_ref[:, third * width : (third + 1) * width].astype(F32)
        sums_ref[row : row + 1, :] += jnp.sum(columns, axis=0, keepdims=True)

    @pl.when(start)
    def _():
        load.wait("qkv")

    d_norm = dot_nt(d_joined_ref[...], load.targets["qkv"][...])
    part, gain, shift = norm_back(
        x_ref[...].astype(F32), vec_ref[LN1_GAIN : LN1_GAIN + 1, :], d_norm
    )
    grad_ref[...] = d_hidden_ref[...] + part
    sums_ref[LN1_GAIN : LN1_GAIN + 1, :] += gain
    sums_ref[LN1_BIAS : LN1_BIAS + 1, :] += shift


def image_body(loader, n_sources, width, tokens, padded, place, x_ref, vec_ref, *rest):
    sources, rest = rest[:n_sources], rest[n_sources:]
    out_ref, joined_ref, mixed_ref, hidden_ref = rest[:4]
    load = loader.bind(sources, rest[4:], place)
    load.start()
    values = x_ref[...].astype(F32)
    norm_one = normed(values, vec_ref[IMAGE_GAIN_ONE : IMAGE_GAIN_ONE + 1, :], 0.0).astype(BF16)
    load.wait("qkv")
    w_qkv = load.targets["qkv"]
    for third in range(3):
        columns = slice(third * width, (third + 1) * width)
        joined_ref[:, columns] = dot_nn(norm_one, w_qkv[:, columns]).astype(BF16)
    row = lax.broadcasted_iota(jnp.int32, (LANES, LANES), 0)
    column = lax.broadcasted_iota(jnp.int32, (LANES, LANES), 1)
    allowed = (row // padded == column // padded) & (column % padded < tokens)
    for part in range(x_ref.shape[0] // LANES):
        rows = slice(part * LANES, (part + 1) * LANES)

        def store(pair, low, values):
            lanes = slice(pair * LANES, (pair + 1) * LANES)
            mixed_ref[rows, lanes] = dot_nn(low, values).astype(BF16)

        attention(joined_ref, rows, width, allowed, store)
    load.wait("out")
    hidden = values + dot_nn(mixed_ref[...], load.targets["out"][...])
    norm_two = normed(hidden, vec_ref[IMAGE_GAIN_TWO : IMAGE_GAIN_TWO + 1, :], 0.0).astype(BF16)
    hidden_ref[...] = hidden
    load.wait("fc1")
    load.wait("fc2")
    w_fc1, w_fc2 = load.targets["fc1"], load.targets["fc2"]
    for k in range(w_fc1.shape[1] // width):
        columns = slice(k * width, (k + 1) * width)
        pre_act = dot_nn(norm_two, w_fc1[:, columns])
        active = (pre_act * (0.5 + 0.5 * lax.erf(pre_act * 0.7071067811865476))).astype(BF16)
        hidden_ref[...] += dot_nn(active, w_fc2[columns, :])
    out_ref[...] = hidden_ref[...].astype(BF16)


SLOTS = 16
CORNERED = (0, 2, 1, 3, 4, 6, 12, 14, 9, 11, 13, 15, 5, 7, 8, 10)


class Job:
    def __init__(self, kind, left, right, start):
        self.kind, self.left, self.right, self.start = kind, left, right, start
        if kind == "rows":
            self.half = right.shape[1] // 2
            self.blocks = 2 if self.half > 1152 else 1
            self.width = self.half
        elif kind == "folds":
            self.half = right.shape[1] // 2
            self.blocks = left.shape[1] // right.shape[1]
            self.width = self.half * self.blocks
        else:
            self.half = self.width = LANES
            self.blocks = 1


class Pieces:
    def __init__(self, jobs, came, group):
        self.jobs, self.came, self.group = jobs, came, group
        first = jobs[0]
        self.tokens = first.left.shape[0]
        self.model = first.left.shape[1] if first.kind == "rows" else first.right.shape[1]
        self.height = self.model // SLOTS
        self.width = sum(job.width for job in jobs)
        self.operands, self.scratch = [], [pltpu.VMEM((SLOTS, self.height, self.width), BF16)]
        self.loads = 0
        if came is not None:
            self.operands.append(came)
            self.scratch.append(pltpu.VMEM((SLOTS, self.height, self.width), BF16))
            self.loads += 1
        for job in jobs:
            self.operands.append(job.left)
            if job.kind == "sums":
                self.scratch += [
                    pltpu.VMEM(job.left.shape, F32),
                    pltpu.VMEM((self.model, LANES), F32),
                ]
                self.loads += 1
                continue
            self.operands.append(job.right)
            left = (self.tokens, self.model)
            wide = job.half // job.blocks if job.kind == "rows" else job.half
            self.scratch += [
                pltpu.VMEM(left if job.kind == "rows" else (job.blocks, *left), BF16),
                pltpu.VMEM((self.tokens, job.half), BF16),
                pltpu.VMEM((self.model, wide), F32),
            ]
            self.loads += job.blocks + 1
        count = SLOTS // group
        self.out_shape = [jax.ShapeDtypeStruct((group, self.height, self.width), BF16)] * count
        self.flops = 2 * self.tokens * self.model * self.width
        self.moved = 2 * sum(a.size for a in self.operands)

    def steps(self, place, operands, outs, scratch, load, send):
        operands, scratch = list(operands), list(scratch)
        pieces = scratch.pop(0)
        adds = self.came is not None
        steps, begin = [], []
        if adds:
            came = scratch.pop(0)
            begin = [load(operands.pop(0), came)]
        f, x, core = place
        side = core if adds else 1 - core
        y, column = f % 2, f // 2
        height = self.height

        def put(slot, columns, value):
            at = CORNERED.index(slot)
            if adds:
                value = value + came[at, :, columns].astype(F32)
            pieces[at, :, columns] = value.astype(BF16)

        def leave(first, count, columns):
            size = min(self.group, count)
            for at in range(first, first + count, size):
                send(
                    pieces.at[pl.ds(at, size), :, columns],
                    outs[at // self.group].at[pl.ds(at % self.group, size), :, columns],
                )

        def put_rows(total, columns):
            for slot in range(SLOTS):
                dy, dx, dz = slot // 8, (slot // 4) % 2, slot % 4
                first = ((f ^ (dy + 2 * dz)) * 2 + (x ^ dx)) * height
                put(slot, columns, total[pl.ds(pl.multiple_of(first, 16), height), :])
            leave(0, SLOTS, columns)

        def rows_step(job, left, right, total, block):
            width = job.half // job.blocks
            start = job.start + block * width

            def compute():
                total[...] = dot_tn(left[...], right[:, block * width : (block + 1) * width])
                put_rows(total, slice(start, start + width))

            return compute

        def folds_step(job, left, right, total, dz):
            rows = total.shape[0] // 2

            def compute():
                total[...] = dot_tn(left[dz], right[...])
                for dy in range(2):
                    for dx in range(2):
                        slot = dy * 8 + dx * 4 + dz
                        first = (y ^ dy) * rows + (x ^ dx) * (rows // 2)
                        for fold in range(job.blocks):
                            lane = job.start + fold * job.half
                            top = pl.multiple_of(first + fold * height, 16)
                            put(slot, slice(lane, lane + job.half), total[pl.ds(top, height), :])
                        leave(
                            CORNERED.index(slot), 1, slice(job.start, job.start + job.width)
                        )

            return compute

        def sums_step(job, table, total):
            def compute():
                own = table[pl.ds(pl.multiple_of(side * 8, 8), 8), :]
                total[...] = jnp.concatenate([own] * (LANES // 8)).T
                put_rows(total, slice(job.start, job.start + LANES))

            return compute

        for job in self.jobs:
            if job.kind == "sums":
                table, total = scratch.pop(0), scratch.pop(0)
                steps.append((begin + [load(operands.pop(0), table)], sums_step(job, table, total)))
                begin = []
                continue
            left_ref, right_ref = operands.pop(0), operands.pop(0)
            left, right, total = scratch.pop(0), scratch.pop(0), scratch.pop(0)
            if job.kind == "rows":
                width = job.half // job.blocks
                begin = begin + [load(left_ref, left)]
                for block in range(job.blocks):
                    first = pl.multiple_of(side * job.half + block * width, LANES)
                    begin.append(
                        load(
                            right_ref.at[:, pl.ds(first, width)],
                            right.at[:, pl.ds(block * width, width)],
                        )
                    )
                    steps.append((begin, rows_step(job, left, right, total, block)))
                    begin = []
            else:
                first = pl.multiple_of(side * job.half, LANES)
                begin = begin + [load(right_ref.at[:, pl.ds(first, job.half)], right)]
                width = left.shape[2]
                for dz in range(job.blocks):
                    lane = pl.multiple_of((column ^ dz) * width, LANES)
                    begin.append(load(left_ref.at[:, pl.ds(lane, width)], left.at[dz]))
                    steps.append((begin, folds_step(job, left, right, total, dz)))
                    begin = []
        return steps


class Adds:
    def __init__(self, groups):
        self.groups = groups
        self.operands, self.scratch, self.out_shape = [], [], []
        for sums in groups:
            count, height = sums[0][0][2], sums[0][0][0].shape[1]
            width = sum(pieces[0][0].shape[2] for pieces in sums)
            for pieces in sums:
                for piece in pieces:
                    self.operands.append(piece[0])
                    self.scratch.append(
                        pltpu.VMEM((count, height, pieces[0][0].shape[2]), BF16)
                    )
            self.out_shape.append(jax.ShapeDtypeStruct((count, height, width), BF16))
        self.scratch += [pltpu.VMEM(a.shape, BF16) for a in self.out_shape]
        self.loads = len(self.operands)
        self.flops = sum(a.size for a in self.out_shape)
        self.moved = 2 * sum(a.size for a in self.out_shape) * 4

    def steps(self, place, operands, outs, scratch, load, send):
        operands, scratch = list(operands), list(scratch)
        totals = scratch[len(operands) :]
        loads, work = [], []
        for sums, out, total in zip(self.groups, outs, totals):
            at = 0
            for pieces in sums:
                held = []
                for _, first, count, *lane in pieces:
                    source, target = operands.pop(0), scratch.pop(0)
                    lanes = pl.ds(lane[0] if lane else 0, target.shape[2])
                    loads.append(load(source.at[pl.ds(first, count), :, lanes], target))
                    held.append(target)
                work.append((held, total, slice(at, at + held[0].shape[2])))
                at += held[0].shape[2]

        def compute():
            for held, total, columns in work:
                value = held[0][...].astype(F32)
                for other in held[1:]:
                    value = value + other[...].astype(F32)
                total[:, :, columns] = value.astype(BF16)
            for out, total in zip(outs, totals):
                send(total, out)

        return [(loads, compute)]


def tasks_body(tasks, counts, place, *refs):
    n_in, n_out = sum(c[0] for c in counts), sum(c[1] for c in counts)
    ins, outs, held = refs[:n_in], refs[n_in : n_in + n_out], refs[n_in + n_out :]
    (in_sem, out_sem), held = held[:2], held[2:]
    where = (place[0], place[1], place[2])
    n_loads = 0

    def load(source, target):
        nonlocal n_loads
        copy = pltpu.make_async_copy(source, target, in_sem.at[n_loads])
        n_loads += 1
        return copy

    def send(source, target):
        pltpu.make_async_copy(source, target, out_sem).start()

    steps, at_in, at_out, at_held = [], 0, 0, 0
    for task, (a, b, c) in zip(tasks, counts):
        steps += task.steps(
            where,
            ins[at_in : at_in + a],
            outs[at_out : at_out + b],
            held[at_held : at_held + c],
            load,
            send,
        )
        at_in, at_out, at_held = at_in + a, at_out + b, at_held + c
    ahead = 1 if any(isinstance(task, Pieces) for task in tasks) else len(steps)
    for loads, _ in steps[:ahead]:
        for copy in loads:
            copy.start()
    for index, (loads, compute) in enumerate(steps):
        for copy in loads:
            copy.wait()
        for later, _ in steps[index + ahead : index + ahead + 1]:
            for copy in later:
                copy.start()
        compute()
    for out in outs:
        pltpu.make_async_copy(out, out, out_sem).wait()


def do_tasks(place, tasks, name, after=()):
    counts = [(len(t.operands), len(t.out_shape), len(t.scratch)) for t in tasks]
    outs = call(
        partial(tasks_body, tasks, counts),
        name,
        sum(t.flops for t in tasks),
        sum(t.moved for t in tasks),
        (place, *[a for t in tasks for a in t.operands]),
        after=after,
        num_prefetch=1,
        grid_spec=dict(
            grid=(1,),
            in_specs=[pl.BlockSpec(memory_space=pl.ANY)] * sum(c[0] for c in counts),
            out_specs=[pl.BlockSpec(memory_space=pl.ANY)] * sum(c[1] for c in counts),
            scratch_shapes=[
                pltpu.SemaphoreType.DMA((sum(t.loads for t in tasks),)),
                pltpu.SemaphoreType.DMA,
            ]
            + [s for t in tasks for s in t.scratch],
        ),
        out_shape=[s for t in tasks for s in t.out_shape],
    )
    outs, results = list(outs), []
    for _, count, _ in counts:
        results.append(outs[:count])
        outs = outs[count:]
    return results


def swap(value, axis, bit):
    size = lax.axis_size(axis)
    return lax.ppermute(value, axis, [(i, i ^ bit) for i in range(size)])


def swap_corner(value):
    n = lax.axis_size("fsdp")
    pairs = [
        (d * n + i, (d ^ 2) * n + (i ^ 1)) for d in range(lax.axis_size("dp")) for i in range(n)
    ]
    return lax.ppermute(value, ("dp", "fsdp"), pairs)


def gate_body(count, *refs):
    pass


def gate(arrays, after):
    return call(
        partial(gate_body, len(arrays)),
        "gate",
        0,
        0,
        arrays,
        after=after,
        grid_spec=dict(
            grid=(1,),
            in_specs=[pl.BlockSpec(memory_space=pl.ANY)] * len(arrays),
            out_specs=[pl.BlockSpec(memory_space=pl.ANY)] * len(arrays),
        ),
        out_shape=[jax.ShapeDtypeStruct(a.shape, a.dtype) for a in arrays],
        input_output_aliases={i: i for i in range(len(arrays))},
    )


def gather_pieces(own):
    column = jnp.stack([own] + [swap(own, "fsdp", bit) for bit in (2, 4, 6)])
    return column, swap(column, "fsdp", 1), swap(column, "dp", 2), swap_corner(column)


def both_cores(here):
    places = ((0, 0), (1, 0), (0, 1), (1, 1))
    return [(a, at + (0,)) for a, at in zip(here, places)] + [
        (swap(a, "dp", 1), at + (1,)) for a, at in zip(here, places)
    ]


def gathered_vectors(buffers, rows, at, width, f):
    held = jnp.stack([buffers[i][0][:, :rows, at : at + width] for i in range(2)])
    held = held.reshape(2, 2, 2, rows, width)
    for axis, bit in ((0, 1), (1, 4), (2, 2)):
        held = jnp.where((f & bit) != 0, jnp.flip(held, axis), held)
    return held.transpose(3, 1, 2, 0, 4).reshape(rows, 8 * width)


class Reduction:
    def __init__(self):
        self.sets = []

    def add(self, slots):
        own, across, beside, later = slots
        self.sets.append((own, swap(across, "dp", 2), swap(beside, "fsdp", 1), later))

    def corners(self):
        return Adds(
            [
                [[(later, 0, 2), (beside, 2, 2)] for _, _, beside, later in self.sets],
                [[(later, 2, 2), (across, 2, 2)] for _, across, _, later in self.sets],
            ]
        )

    def after_corners(self, outs):
        x_odd, y_even = outs
        self.x_odd, self.y_even = swap(x_odd, "dp", 2), swap(y_even, "fsdp", 1)

    def sides(self, straight=False):
        groups = []
        for odd in range(2):
            for at, count in ((0, 1), (1, 1)) if straight else ((0, 2),):
                sums, lane = [], 0
                for own, across, beside, _ in self.sets:
                    width = own.shape[2]
                    near, far = (beside, self.x_odd) if odd else (across, self.y_even)
                    sums.append(
                        [
                            (own, 2 * odd + at, count),
                            (near, at, count),
                            (far, at, count, lane),
                        ]
                    )
                    lane += width
                groups.append(sums)
        return Adds(groups)

    def after_sides(self, outs):
        self.low, high = outs
        self.high = swap(high, "fsdp", 2)

    def halves(self):
        return Adds([[[(self.low, i, 1), (self.high, i, 1)]] for i in range(2)])

    def after_halves(self, outs):
        own, send = outs
        self.last = [own, swap(send, "fsdp", 4)]

    def after_sides_straight(self, outs):
        own, two, one, three = outs
        self.last = [own, swap(one, "fsdp", 2), swap(two, "fsdp", 4), swap(three, "fsdp", 6)]

    def column(self):
        return [(a, 0, 1) for a in self.last]


def replicas(total):
    total = total[0]
    across = swap(total, "dp", 2)
    return total, across, swap(total, "dp", 1), swap(across, "dp", 1)


def finish_body(parts, place, own_ref, across_ref, other_ref, diagonal_ref, *outs):
    x_first, core_first = place[1] == 0, place[2] == 0
    sides = []
    for mine, theirs in ((own_ref, across_ref), (other_ref, diagonal_ref)):
        mine, theirs = mine[...].astype(F32), theirs[...].astype(F32)
        sides.append((jnp.where(x_first, mine, theirs), jnp.where(x_first, theirs, mine)))
    at = 0
    for out, (width, folds) in zip(outs, parts):
        height = own_ref.shape[0]
        for dx in range(2):
            one, two = sides[0][dx], sides[1][dx]
            for fold in range(folds):
                lanes = slice(at + fold * width, at + (fold + 1) * width)
                rows = slice((dx * folds + fold) * height, (dx * folds + fold + 1) * height)
                out[rows, :width] = jnp.where(core_first, one[:, lanes], two[:, lanes])
                out[rows, width:] = jnp.where(core_first, two[:, lanes], one[:, lanes])
        at += width * folds


def finish(place, pieces, parts):
    height, width = pieces[0].shape
    shapes = [(2 * folds * height, 2 * columns) for columns, folds in parts]
    return call(
        partial(finish_body, parts),
        "finish",
        0,
        width * height * 24,
        (place, *pieces),
        num_prefetch=1,
        grid_spec=dict(
            grid=(1,),
            in_specs=[pl.BlockSpec((height, width), lambda i, place: (0, 0))] * 4,
            out_specs=[pl.BlockSpec(shape, lambda i, place: (0, 0)) for shape in shapes],
        ),
        out_shape=[jax.ShapeDtypeStruct(shape, F32) for shape in shapes],
    )


def per_device(
    text_in,
    text_segments,
    text_cotangent,
    image_in,
    ln1_gain,
    ln1_bias,
    w_qkv,
    q_bias,
    v_bias,
    w_out,
    out_bias,
    ln2_gain,
    ln2_bias,
    w_fc1,
    fc1_bias,
    w_fc2,
    fc2_bias,
    image_norms,
    image_qkv,
    image_proj,
    image_fc1,
    image_fc2,
):
    n_fsdp, n_dp = lax.axis_size("fsdp"), lax.axis_size("dp")
    batch_rows, length, model = text_in.shape
    hidden_units = w_fc1.shape[1]
    tokens = batch_rows * length
    folds = hidden_units // model
    f, replica = lax.axis_index("fsdp"), lax.axis_index("dp")
    x, core = replica // 2, replica % 2
    place = jnp.stack([f, x, core]).astype(jnp.int32)
    shard = model // n_fsdp
    by_pieces = n_fsdp == 8 and n_dp == 4 and shard % 32 == 0

    shapes = {
        "qkv": (model, 3 * model),
        "out": (model, model),
        "fc1": (model, hidden_units),
        "fc2": (hidden_units, model),
    }
    text = {"qkv": w_qkv, "out": w_out, "fc1": w_fc1, "fc2": w_fc2}
    image = {"qkv": image_qkv, "out": image_proj, "fc1": image_fc1, "fc2": image_fc2}

    def parts_of(names):
        return pack_parts([(name, shapes[name], model) for name in names])

    vectors = jnp.concatenate(
        [
            jnp.stack(
                [ln1_gain, ln1_bias, q_bias, v_bias, out_bias, ln2_gain, ln2_bias, fc2_bias]
            ),
            image_norms,
            fc1_bias.reshape(folds, shard),
        ]
    )
    vectors = jnp.pad(vectors, ((0, VECTOR_ROWS - vectors.shape[0]), (0, 0)))
    if by_pieces:
        names = ("qkv",), ("fc2",), ("out", "fc1"), ("qkv", "out", "fc1", "fc2")
        packs = [parts_of(each) + (text,) for each in names[:3]] + [parts_of(names[3]) + (image,)]
        lanes = jnp.pad(vectors, ((0, 0), (0, LANES - shard)))
        cuts = cut_pieces(place, None, packs[1:])
        cuts = cut_pieces(place, lanes, packs[:1]) + cuts
        text_qkv = Relative(packs[0][0], both_cores(gather_pieces(cuts[0])))
        (own,) = gate([cuts[1]], (text_qkv.buffers[0][0],))
        pieces_fc2 = gather_pieces(own)
        text_rest = Listed(packs[2][0], lax.all_gather(cuts[2], ("fsdp", "dp")))
        image_source = Listed(packs[3][0], lax.all_gather(cuts[3], ("fsdp", "dp")))
        vectors = gathered_vectors(text_qkv.buffers, VECTOR_ROWS, packs[0][1], shard, f)
        vectors = vectors.astype(F32)
    else:
        vectors = lax.all_gather(vectors, "fsdp", axis=1, tiled=True).astype(F32)
        gathered = {n: lax.all_gather(a, "fsdp", axis=0, tiled=True) for n, a in text.items()}
        text_qkv = text_fc2 = text_rest = Whole(gathered)
        image_source = Whole(
            {n: lax.all_gather(a, "fsdp", axis=0, tiled=True) for n, a in image.items()}
        )
    fc1_vector = vectors[FC1_BIAS : FC1_BIAS + folds].reshape(folds, n_fsdp, shard)
    fc1_vector = fc1_vector.transpose(1, 0, 2).reshape(1, hidden_units)

    inflow = text_in.reshape(tokens, model)
    cotangent = text_cotangent.reshape(tokens, model)
    ids = text_segments + 16 * (lax.broadcasted_iota(jnp.int32, text_segments.shape, 0) % (LANES // length))
    ids = ids.astype(F32).reshape(tokens // LANES, 1, LANES)
    steps = tokens // TILE
    groups = TILE // LANES
    pairs = model // LANES

    def rows_of(width):
        return pl.BlockSpec((TILE, width), lambda i, place: (i, 0))

    def fixed(*shape):
        return pl.BlockSpec(shape, lambda i, place: (0,) * len(shape))

    def array(*shape, dtype=BF16):
        return jax.ShapeDtypeStruct(shape, dtype)

    weights_spec = pl.BlockSpec((groups, pairs, LANES, 2 * LANES), lambda i, place: (i, 0, 0, 0))
    vec_spec = fixed(VECTOR_ROWS, model)

    def run(body, wanted, name, flops, moved, in_specs, out_specs, out_shape, operands, grid=(steps,), extra=(), after=(), weight=100):
        loader = Loader(wanted, shapes)
        return call(
            partial(body, loader, len(loader.arrays)),
            name,
            flops,
            moved + loader.bytes,
            (place, *operands, *loader.arrays),
            after=after,
            weight=weight,
            num_prefetch=1,
            grid_spec=dict(
                grid=grid,
                in_specs=list(in_specs) + loader.specs,
                out_specs=out_specs,
                scratch_shapes=list(extra) + loader.scratch,
            ),
            out_shape=out_shape,
        )

    def bind(body, *values):
        return lambda loader, count, *refs: body(loader, count, *values, *refs)

    square = 2 * tokens * model * model
    norm_one, joined, mixed, weights, exact = run(
        bind(text_attend_body, model),
        [(text_qkv, ["qkv"])],
        "text_attend",
        4 * square,
        tokens * model * 24,
        [rows_of(model), pl.BlockSpec((groups, 1, LANES), lambda i, place: (i, 0, 0)), vec_spec],
        [rows_of(model), rows_of(3 * model), rows_of(model), weights_spec, rows_of(model)],
        [
            array(tokens, model),
            array(tokens, 3 * model),
            array(tokens, model),
            array(tokens // LANES, pairs, LANES, 2 * LANES),
            array(tokens, model, dtype=F32),
        ],
        (inflow, ids, vectors),
    )
    hidden, norm_two, active, slope = run(
        text_forward_body,
        [(text_rest, ["out", "fc1"])],
        "text_forward",
        (1 + folds) * square,
        tokens * model * (10 + 4 * folds),
        [rows_of(model), rows_of(model), vec_spec, fixed(1, hidden_units)],
        [rows_of(model), rows_of(model), rows_of(hidden_units), rows_of(hidden_units)],
        [
            array(tokens, model, dtype=F32),
            array(tokens, model),
            array(tokens, hidden_units),
            array(tokens, hidden_units),
        ],
        (inflow, mixed, vectors, fc1_vector),
    )
    done = (active,)
    if by_pieces:
        pieces_fc2 = gate(pieces_fc2, done)
        text_fc2 = Relative(packs[1][0], both_cores(pieces_fc2))
        done = (pieces_fc2[0],)
        fc2_jobs = [Job("folds", active, cotangent, 0)]
        (((other,)),) = do_tasks(place, [Pieces(fc2_jobs, None, SLOTS)], "grads_one", done)
        came = swap(other, "dp", 1)
        done = (other,)
    d_pre, d_hidden, dy1, d_mixed, sums_two, sums_wide = run(
        text_back_body,
        [(text_fc2, ["fc2"]), (text_rest, ["fc1", "out"])],
        "text_back",
        (1 + 2 * folds) * square,
        tokens * model * (16 + 4 * folds),
        [rows_of(model), rows_of(model), rows_of(hidden_units), vec_spec],
        [
            rows_of(hidden_units),
            rows_of(model),
            rows_of(model),
            rows_of(model),
            fixed(8, model),
            fixed(8, hidden_units),
        ],
        [
            array(tokens, hidden_units),
            array(tokens, model, dtype=F32),
            array(tokens, model),
            array(tokens, model),
            array(8, model, dtype=F32),
            array(8, hidden_units, dtype=F32),
        ],
        (cotangent, hidden, slope, vectors),
        after=done,
    )
    done = (d_mixed,)
    if by_pieces:
        mid_jobs = [Job("rows", norm_two, d_pre, 0), Job("rows", mixed, dy1, hidden_units // 2)]
        (((other,)),) = do_tasks(place, [Pieces(mid_jobs, None, SLOTS)], "grads_two", done)
        (slots,) = do_tasks(place, [Pieces(fc2_jobs, came, 4)], "grads_three", (other,))
        wide = Reduction()
        wide.add(slots)
        came = swap(other, "dp", 1)
        (slots,) = do_tasks(place, [Pieces(mid_jobs, came, 4)], "grads_four", (slots[0],))
        wide.add(slots)
        done = (slots[0],)
    d_joined, text_grad, sums_one = run(
        bind(text_unjoin_body, model),
        [(text_qkv, ["qkv"])],
        "text_unjoin",
        5 * square,
        tokens * model * 32,
        [
            rows_of(3 * model),
            weights_spec,
            rows_of(model),
            rows_of(model),
            rows_of(model),
            rows_of(model),
            vec_spec,
        ],
        [rows_of(3 * model), rows_of(model), fixed(8, model)],
        [
            array(tokens, 3 * model),
            array(tokens, model, dtype=F32),
            array(8, model, dtype=F32),
        ],
        (joined, weights, d_mixed, exact, inflow, d_hidden, vectors),
        after=done,
    )
    done = (text_grad,)
    units = sums_wide[0].reshape(n_fsdp, folds, shard).transpose(1, 0, 2).reshape(folds, model)
    sums = jnp.concatenate([sums_one + sums_two, units])
    sums = jnp.pad(sums, ((0, VECTOR_ROWS - sums.shape[0]), (0, 0)))
    if by_pieces:
        late_jobs = [
            Job("rows", norm_one, d_joined, 0),
            Job("sums", sums, None, 3 * model // 2),
        ]
        (other,), outs = do_tasks(
            place,
            [Pieces(late_jobs, None, SLOTS), wide.corners()],
            "grads_five",
            done,
        )
        wide.after_corners(outs)
        came = swap(other, "dp", 1)
        done = (other,)
    text_out = run(
        text_out_body,
        [(text_fc2, ["fc2"])],
        "text_out",
        folds * square,
        tokens * model * (6 + 2 * folds),
        [rows_of(model), rows_of(hidden_units), vec_spec],
        rows_of(model),
        array(tokens, model),
        (hidden, active, vectors),
        after=done,
    )
    done = (text_out,)
    if by_pieces:
        slots, outs = do_tasks(
            place, [Pieces(late_jobs, came, 4), wide.sides()], "grads_six", done
        )
        narrow = Reduction()
        narrow.add(slots)
        wide.after_sides(outs)
        done = (slots[0],)

    images, image_tokens, _ = image_in.shape
    padded = -(-image_tokens // 64) * 64
    image_rows = jnp.pad(image_in, ((0, 0), (0, padded - image_tokens), (0, 0)))
    image_rows = image_rows.reshape(images * padded, model)
    held = images * padded
    image_out = run(
        bind(image_body, model, image_tokens, padded),
        [(image_source, ["qkv", "out", "fc1", "fc2"])],
        "image_block",
        2 * held * model * model * (4 + 2 * folds),
        4 * held * model,
        [fixed(held, model), vec_spec],
        fixed(held, model),
        array(held, model),
        (image_rows, vectors),
        grid=(1,),
        extra=[
            pltpu.VMEM((held, 3 * model), BF16),
            pltpu.VMEM((held, model), BF16),
            pltpu.VMEM((held, model), F32),
        ],
        after=done,
    )
    done = (image_out,)
    image_out = image_out.reshape(images, padded, model)[:, :image_tokens]

    if by_pieces:
        outs, second = do_tasks(place, [narrow.corners(), wide.halves()], "sums_seven", done)
        narrow.after_corners(outs)
        wide.after_halves(second)
        (outs,) = do_tasks(place, [narrow.sides(straight=True)], "sums_eight", (outs[0],))
        narrow.after_sides_straight(outs)
        (((total,)),) = do_tasks(
            place, [Adds([[wide.column(), narrow.column()]])], "sums_nine", (outs[0],)
        )
        parts = (
            (model // 2, folds),
            (hidden_units // 2, 1),
            (model // 2, 1),
            (3 * model // 2, 1),
            (LANES, 1),
        )
        grad_fc2, grad_fc1, grad_out, grad_qkv, sums = finish(place, replicas(total), parts)
        sums = jnp.concatenate([sums[:, :8], sums[:, LANES : LANES + 8]], axis=1).T
    else:

        def product(left, right):
            total = lax.psum_scatter(dot_tn(left, right), "fsdp", scatter_dimension=0, tiled=True)
            return lax.psum(total, "dp")

        grad_fc2 = product(active, cotangent)
        grad_fc1 = product(norm_two, d_pre)
        grad_out = product(mixed, dy1)
        grad_qkv = product(norm_one, d_joined)
        sums = lax.psum_scatter(sums, "fsdp", scatter_dimension=1, tiled=True)
        sums = lax.psum(sums, "dp")

    return (
        text_out.reshape(text_in.shape),
        image_out,
        text_grad.reshape(text_in.shape),
        sums[LN1_GAIN],
        sums[LN1_BIAS],
        grad_qkv,
        sums[Q_BIAS],
        sums[V_BIAS],
        grad_out,
        sums[OUT_BIAS],
        sums[LN2_GAIN],
        sums[LN2_BIAS],
        grad_fc1,
        sums[8 : 8 + folds].reshape(-1),
        grad_fc2,
        sums[FC2_BIAS],
    )


def solution(mesh):
    rows = P(("dp", "fsdp"), None, None)
    vector, matrix = P("fsdp"), P("fsdp", None)
    in_specs = (
        rows,
        P(("dp", "fsdp"), None),
        rows,
        rows,
        vector,
        vector,
        matrix,
        vector,
        vector,
        matrix,
        vector,
        vector,
        vector,
        matrix,
        vector,
        matrix,
        vector,
        P(None, "fsdp"),
        matrix,
        matrix,
        matrix,
        matrix,
    )
    out_specs = (
        rows,
        rows,
        rows,
        vector,
        vector,
        matrix,
        vector,
        vector,
        matrix,
        vector,
        vector,
        vector,
        matrix,
        vector,
        matrix,
        vector,
    )
    return jax.shard_map(
        per_device, mesh=mesh, in_specs=in_specs, out_specs=out_specs, check_vma=False
    )
```

```python
from functools import partial

import jax
import jax.numpy as jnp
from jax import lax
from jax.experimental import pallas as pl
from jax.experimental.pallas import tpu as pltpu
from jax.sharding import PartitionSpec as P

HEADS = 12
EPSILON = 1e-06
LANES = 128
TILE = 256
MIB = 1024 * 1024
F32 = jnp.float32
BF16 = jnp.bfloat16

LN1_GAIN, LN1_BIAS, Q_BIAS, V_BIAS, OUT_BIAS, LN2_GAIN, LN2_BIAS, FC2_BIAS = range(8)
IMAGE_GAIN_ONE, IMAGE_GAIN_TWO, FC1_BIAS = 8, 9, 10
VECTOR_ROWS = 16


def dot_nn(a, b):
    return lax.dot_general(a, b, (((1,), (0,)), ((), ())), preferred_element_type=F32)


def dot_nt(a, b):
    return lax.dot_general(a, b, (((1,), (1,)), ((), ())), preferred_element_type=F32)


def dot_tn(a, b):
    return lax.dot_general(a, b, (((0,), (0,)), ((), ())), preferred_element_type=F32)


def call(body, name, flops, moved, operands, after=(), num_prefetch=0, weight=1, **kwargs):
    grid_spec = kwargs.pop("grid_spec")
    first = num_prefetch + len(grid_spec["in_specs"])

    def ordered(*refs):
        return body(*refs[:first], *refs[first + len(after) :])

    grid_spec["in_specs"] = list(grid_spec["in_specs"]) + [
        pl.BlockSpec(memory_space=pltpu.HBM)
    ] * len(after)
    return pl.pallas_call(
        ordered,
        name=name,
        grid_spec=pltpu.PrefetchScalarGridSpec(num_scalar_prefetch=num_prefetch, **grid_spec),
        compiler_params=pltpu.CompilerParams(vmem_limit_bytes=63 * MIB),
        cost_estimate=pl.CostEstimate(
            flops=int(flops) * weight, bytes_accessed=int(moved), transcendentals=0
        ),
        **kwargs,
    )(*operands, *after)


class Part:
    def __init__(self, name, start, width, folds):
        self.name, self.start, self.width, self.folds = name, start, width, folds


def pack_parts(shapes):
    parts, at = {}, 0
    for name, (rows, columns), model in shapes:
        folds = rows // model
        parts[name] = Part(name, at, columns // 2, folds)
        at += folds * (columns // 2)
    return parts, at


def cut_body(plan, at, place, *refs):
    vectors, refs = (refs[0], refs[1:]) if at is not None else (None, refs)
    sources, outs = refs[: len(plan)], refs[len(plan) :]
    for source, (target, part) in zip(sources, plan):
        step = source.shape[0] // part.folds
        for fold in range(part.folds):
            left = part.start + fold * part.width
            outs[target][:, left : left + part.width] = source[fold * step : (fold + 1) * step, :]
    if vectors is None:
        return
    block = jnp.zeros((outs[0].shape[0], LANES), BF16)
    outs[0][:, at : at + LANES] = block
    outs[0][: vectors.shape[0], at : at + LANES] = vectors[...]


def cut_pieces(place, vectors, packs, after=()):
    plan, sources, shapes, specs = [], [], [], []
    for target, (parts, width, matrices) in enumerate(packs):
        for name, part in parts.items():
            plan.append((target, part))
            sources.append(matrices[name])
            rows = matrices[name].shape[0] // 2
            specs.append(pl.BlockSpec((rows, part.width), lambda i, place: (place[1], place[2])))
        width += LANES if vectors is not None else 0
        shapes.append(jax.ShapeDtypeStruct((rows // part.folds, width), BF16))
    return call(
        partial(cut_body, plan, None if vectors is None else packs[0][1]),
        "cut_pieces",
        0,
        sum(a.size for a in sources),
        (place, *([] if vectors is None else [vectors]), *sources),
        after=after,
        weight=1,
        num_prefetch=1,
        grid_spec=dict(
            grid=(1,),
            in_specs=(
                []
                if vectors is None
                else [pl.BlockSpec(vectors.shape, lambda i, place: (0, 0))]
            )
            + specs,
            out_specs=[pl.BlockSpec(a.shape, lambda i, place: (0, 0)) for a in shapes],
        ),
        out_shape=shapes,
    )


class Whole:
    def __init__(self, arrays):
        self.arrays = arrays

    def operands(self, names):
        self.asked = list(names)
        return [self.arrays[name] for name in names]

    def start(self, refs, place, names, targets, semaphores):
        for name in names:
            ref = refs[self.asked.index(name)]
            pltpu.make_async_copy(ref, targets[name], semaphores[name]).start()


def start_piece(source, parts, names, targets, semaphores, f, x, core):
    for name in names:
        part = parts[name]
        height = source.shape[0]
        first = f * (2 * part.folds * height) + x * (part.folds * height)
        for fold in range(part.folds):
            columns = part.start + fold * part.width
            pltpu.make_async_copy(
                source.at[:, pl.ds(columns, part.width)],
                targets[name].at[
                    pl.ds(pl.multiple_of(first + fold * height, 16), height),
                    pl.ds(pl.multiple_of(core * part.width, LANES), part.width),
                ],
                semaphores[name],
            ).start()


class Relative:
    def __init__(self, parts, buffers):
        self.parts, self.buffers = parts, buffers

    def operands(self, names):
        return [array for array, _ in self.buffers]

    def start(self, refs, place, names, targets, semaphores):
        f, x, core = place
        for ref, (_, (dy, dx, dc)) in zip(refs, self.buffers):
            for dz in range(ref.shape[0]):
                start_piece(
                    ref.at[dz],
                    self.parts,
                    names,
                    targets,
                    semaphores,
                    f ^ (dy + 2 * dz),
                    x ^ dx,
                    core ^ dc,
                )


class Listed:
    def __init__(self, parts, array):
        self.parts, self.array = parts, array

    def operands(self, names):
        return [self.array]

    def start(self, refs, place, names, targets, semaphores):
        (ref,) = refs

        def step(i, carry):
            start_piece(
                ref.at[i], self.parts, names, targets, semaphores, i // 4, (i // 2) % 2, i % 2
            )
            return carry

        lax.fori_loop(0, ref.shape[0], step, 0)


class Loader:
    def __init__(self, wanted, shapes):
        self.wanted, self.shapes = wanted, shapes
        self.names = [name for _, names in wanted for name in names]
        self.arrays = [a for source, names in wanted for a in source.operands(names)]
        self.specs = [pl.BlockSpec(memory_space=pltpu.HBM)] * len(self.arrays)
        self.scratch = [pltpu.VMEM(shapes[name], BF16) for name in self.names] + [
            pltpu.SemaphoreType.DMA((len(self.names),))
        ]
        self.bytes = sum(2 * shapes[name][0] * shapes[name][1] for name in self.names)

    def bind(self, refs, scratch, place_ref):
        self.refs = refs
        self.targets = dict(zip(self.names, scratch))
        self.semaphores = {name: scratch[-1].at[i] for i, name in enumerate(self.names)}
        self.place = (place_ref[0], place_ref[1], place_ref[2])
        return self

    def start(self, only=None):
        at = 0
        for source, names in self.wanted:
            count = len(source.operands(names))
            refs = self.refs[at : at + count]
            at += count
            names = [name for name in names if only is None or name in only]
            if names:
                source.start(refs, self.place, names, self.targets, self.semaphores)

    def wait(self, name):
        target = self.targets[name]
        pltpu.make_async_copy(target, target, self.semaphores[name]).wait()


def normed(values, gain, shift):
    centre = values - jnp.mean(values, axis=-1, keepdims=True)
    spread = lax.rsqrt(jnp.mean(centre * centre, axis=-1, keepdims=True) + EPSILON)
    return centre * spread * gain + shift


def norm_back(values, gain, grad):
    centre = values - jnp.mean(values, axis=-1, keepdims=True)
    spread = lax.rsqrt(jnp.mean(centre * centre, axis=-1, keepdims=True) + EPSILON)
    scaled = centre * spread
    grad_gain = jnp.sum(grad * scaled, axis=0, keepdims=True)
    grad_shift = jnp.sum(grad, axis=0, keepdims=True)
    inner = grad * gain
    inner = inner - jnp.mean(inner, axis=-1, keepdims=True) - scaled * jnp.mean(
        inner * scaled, axis=-1, keepdims=True
    )
    return inner * spread, grad_gain, grad_shift


def lane_sides(scale=1.0):
    lane = lax.broadcasted_iota(jnp.int32, (LANES, LANES), 1)
    left = jnp.where(lane < LANES // 2, scale, 0.0)
    return left.astype(BF16), (scale - left).astype(BF16)


def by_head(values, sides):
    return jnp.concatenate([values * sides[0], values * sides[1]], axis=0)


def pair_columns(width, pair):
    return [slice(third * width + pair * LANES, third * width + (pair + 1) * LANES) for third in range(3)]


def head_ones():
    row = lax.broadcasted_iota(jnp.int32, (2 * LANES, LANES), 0)
    lane = lax.broadcasted_iota(jnp.int32, (2 * LANES, LANES), 1)
    return jnp.where((row < LANES) == (lane < LANES // 2), 1.0, 0.0).astype(BF16)


def spread_ones():
    row = lax.broadcasted_iota(jnp.int32, (2 * LANES, 2 * LANES), 0)
    lane = lax.broadcasted_iota(jnp.int32, (2 * LANES, 2 * LANES), 1)
    return jnp.where((row % LANES < LANES // 2) == (lane < LANES), 1.0, 0.0).astype(BF16)


def attention(joined_ref, rows, width, allowed, store):
    sides, key_sides = lane_sides(), lane_sides((width // HEADS) ** -0.5)
    places = [pair_columns(width, pair) for pair in range(width // LANES)]
    scores = [
        dot_nt(joined_ref[rows, one], by_head(joined_ref[rows, two], key_sides))
        for one, two, _ in places
    ]
    weights = []
    for both in scores:
        parts = []
        for head in range(2):
            own = jnp.where(allowed, both[:, head * LANES : (head + 1) * LANES], -1e30)
            raised = jnp.exp(own - jnp.max(own, axis=-1, keepdims=True))
            parts.append(raised * (1.0 / jnp.sum(raised, axis=-1, keepdims=True)))
        weights.append(jnp.concatenate(parts, axis=1).astype(BF16))
    for pair, (low, (_, _, three)) in enumerate(zip(weights, places)):
        store(pair, low, by_head(joined_ref[rows, three], sides))


def gelu_both(values):
    below = 0.5 + 0.5 * lax.erf(values * 0.7071067811865476)
    bell = jnp.exp(values * values * -0.5) * 0.3989422804014327
    return values * below, below + values * bell


def text_attend_body(loader, n_sources, width, place, x_ref, ids_ref, vec_ref, *rest):
    sources, rest = rest[:n_sources], rest[n_sources:]
    pair_ref, joined_ref, weights_ref, exact_ref = rest[:4]
    load = loader.bind(sources, rest[4:], place)

    @pl.when(pl.program_id(0) == 0)
    def _():
        load.start()
        load.wait("qkv")

    w_qkv = load.targets["qkv"]
    values = x_ref[...].astype(F32)
    norm_one = normed(
        values, vec_ref[LN1_GAIN : LN1_GAIN + 1, :], vec_ref[LN1_BIAS : LN1_BIAS + 1, :]
    ).astype(BF16)
    pair_ref[:, :width] = norm_one
    for third, bias in enumerate((Q_BIAS, None, V_BIAS)):
        columns = slice(third * width, (third + 1) * width)
        product = dot_nn(norm_one, w_qkv[:, columns])
        if bias is not None:
            product = product + vec_ref[bias : bias + 1, :]
        joined_ref[:, columns] = product.astype(BF16)
    ones = head_ones()
    for part in range(x_ref.shape[0] // LANES):
        rows = slice(part * LANES, (part + 1) * LANES)
        ids = jnp.broadcast_to(ids_ref[part], (LANES, LANES))

        def store(pair, low, values):
            lanes = slice(pair * LANES, (pair + 1) * LANES)
            weights_ref[part, pair] = low
            both = dot_nn(low, jnp.concatenate([values, ones], axis=1))
            later = slice(width + pair * LANES, width + (pair + 1) * LANES)
            pair_ref[rows, later] = both[:, :LANES].astype(BF16)
            exact_ref[rows, lanes] = both[:, :LANES] / both[:, LANES:]

        attention(joined_ref, rows, width, ids == ids.T, store)


def text_forward_body(loader, n_sources, place, x_ref, mixed_ref, vec_ref, fc1_bias_ref, *rest):
    sources, rest = rest[:n_sources], rest[n_sources:]
    hidden_ref, active_ref, slope_ref = rest[:3]
    load = loader.bind(sources, rest[3:], place)
    first = pl.program_id(0) == 0

    @pl.when(first)
    def _():
        load.start(["out"])
        load.wait("out")
        load.start(["fc1"])

    hidden = (
        x_ref[...].astype(F32)
        + dot_nn(mixed_ref[...], load.targets["out"][...])
        + vec_ref[OUT_BIAS : OUT_BIAS + 1, :]
    )
    hidden_ref[...] = hidden
    norm_two = normed(
        hidden, vec_ref[LN2_GAIN : LN2_GAIN + 1, :], vec_ref[LN2_BIAS : LN2_BIAS + 1, :]
    ).astype(BF16)
    active_ref[:, slope_ref.shape[1] :] = norm_two

    @pl.when(first)
    def _():
        load.wait("fc1")

    w_fc1 = load.targets["fc1"]
    step = hidden.shape[1]
    for k in range(w_fc1.shape[1] // step):
        columns = slice(k * step, (k + 1) * step)
        pre_act = dot_nn(norm_two, w_fc1[:, columns]) + fc1_bias_ref[:, columns]
        active, slope = gelu_both(pre_act)
        active_ref[:, columns] = active.astype(BF16)
        slope_ref[:, columns] = slope.astype(BF16)


def text_back_body(loader, n_sources, place, g_ref, hidden_ref, slope_ref, vec_ref, *rest):
    sources, rest = rest[:n_sources], rest[n_sources:]
    pre_ref, share_ref, d_hidden_ref, d_mixed_ref, sums_ref, wide_ref = rest[:6]
    load = loader.bind(sources, rest[6:], place)
    first = pl.program_id(0) == 0

    @pl.when(first)
    def _():
        load.start(["fc2"])
        sums_ref[...] = jnp.zeros_like(sums_ref)
        wide_ref[...] = jnp.zeros_like(wide_ref)
        load.wait("fc2")
        load.start(["fc1", "out"])

    g = g_ref[...]
    w_fc2 = load.targets["fc2"]
    step = g.shape[1]
    for k in range(slope_ref.shape[1] // step):
        columns = slice(k * step, (k + 1) * step)
        low = (dot_nt(g, w_fc2[columns, :]) * slope_ref[:, columns].astype(F32)).astype(BF16)
        pre_ref[:, columns] = low
        half = slope_ref.shape[1] // 2

        @pl.when(place[2] != k * step // half)
        def _():
            share_ref[:, k * step % half : k * step % half + step] = low

        wide_ref[0:1, columns] += jnp.sum(low.astype(F32), axis=0, keepdims=True)

    @pl.when(first)
    def _():
        load.wait("fc1")
        load.wait("out")

    d_norm = dot_nt(pre_ref[...], load.targets["fc1"][...])
    part, gain, shift = norm_back(
        hidden_ref[...], vec_ref[LN2_GAIN : LN2_GAIN + 1, :], d_norm
    )
    d_hidden = g.astype(F32) + part
    d_hidden_ref[...] = d_hidden
    dy1 = d_hidden.astype(BF16)
    share_ref[:, slope_ref.shape[1] // 2 :] = dy1
    d_mixed_ref[...] = dot_nt(dy1, load.targets["out"][...]).astype(BF16)
    sums_ref[LN2_GAIN : LN2_GAIN + 1, :] += gain
    sums_ref[LN2_BIAS : LN2_BIAS + 1, :] += shift
    sums_ref[OUT_BIAS : OUT_BIAS + 1, :] += jnp.sum(dy1.astype(F32), axis=0, keepdims=True)
    sums_ref[FC2_BIAS : FC2_BIAS + 1, :] += jnp.sum(g.astype(F32), axis=0, keepdims=True)


def text_out_body(loader, n_sources, place, hidden_ref, active_ref, vec_ref, *rest):
    sources, rest = rest[:n_sources], rest[n_sources:]
    (out_ref,) = rest[:1]
    load = loader.bind(sources, rest[1:], place)

    @pl.when(pl.program_id(0) == 0)
    def _():
        load.start()
        load.wait("fc2")

    out_ref[...] = (
        hidden_ref[...]
        + dot_nn(active_ref[...], load.targets["fc2"][...])
        + vec_ref[FC2_BIAS : FC2_BIAS + 1, :]
    ).astype(BF16)


def text_unjoin_body(
    loader,
    n_sources,
    width,
    place,
    joined_ref,
    weights_ref,
    d_mixed_ref,
    exact_ref,
    x_ref,
    d_hidden_ref,
    vec_ref,
    begin_ref,
    *rest,
):
    sources, rest = rest[:n_sources], rest[n_sources:]
    d_joined_ref, share_ref, grad_ref, sums_ref = rest[:4]
    load = loader.bind(sources, rest[4:], place)
    start = pl.program_id(0) == 0

    @pl.when(start)
    def _():
        load.start()
        sums_ref[...] = begin_ref[...]

    scale = (width // HEADS) ** -0.5
    sides, key_sides = lane_sides(), lane_sides(scale)
    left = lax.broadcasted_iota(jnp.int32, (LANES, LANES), 1) < LANES // 2
    ones = spread_ones()
    places = [pair_columns(width, pair) for pair in range(width // LANES)]
    for part in range(joined_ref.shape[0] // LANES):
        rows = slice(part * LANES, (part + 1) * LANES)
        d_weights = [
            dot_nt(d_mixed_ref[rows, one], by_head(joined_ref[rows, three], sides))
            for one, _, three in places
        ]
        d_scores = []
        for pair, (one, _, _) in enumerate(places):
            product = d_mixed_ref[rows, one].astype(F32) * exact_ref[rows, one]
            high = product.astype(BF16)
            low = (product - high.astype(F32)).astype(BF16)
            total = dot_nn(jnp.concatenate([high, low], axis=1), ones)
            d_scores.append(
                (weights_ref[part, pair].astype(F32) * (d_weights[pair] - total)).astype(BF16)
            )
        for pair, (one, two, three) in enumerate(places):
            d_joined_ref[rows, one] = dot_nn(
                d_scores[pair], by_head(joined_ref[rows, two], key_sides)
            ).astype(BF16)
            d_keys = dot_tn(d_scores[pair], joined_ref[rows, one]) * scale
            d_joined_ref[rows, two] = jnp.where(left, d_keys[:LANES], d_keys[LANES:]).astype(BF16)
            d_values = dot_tn(weights_ref[part, pair], d_mixed_ref[rows, one])
            d_joined_ref[rows, three] = jnp.where(
                left, d_values[:LANES], d_values[LANES:]
            ).astype(BF16)
    for row, third in ((Q_BIAS, 0), (V_BIAS, 2)):
        columns = d_joined_ref[:, third * width : (third + 1) * width].astype(F32)
        sums_ref[row : row + 1, :] += jnp.sum(columns, axis=0, keepdims=True)

    @pl.when(start)
    def _():
        load.wait("qkv")

    half = share_ref.shape[1]
    theirs = pl.ds(pl.multiple_of((1 - place[2]) * half, LANES), half)
    share_ref[...] = d_joined_ref[:, theirs]
    d_norm = dot_nt(d_joined_ref[...], load.targets["qkv"][...])
    part, gain, shift = norm_back(
        x_ref[...].astype(F32), vec_ref[LN1_GAIN : LN1_GAIN + 1, :], d_norm
    )
    grad_ref[...] = d_hidden_ref[...] + part
    sums_ref[LN1_GAIN : LN1_GAIN + 1, :] += gain
    sums_ref[LN1_BIAS : LN1_BIAS + 1, :] += shift


def image_body(loader, n_sources, width, tokens, padded, place, x_ref, vec_ref, *rest):
    sources, rest = rest[:n_sources], rest[n_sources:]
    out_ref, joined_ref, mixed_ref, hidden_ref = rest[:4]
    load = loader.bind(sources, rest[4:], place)
    load.start()
    hidden_ref[...] = jnp.zeros_like(hidden_ref)
    for image in range(x_ref.shape[0]):
        hidden_ref[image * padded : image * padded + tokens, :] = x_ref[image].astype(F32)
    values = hidden_ref[...]
    norm_one = normed(values, vec_ref[IMAGE_GAIN_ONE : IMAGE_GAIN_ONE + 1, :], 0.0).astype(BF16)
    load.wait("qkv")
    w_qkv = load.targets["qkv"]
    for third in range(3):
        columns = slice(third * width, (third + 1) * width)
        joined_ref[:, columns] = dot_nn(norm_one, w_qkv[:, columns]).astype(BF16)
    row = lax.broadcasted_iota(jnp.int32, (LANES, LANES), 0)
    column = lax.broadcasted_iota(jnp.int32, (LANES, LANES), 1)
    allowed = (row // padded == column // padded) & (column % padded < tokens)
    for part in range(hidden_ref.shape[0] // LANES):
        rows = slice(part * LANES, (part + 1) * LANES)

        def store(pair, low, values):
            lanes = slice(pair * LANES, (pair + 1) * LANES)
            mixed_ref[rows, lanes] = dot_nn(low, values).astype(BF16)

        attention(joined_ref, rows, width, allowed, store)
    load.wait("out")
    hidden = values + dot_nn(mixed_ref[...], load.targets["out"][...])
    norm_two = normed(hidden, vec_ref[IMAGE_GAIN_TWO : IMAGE_GAIN_TWO + 1, :], 0.0).astype(BF16)
    hidden_ref[...] = hidden
    load.wait("fc1")
    load.wait("fc2")
    w_fc1, w_fc2 = load.targets["fc1"], load.targets["fc2"]
    for k in range(w_fc1.shape[1] // width):
        columns = slice(k * width, (k + 1) * width)
        pre_act = dot_nn(norm_two, w_fc1[:, columns])
        active = (pre_act * (0.5 + 0.5 * lax.erf(pre_act * 0.7071067811865476))).astype(BF16)
        hidden_ref[...] += dot_nn(active, w_fc2[columns, :])
    for image in range(x_ref.shape[0]):
        own = hidden_ref[image * padded : image * padded + tokens, :]
        out_ref[image] = own.astype(BF16)


SLOTS = 16
CORNERED = (0, 2, 1, 3, 4, 6, 12, 14, 9, 11, 13, 15, 5, 7, 8, 10)


class Job:
    def __init__(self, kind, lefts, rights, start, half, folds=1, wholes=(True, True)):
        self.kind, self.lefts, self.rights, self.start = kind, lefts, rights, start
        self.half, self.folds, self.wholes = half, folds, wholes
        self.width = half * folds
        self.block = half // 2 if half > 1152 else half


class Pieces:
    def __init__(self, jobs, model):
        self.jobs, self.model = jobs, model
        self.height = model // SLOTS
        self.width = sum(job.width for job in jobs)
        self.operands = []
        self.scratch = [pltpu.VMEM((SLOTS, self.height, self.width), BF16)]
        self.loads = self.flops = 0
        for job in jobs:
            self.operands += [array for array, _ in job.lefts]
            self.operands += [array for array, _ in job.rights]
            if job.kind == "sums":
                self.scratch += [
                    pltpu.VMEM((4, *job.lefts[0][0].shape), F32),
                    pltpu.VMEM((model, LANES), F32),
                ]
                self.loads += 4
                continue
            tokens = job.lefts[0][0].shape[0]
            self.scratch += [
                pltpu.VMEM((job.folds, 2 * tokens, model), BF16),
                pltpu.VMEM((2 * tokens, job.half), BF16),
                pltpu.VMEM((model, job.block), F32),
            ]
            self.loads += 2 * job.folds + 2 * job.half // job.block
            self.flops += 4 * tokens * model * job.width
        self.out_shape = [jax.ShapeDtypeStruct((4, self.height, self.width), BF16)] * 4
        self.moved = 2 * sum(a.size for a in self.operands)

    def steps(self, place, operands, outs, scratch, load, send):
        operands, scratch = list(operands), list(scratch)
        pieces = scratch.pop(0)
        steps = []
        f, x, core = place
        y, column = f % 2, f // 2
        height, model = self.height, self.model

        def put(slot, columns, value):
            pieces[CORNERED.index(slot), :, columns] = value.astype(BF16)

        def put_rows(total, columns):
            for slot in range(SLOTS):
                dy, dx, dz = slot // 8, (slot // 4) % 2, slot % 4
                first = ((f ^ (dy + 2 * dz)) * 2 + (x ^ dx)) * height
                put(slot, columns, total[pl.ds(pl.multiple_of(first, 16), height), :])
            for i, out in enumerate(outs):
                send(pieces.at[pl.ds(4 * i, 4), :, columns], out.at[:, :, columns])

        def rows_step(job, left, right, total, at):
            def compute():
                total[...] = dot_tn(left[0], right[:, at : at + job.block])
                put_rows(total, slice(job.start + at, job.start + at + job.block))

            return compute

        def folds_step(job, left, right, total, dz):
            rows = total.shape[0] // 2

            def compute():
                total[...] = dot_tn(left[dz], right[...])
                for dy in range(2):
                    for dx in range(2):
                        slot = dy * 8 + dx * 4 + dz
                        first = (y ^ dy) * rows + (x ^ dx) * (rows // 2)
                        for fold in range(job.folds):
                            lane = job.start + fold * job.half
                            top = pl.multiple_of(first + fold * height, 16)
                            put(slot, slice(lane, lane + job.half), total[pl.ds(top, height), :])
                        at = CORNERED.index(slot)
                        columns = slice(job.start, job.start + job.width)
                        send(pieces.at[at, :, columns], outs[at // 4].at[at % 4, :, columns])

            return compute

        def sums_step(job, table, total):
            def compute():
                own = jnp.where(core == 0, table[0] + table[1], table[2] + table[3])
                total[...] = jnp.concatenate([own] * (LANES // 8)).T
                put_rows(total, slice(job.start, job.start + LANES))

            return compute

        for job in self.jobs:
            left_refs = operands.pop(0), operands.pop(0)
            right_refs = operands.pop(0), operands.pop(0)
            if job.kind == "sums":
                table, total = scratch.pop(0), scratch.pop(0)
                loads = [load(ref, table.at[i]) for i, ref in enumerate(left_refs + right_refs)]
                steps.append((loads, sums_step(job, table, total)))
                continue
            left, right, total = scratch.pop(0), scratch.pop(0), scratch.pop(0)
            tokens = left.shape[1] // 2

            def load_left(fold, lane):
                return [
                    load(
                        ref.at[:, pl.ds(pl.multiple_of(first + lane, LANES), model)],
                        left.at[fold, pl.ds(i * tokens, tokens)],
                    )
                    for i, (ref, (_, first)) in enumerate(zip(left_refs, job.lefts))
                ]

            def load_right(at):
                copies = []
                for i, (ref, (_, first), both) in enumerate(
                    zip(right_refs, job.rights, job.wholes)
                ):
                    lane = first + at + (core * job.half if both else 0)
                    copies.append(
                        load(
                            ref.at[:, pl.ds(pl.multiple_of(lane, LANES), job.block)],
                            right.at[pl.ds(i * tokens, tokens), pl.ds(at, job.block)],
                        )
                    )
                return copies

            if job.kind == "folds":
                begin = load_right(0)
                for dz in range(job.folds):
                    steps.append(
                        (
                            begin + load_left(dz, (column ^ dz) * model),
                            folds_step(job, left, right, total, dz),
                        )
                    )
                    begin = []
                continue
            begin = load_left(0, 0)
            for at in range(0, job.half, job.block):
                steps.append((begin + load_right(at), rows_step(job, left, right, total, at)))
                begin = []
        return steps


class Adds:
    def __init__(self, groups):
        self.groups = groups
        self.operands, self.scratch, self.out_shape = [], [], []
        for sums in groups:
            count, height = sums[0][0][2], sums[0][0][0].shape[1]
            width = sum(pieces[0][0].shape[2] for pieces in sums)
            for pieces in sums:
                for piece in pieces:
                    self.operands.append(piece[0])
                    self.scratch.append(
                        pltpu.VMEM((count, height, pieces[0][0].shape[2]), BF16)
                    )
            self.out_shape.append(jax.ShapeDtypeStruct((count, height, width), BF16))
        self.scratch += [pltpu.VMEM(a.shape, BF16) for a in self.out_shape]
        self.loads = len(self.operands)
        self.flops = sum(a.size for a in self.out_shape)
        self.moved = 2 * sum(a.size for a in self.out_shape) * 4

    def steps(self, place, operands, outs, scratch, load, send):
        operands, scratch = list(operands), list(scratch)
        totals = scratch[len(operands) :]
        loads, work = [], []
        for sums, out, total in zip(self.groups, outs, totals):
            at = 0
            for pieces in sums:
                held = []
                for _, first, count, *lane in pieces:
                    source, target = operands.pop(0), scratch.pop(0)
                    lanes = pl.ds(lane[0] if lane else 0, target.shape[2])
                    loads.append(load(source.at[pl.ds(first, count), :, lanes], target))
                    held.append(target)
                work.append((held, total, slice(at, at + held[0].shape[2])))
                at += held[0].shape[2]

        def compute():
            for held, total, columns in work:
                value = held[0][...].astype(F32)
                for other in held[1:]:
                    value = value + other[...].astype(F32)
                total[:, :, columns] = value.astype(BF16)
            for out, total in zip(outs, totals):
                send(total, out)

        return [(loads, compute)]


def tasks_body(tasks, counts, place, *refs):
    n_in, n_out = sum(c[0] for c in counts), sum(c[1] for c in counts)
    ins, outs, held = refs[:n_in], refs[n_in : n_in + n_out], refs[n_in + n_out :]
    (in_sem, out_sem), held = held[:2], held[2:]
    where = (place[0], place[1], place[2])
    n_loads = 0

    def load(source, target):
        nonlocal n_loads
        copy = pltpu.make_async_copy(source, target, in_sem.at[n_loads])
        n_loads += 1
        return copy

    def send(source, target):
        pltpu.make_async_copy(source, target, out_sem).start()

    steps, at_in, at_out, at_held = [], 0, 0, 0
    for task, (a, b, c) in zip(tasks, counts):
        steps += task.steps(
            where,
            ins[at_in : at_in + a],
            outs[at_out : at_out + b],
            held[at_held : at_held + c],
            load,
            send,
        )
        at_in, at_out, at_held = at_in + a, at_out + b, at_held + c
    ahead = 1 if any(isinstance(task, Pieces) for task in tasks) else len(steps)
    for loads, _ in steps[:ahead]:
        for copy in loads:
            copy.start()
    for index, (loads, compute) in enumerate(steps):
        for copy in loads:
            copy.wait()
        for later, _ in steps[index + ahead : index + ahead + 1]:
            for copy in later:
                copy.start()
        compute()
    for out in outs:
        pltpu.make_async_copy(out, out, out_sem).wait()


def do_tasks(place, tasks, name, after=(), weight=1):
    counts = [(len(t.operands), len(t.out_shape), len(t.scratch)) for t in tasks]
    outs = call(
        partial(tasks_body, tasks, counts),
        name,
        sum(t.flops for t in tasks),
        sum(t.moved for t in tasks),
        (place, *[a for t in tasks for a in t.operands]),
        after=after,
        weight=weight,
        num_prefetch=1,
        grid_spec=dict(
            grid=(1,),
            in_specs=[pl.BlockSpec(memory_space=pl.ANY)] * sum(c[0] for c in counts),
            out_specs=[pl.BlockSpec(memory_space=pl.ANY)] * sum(c[1] for c in counts),
            scratch_shapes=[
                pltpu.SemaphoreType.DMA((sum(t.loads for t in tasks),)),
                pltpu.SemaphoreType.DMA,
            ]
            + [s for t in tasks for s in t.scratch],
        ),
        out_shape=[s for t in tasks for s in t.out_shape],
    )
    outs, results = list(outs), []
    for _, count, _ in counts:
        results.append(outs[:count])
        outs = outs[count:]
    return results


def swap(value, axis, bit):
    size = lax.axis_size(axis)
    return lax.ppermute(value, axis, [(i, i ^ bit) for i in range(size)])


def swap_corner(value):
    n = lax.axis_size("fsdp")
    pairs = [
        (d * n + i, (d ^ 2) * n + (i ^ 1)) for d in range(lax.axis_size("dp")) for i in range(n)
    ]
    return lax.ppermute(value, ("dp", "fsdp"), pairs)


def gate_body(count, *refs):
    pass


def gate(arrays, after):
    return call(
        partial(gate_body, len(arrays)),
        "gate",
        0,
        0,
        arrays,
        after=after,
        grid_spec=dict(
            grid=(1,),
            in_specs=[pl.BlockSpec(memory_space=pl.ANY)] * len(arrays),
            out_specs=[pl.BlockSpec(memory_space=pl.ANY)] * len(arrays),
        ),
        out_shape=[jax.ShapeDtypeStruct(a.shape, a.dtype) for a in arrays],
        input_output_aliases={i: i for i in range(len(arrays))},
    )


def gather_column(own):
    return jnp.stack([own] + [swap(own, "fsdp", bit) for bit in (2, 4, 6)])


def gather_pieces(column):
    return column, swap(column, "fsdp", 1), swap(column, "dp", 2), swap_corner(column)


def both_cores(here):
    places = ((0, 0), (1, 0), (0, 1), (1, 1))
    return [(a, at + (0,)) for a, at in zip(here, places)] + [
        (swap(a, "dp", 1), at + (1,)) for a, at in zip(here, places)
    ]


def gathered_vectors(buffers, rows, at, width, f):
    held = jnp.stack([buffers[i][0][:, :rows, at : at + width] for i in range(2)])
    held = held.reshape(2, 2, 2, rows, width)
    for axis, bit in ((0, 1), (1, 4), (2, 2)):
        held = jnp.where((f & bit) != 0, jnp.flip(held, axis), held)
    return held.transpose(3, 1, 2, 0, 4).reshape(rows, 8 * width)


class Reduction:
    def __init__(self, *sets):
        self.sets = [
            (own, swap(across, "dp", 2), swap(beside, "fsdp", 1), later)
            for own, across, beside, later in sets
        ]

    def corners(self):
        return Adds(
            [
                [[(later, 0, 2), (beside, 2, 2)] for _, _, beside, later in self.sets],
                [[(later, 2, 2), (across, 2, 2)] for _, across, _, later in self.sets],
            ]
        )

    def after_corners(self, outs):
        x_odd, y_even = outs
        self.x_odd, self.y_even = swap(x_odd, "dp", 2), swap(y_even, "fsdp", 1)

    def sides(self, straight=False):
        groups = []
        for odd in range(2):
            for at, count in ((0, 1), (1, 1)) if straight else ((0, 2),):
                sums, lane = [], 0
                for own, across, beside, _ in self.sets:
                    width = own.shape[2]
                    near, far = (beside, self.x_odd) if odd else (across, self.y_even)
                    sums.append(
                        [
                            (own, 2 * odd + at, count),
                            (near, at, count),
                            (far, at, count, lane),
                        ]
                    )
                    lane += width
                groups.append(sums)
        return Adds(groups)

    def after_sides(self, outs):
        self.low, high = outs
        self.high = swap(high, "fsdp", 2)

    def halves(self):
        return Adds([[[(self.low, i, 1), (self.high, i, 1)]] for i in range(2)])

    def after_halves(self, outs):
        own, send = outs
        self.last = [own, swap(send, "fsdp", 4)]

    def after_sides_straight(self, outs):
        own, two, one, three = outs
        self.last = [own, swap(one, "fsdp", 2), swap(two, "fsdp", 4), swap(three, "fsdp", 6)]

    def column(self):
        return [(a, 0, 1) for a in self.last]


def replicas(total):
    total = total[0]
    across = swap(total, "dp", 2)
    return total, across, swap(total, "dp", 1), swap(across, "dp", 1)


def finish_body(lots, place, *refs):
    refs, outs = refs[: 4 * len(lots)], list(refs[4 * len(lots) :])
    x_first, core_first = place[1] == 0, place[2] == 0
    for parts in lots:
        own_ref, across_ref, other_ref, diagonal_ref = refs[:4]
        refs = refs[4:]
        sides = []
        for mine, theirs in ((own_ref, across_ref), (other_ref, diagonal_ref)):
            mine, theirs = mine[...].astype(F32), theirs[...].astype(F32)
            sides.append((jnp.where(x_first, mine, theirs), jnp.where(x_first, theirs, mine)))
        at = 0
        for width, folds in parts:
            out = outs.pop(0)
            height = own_ref.shape[0]
            for dx in range(2):
                one, two = sides[0][dx], sides[1][dx]
                for fold in range(folds):
                    lanes = slice(at + fold * width, at + (fold + 1) * width)
                    rows = slice((dx * folds + fold) * height, (dx * folds + fold + 1) * height)
                    out[rows, :width] = jnp.where(core_first, one[:, lanes], two[:, lanes])
                    out[rows, width:] = jnp.where(core_first, two[:, lanes], one[:, lanes])
            at += width * folds


def finish(place, lots, parts):
    arrays = [a for lot in lots for a in lot]
    height = arrays[0].shape[0]
    shapes = [(2 * folds * height, 2 * columns) for lot in parts for columns, folds in lot]
    return call(
        partial(finish_body, parts),
        "finish",
        0,
        sum(a.size for a in arrays) * 6,
        (place, *arrays),
        num_prefetch=1,
        grid_spec=dict(
            grid=(1,),
            in_specs=[pl.BlockSpec(a.shape, lambda i, place: (0, 0)) for a in arrays],
            out_specs=[pl.BlockSpec(shape, lambda i, place: (0, 0)) for shape in shapes],
        ),
        out_shape=[jax.ShapeDtypeStruct(shape, F32) for shape in shapes],
    )


def per_device(
    text_in,
    text_segments,
    text_cotangent,
    image_in,
    ln1_gain,
    ln1_bias,
    w_qkv,
    q_bias,
    v_bias,
    w_out,
    out_bias,
    ln2_gain,
    ln2_bias,
    w_fc1,
    fc1_bias,
    w_fc2,
    fc2_bias,
    image_norms,
    image_qkv,
    image_proj,
    image_fc1,
    image_fc2,
):
    n_fsdp, n_dp = lax.axis_size("fsdp"), lax.axis_size("dp")
    batch_rows, length, model = text_in.shape
    hidden_units = w_fc1.shape[1]
    tokens = batch_rows * length
    folds = hidden_units // model
    f, replica = lax.axis_index("fsdp"), lax.axis_index("dp")
    x, core = replica // 2, replica % 2
    place = jnp.stack([f, x, core]).astype(jnp.int32)
    shard = model // n_fsdp
    by_pieces = n_fsdp == 8 and n_dp == 4 and shard % 32 == 0

    shapes = {
        "qkv": (model, 3 * model),
        "out": (model, model),
        "fc1": (model, hidden_units),
        "fc2": (hidden_units, model),
    }
    text = {"qkv": w_qkv, "out": w_out, "fc1": w_fc1, "fc2": w_fc2}
    image = {"qkv": image_qkv, "out": image_proj, "fc1": image_fc1, "fc2": image_fc2}

    def parts_of(names):
        return pack_parts([(name, shapes[name], model) for name in names])

    vectors = jnp.concatenate(
        [
            jnp.stack(
                [ln1_gain, ln1_bias, q_bias, v_bias, out_bias, ln2_gain, ln2_bias, fc2_bias]
            ),
            image_norms,
            fc1_bias.reshape(folds, shard),
        ]
    )
    vectors = jnp.pad(vectors, ((0, VECTOR_ROWS - vectors.shape[0]), (0, 0)))
    if by_pieces:
        names = ("qkv",), ("fc2",), ("out", "fc1"), ("qkv", "out", "fc1", "fc2")
        packs = [parts_of(each) + (text,) for each in names[:3]] + [parts_of(names[3]) + (image,)]
        lanes = jnp.pad(vectors, ((0, 0), (0, LANES - shard)))
        cuts = cut_pieces(place, None, packs[1:])
        cuts = cut_pieces(place, lanes, packs[:1], (cuts[0],)) + cuts
        text_qkv = Relative(packs[0][0], both_cores(gather_pieces(gather_column(cuts[0]))))
        (own,) = gate([cuts[1]], (text_qkv.buffers[0][0],))
        column_fc2 = gather_column(own)
        early = (column_fc2,)
        text_rest = Listed(packs[2][0], lax.all_gather(cuts[2], ("fsdp", "dp")))
        vectors = gathered_vectors(text_qkv.buffers, VECTOR_ROWS, packs[0][1], shard, f)
        vectors = vectors.astype(F32)
    else:
        vectors = lax.all_gather(vectors, "fsdp", axis=1, tiled=True).astype(F32)
        gathered = {n: lax.all_gather(a, "fsdp", axis=0, tiled=True) for n, a in text.items()}
        text_qkv = text_fc2 = text_rest = Whole(gathered)
        image_source = Whole(
            {n: lax.all_gather(a, "fsdp", axis=0, tiled=True) for n, a in image.items()}
        )
    fc1_vector = vectors[FC1_BIAS : FC1_BIAS + folds].reshape(folds, n_fsdp, shard)
    fc1_vector = fc1_vector.transpose(1, 0, 2).reshape(1, hidden_units)

    inflow = text_in.reshape(tokens, model)
    cotangent = text_cotangent.reshape(tokens, model)
    ids = text_segments + 16 * (lax.broadcasted_iota(jnp.int32, text_segments.shape, 0) % (LANES // length))
    ids = ids.astype(F32).reshape(tokens // LANES, 1, LANES)
    steps = tokens // TILE
    groups = TILE // LANES
    pairs = model // LANES

    def rows_of(width):
        return pl.BlockSpec((TILE, width), lambda i, place: (i, 0))

    def fixed(*shape):
        return pl.BlockSpec(shape, lambda i, place: (0,) * len(shape))

    def array(*shape, dtype=BF16):
        return jax.ShapeDtypeStruct(shape, dtype)

    weights_spec = pl.BlockSpec((groups, pairs, LANES, 2 * LANES), lambda i, place: (i, 0, 0, 0))
    vec_spec = fixed(VECTOR_ROWS, model)

    def run(body, wanted, name, flops, moved, in_specs, out_specs, out_shape, operands, grid=(steps,), extra=(), after=(), weight=1):
        loader = Loader(wanted, shapes)
        return call(
            partial(body, loader, len(loader.arrays)),
            name,
            flops,
            moved + loader.bytes,
            (place, *operands, *loader.arrays),
            after=after,
            weight=weight,
            num_prefetch=1,
            grid_spec=dict(
                grid=grid,
                in_specs=list(in_specs) + loader.specs,
                out_specs=out_specs,
                scratch_shapes=list(extra) + loader.scratch,
            ),
            out_shape=out_shape,
        )

    def bind(body, *values):
        return lambda loader, count, *refs: body(loader, count, *values, *refs)

    square = 2 * tokens * model * model
    def columns_of(width, index):
        return pl.BlockSpec((TILE, width), lambda i, place: (i, index))

    if not by_pieces:
        early = ()
    pair, joined, weights, exact = run(
        bind(text_attend_body, model),
        [(text_qkv, ["qkv"])],
        "text_attend",
        4 * square,
        tokens * model * 24,
        [rows_of(model), pl.BlockSpec((groups, 1, LANES), lambda i, place: (i, 0, 0)), vec_spec],
        [rows_of(2 * model), rows_of(3 * model), weights_spec, rows_of(model)],
        [
            array(tokens, 2 * model),
            array(tokens, 3 * model),
            array(tokens // LANES, pairs, LANES, 2 * LANES),
            array(tokens, model, dtype=F32),
        ],
        (inflow, ids, vectors),
        after=early,
    )
    done = (pair,)
    if by_pieces:
        (column_fc2,) = gate([column_fc2], done)
        pieces_fc2 = gather_pieces(column_fc2)
        their_pair, their_cotangent = swap(pair, "dp", 1), swap(cotangent, "dp", 1)
        done = (column_fc2,)
    hidden, forward, slope = run(
        text_forward_body,
        [(text_rest, ["out", "fc1"])],
        "text_forward",
        (1 + folds) * square,
        tokens * model * (10 + 4 * folds),
        [rows_of(model), columns_of(model, 1), vec_spec, fixed(1, hidden_units)],
        [rows_of(model), rows_of(hidden_units + model), rows_of(hidden_units)],
        [
            array(tokens, model, dtype=F32),
            array(tokens, hidden_units + model),
            array(tokens, hidden_units),
        ],
        (inflow, pair, vectors, fc1_vector),
        after=done,
    )
    done = (forward,)
    if by_pieces:
        *pieces_fc2, own = gate([*pieces_fc2, cuts[3]], (*done, their_pair, their_cotangent))
        image_source = Listed(packs[3][0], lax.all_gather(own, ("fsdp", "dp")))
        text_fc2 = Relative(packs[1][0], both_cores(pieces_fc2))
        (forward,) = gate([forward], [a for a, _ in text_fc2.buffers[4:]])
        done = (forward,)
        their_forward = swap(forward, "dp", 1)
    d_pre, share, d_hidden, d_mixed, sums_two, sums_wide = run(
        text_back_body,
        [(text_fc2, ["fc2"]), (text_rest, ["fc1", "out"])],
        "text_back",
        (1 + 2 * folds) * square,
        tokens * model * (16 + 4 * folds),
        [rows_of(model), rows_of(model), rows_of(hidden_units), vec_spec],
        [
            rows_of(hidden_units),
            rows_of(hidden_units // 2 + model),
            rows_of(model),
            rows_of(model),
            fixed(8, model),
            fixed(8, hidden_units),
        ],
        [
            array(tokens, hidden_units),
            array(tokens, hidden_units // 2 + model),
            array(tokens, model, dtype=F32),
            array(tokens, model),
            array(8, model, dtype=F32),
            array(8, hidden_units, dtype=F32),
        ],
        (cotangent, hidden, slope, vectors),
        after=done,
    )
    done = (d_mixed,)
    units = sums_wide[0].reshape(n_fsdp, folds, shard).transpose(1, 0, 2).reshape(folds, model)
    units = jnp.pad(units, ((0, 8 - folds), (0, 0)))
    if by_pieces:
        their_share, their_units = swap(share, "dp", 1), swap(units, "dp", 1)
        jobs = [
            Job(
                "folds",
                [(forward, 0), (their_forward, 0)],
                [(cotangent, 0), (their_cotangent, 0)],
                0,
                model // 2,
                folds,
            )
        ]
        (first,) = do_tasks(place, [Pieces(jobs, model)], "grads_one", done)
        half = hidden_units // 2
        jobs = [
            Job(
                "rows",
                [(forward, hidden_units), (their_forward, hidden_units)],
                [(d_pre, 0), (their_share, 0)],
                0,
                half,
                wholes=(True, False),
            ),
            Job(
                "rows",
                [(pair, model), (their_pair, model)],
                [(share, half), (their_share, half)],
                half,
                model // 2,
            ),
        ]
        (second,) = do_tasks(place, [Pieces(jobs, model)], "grads_two", (first[0],))
        wide = Reduction(first, second)
        done = second[0], their_units, *wide.sets[0][1:3]
    d_joined, share, text_grad, sums_one = run(
        bind(text_unjoin_body, model),
        [(text_qkv, ["qkv"])],
        "text_unjoin",
        5 * square,
        tokens * model * 32,
        [
            rows_of(3 * model),
            weights_spec,
            rows_of(model),
            rows_of(model),
            rows_of(model),
            rows_of(model),
            vec_spec,
            fixed(8, model),
        ],
        [rows_of(3 * model), rows_of(3 * model // 2), rows_of(model), fixed(8, model)],
        [
            array(tokens, 3 * model),
            array(tokens, 3 * model // 2),
            array(tokens, model, dtype=F32),
            array(8, model, dtype=F32),
        ],
        (joined, weights, d_mixed, exact, inflow, d_hidden, vectors, sums_two),
        after=done,
    )
    done = (text_grad,)
    if by_pieces:
        their_share, their_sums = swap(share, "dp", 1), swap(sums_one, "dp", 1)
    text_out = run(
        text_out_body,
        [(text_fc2, ["fc2"])],
        "text_out",
        folds * square,
        tokens * model * (6 + 2 * folds),
        [rows_of(model), rows_of(hidden_units), vec_spec],
        rows_of(model),
        array(tokens, model),
        (hidden, forward, vectors),
        after=done,
    )
    done = (text_out,)
    if by_pieces:
        (outs,) = do_tasks(place, [wide.corners()], "sums_one", done, weight=100000)
        wide.after_corners(outs)
        jobs = [
            Job(
                "rows",
                [(pair, 0), (their_pair, 0)],
                [(d_joined, 0), (their_share, 0)],
                0,
                3 * model // 2,
                wholes=(True, False),
            ),
            Job(
                "sums",
                [(sums_one, 0), (their_sums, 0)],
                [(units, 0), (their_units, 0)],
                3 * model // 2,
                LANES,
            ),
        ]
        (slots,) = do_tasks(place, [Pieces(jobs, model)], "grads_three", (outs[0],))
        narrow = Reduction(slots)
        (outs,) = do_tasks(place, [wide.sides()], "sums_two", (slots[0],))
        wide.after_sides(outs)
        done = (outs[0],)

    images, image_tokens, _ = image_in.shape
    padded = -(-image_tokens // 64) * 64
    held = images * padded
    image_out = run(
        bind(image_body, model, image_tokens, padded),
        [(image_source, ["qkv", "out", "fc1", "fc2"])],
        "image_block",
        2 * held * model * model * (4 + 2 * folds),
        4 * held * model,
        [fixed(*image_in.shape), vec_spec],
        fixed(*image_in.shape),
        array(*image_in.shape),
        (image_in, vectors),
        grid=(1,),
        extra=[
            pltpu.VMEM((held, 3 * model), BF16),
            pltpu.VMEM((held, model), BF16),
            pltpu.VMEM((held, model), F32),
        ],
        after=done,
    )
    done = (image_out,)

    if by_pieces:
        first, second = do_tasks(place, [narrow.corners(), wide.halves()], "sums_three", done)
        narrow.after_corners(first)
        wide.after_halves(second)
        (outs,) = do_tasks(place, [narrow.sides(straight=True)], "sums_four", (first[0],))
        narrow.after_sides_straight(outs)
        (((total,)),) = do_tasks(place, [Adds([[wide.column()]])], "sums_five", (outs[0],))
        early = replicas(total)
        (((total,)),) = do_tasks(place, [Adds([[narrow.column()]])], "sums_six", (total,))
        parts = ((model // 2, folds), (hidden_units // 2, 1), (model // 2, 1)), (
            (3 * model // 2, 1),
            (LANES, 1),
        )
        grad_fc2, grad_fc1, grad_out, grad_qkv, sums = finish(
            place, (early, replicas(total)), parts
        )
        sums = jnp.concatenate([sums[:, :8], sums[:, LANES : LANES + 8]], axis=1).T
    else:

        def product(left, right):
            total = lax.psum_scatter(dot_tn(left, right), "fsdp", scatter_dimension=0, tiled=True)
            return lax.psum(total, "dp")

        grad_fc2 = product(forward[:, :hidden_units], cotangent)
        grad_fc1 = product(forward[:, hidden_units:], d_pre)
        grad_out = product(pair[:, model:], d_hidden.astype(BF16))
        grad_qkv = product(pair[:, :model], d_joined)
        sums = jnp.concatenate([sums_one, units])
        sums = lax.psum_scatter(sums, "fsdp", scatter_dimension=1, tiled=True)
        sums = lax.psum(sums, "dp")

    return (
        text_out.reshape(text_in.shape),
        image_out,
        text_grad.reshape(text_in.shape),
        sums[LN1_GAIN],
        sums[LN1_BIAS],
        grad_qkv,
        sums[Q_BIAS],
        sums[V_BIAS],
        grad_out,
        sums[OUT_BIAS],
        sums[LN2_GAIN],
        sums[LN2_BIAS],
        grad_fc1,
        sums[8 : 8 + folds].reshape(-1),
        grad_fc2,
        sums[FC2_BIAS],
    )


def solution(mesh):
    rows = P(("dp", "fsdp"), None, None)
    vector, matrix = P("fsdp"), P("fsdp", None)
    in_specs = (
        rows,
        P(("dp", "fsdp"), None),
        rows,
        rows,
        vector,
        vector,
        matrix,
        vector,
        vector,
        matrix,
        vector,
        vector,
        vector,
        matrix,
        vector,
        matrix,
        vector,
        P(None, "fsdp"),
        matrix,
        matrix,
        matrix,
        matrix,
    )
    out_specs = (
        rows,
        rows,
        rows,
        vector,
        vector,
        matrix,
        vector,
        vector,
        matrix,
        vector,
        vector,
        vector,
        matrix,
        vector,
        matrix,
        vector,
    )
    return jax.shard_map(
        per_device, mesh=mesh, in_specs=in_specs, out_specs=out_specs, check_vma=False
    )
```

```python
from functools import partial

import jax
import jax.numpy as jnp
from jax import lax
from jax.experimental import pallas as pl
from jax.experimental.pallas import tpu as pltpu
from jax.sharding import PartitionSpec as P

HEADS = 12
EPSILON = 1e-06
LANES = 128
TILE = 256
MIB = 1024 * 1024
F32 = jnp.float32
BF16 = jnp.bfloat16

LN1_GAIN, LN1_BIAS, Q_BIAS, V_BIAS, OUT_BIAS, LN2_GAIN, LN2_BIAS, FC2_BIAS = range(8)
IMAGE_GAIN_ONE, IMAGE_GAIN_TWO, FC1_BIAS = 8, 9, 10
VECTOR_ROWS = 16


def dot_nn(a, b):
    return lax.dot_general(a, b, (((1,), (0,)), ((), ())), preferred_element_type=F32)


def dot_nt(a, b):
    return lax.dot_general(a, b, (((1,), (1,)), ((), ())), preferred_element_type=F32)


def dot_tn(a, b):
    return lax.dot_general(a, b, (((0,), (0,)), ((), ())), preferred_element_type=F32)


def call(body, name, flops, moved, operands, after=(), num_prefetch=0, weight=1, **kwargs):
    grid_spec = kwargs.pop("grid_spec")
    first = num_prefetch + len(grid_spec["in_specs"])

    def ordered(*refs):
        return body(*refs[:first], *refs[first + len(after) :])

    grid_spec["in_specs"] = list(grid_spec["in_specs"]) + [
        pl.BlockSpec(memory_space=pltpu.HBM)
    ] * len(after)
    return pl.pallas_call(
        ordered,
        name=name,
        grid_spec=pltpu.PrefetchScalarGridSpec(num_scalar_prefetch=num_prefetch, **grid_spec),
        compiler_params=pltpu.CompilerParams(vmem_limit_bytes=63 * MIB),
        cost_estimate=pl.CostEstimate(
            flops=int(flops) * weight, bytes_accessed=int(moved), transcendentals=0
        ),
        **kwargs,
    )(*operands, *after)


class Part:
    def __init__(self, name, start, width, folds):
        self.name, self.start, self.width, self.folds = name, start, width, folds


def pack_parts(shapes):
    parts, at = {}, 0
    for name, (rows, columns), model in shapes:
        folds = rows // model
        parts[name] = Part(name, at, columns // 2, folds)
        at += folds * (columns // 2)
    return parts, at


def cut_body(plan, at, place, *refs):
    vectors, refs = (refs[0], refs[1:]) if at is not None else (None, refs)
    sources, outs = refs[: len(plan)], refs[len(plan) :]
    for source, (target, part) in zip(sources, plan):
        step = source.shape[0] // part.folds
        for fold in range(part.folds):
            left = part.start + fold * part.width
            outs[target][:, left : left + part.width] = source[fold * step : (fold + 1) * step, :]
    if vectors is None:
        return
    block = jnp.zeros((outs[0].shape[0], LANES), BF16)
    outs[0][:, at : at + LANES] = block
    outs[0][: vectors.shape[0], at : at + LANES] = vectors[...]


def cut_pieces(place, vectors, packs, after=()):
    plan, sources, shapes, specs = [], [], [], []
    for target, (parts, width, matrices) in enumerate(packs):
        for name, part in parts.items():
            plan.append((target, part))
            sources.append(matrices[name])
            rows = matrices[name].shape[0] // 2
            specs.append(pl.BlockSpec((rows, part.width), lambda i, place: (place[1], place[2])))
        width += LANES if vectors is not None else 0
        shapes.append(jax.ShapeDtypeStruct((rows // part.folds, width), BF16))
    return call(
        partial(cut_body, plan, None if vectors is None else packs[0][1]),
        "cut_pieces",
        0,
        sum(a.size for a in sources),
        (place, *([] if vectors is None else [vectors]), *sources),
        after=after,
        weight=1,
        num_prefetch=1,
        grid_spec=dict(
            grid=(1,),
            in_specs=(
                []
                if vectors is None
                else [pl.BlockSpec(vectors.shape, lambda i, place: (0, 0))]
            )
            + specs,
            out_specs=[pl.BlockSpec(a.shape, lambda i, place: (0, 0)) for a in shapes],
        ),
        out_shape=shapes,
    )


class Whole:
    def __init__(self, arrays):
        self.arrays = arrays

    def operands(self, names):
        self.asked = list(names)
        return [self.arrays[name] for name in names]

    def start(self, refs, place, names, targets, semaphores):
        for name in names:
            ref = refs[self.asked.index(name)]
            pltpu.make_async_copy(ref, targets[name], semaphores[name]).start()


def start_piece(source, parts, names, targets, semaphores, f, x, core):
    for name in names:
        part = parts[name]
        height = source.shape[0]
        first = f * (2 * part.folds * height) + x * (part.folds * height)
        for fold in range(part.folds):
            columns = part.start + fold * part.width
            pltpu.make_async_copy(
                source.at[:, pl.ds(columns, part.width)],
                targets[name].at[
                    pl.ds(pl.multiple_of(first + fold * height, 16), height),
                    pl.ds(pl.multiple_of(core * part.width, LANES), part.width),
                ],
                semaphores[name],
            ).start()


class Relative:
    def __init__(self, parts, buffers):
        self.parts, self.buffers = parts, buffers

    def operands(self, names):
        return [array for array, _ in self.buffers]

    def start(self, refs, place, names, targets, semaphores):
        f, x, core = place
        for ref, (_, (dy, dx, dc)) in zip(refs, self.buffers):
            for dz in range(ref.shape[0]):
                start_piece(
                    ref.at[dz],
                    self.parts,
                    names,
                    targets,
                    semaphores,
                    f ^ (dy + 2 * dz),
                    x ^ dx,
                    core ^ dc,
                )


class Listed:
    def __init__(self, parts, array):
        self.parts, self.array = parts, array

    def operands(self, names):
        return [self.array]

    def start(self, refs, place, names, targets, semaphores):
        (ref,) = refs

        def step(i, carry):
            start_piece(
                ref.at[i], self.parts, names, targets, semaphores, i // 4, (i // 2) % 2, i % 2
            )
            return carry

        lax.fori_loop(0, ref.shape[0], step, 0)


class Loader:
    def __init__(self, wanted, shapes):
        self.wanted, self.shapes = wanted, shapes
        self.names = [name for _, names in wanted for name in names]
        self.arrays = [a for source, names in wanted for a in source.operands(names)]
        self.specs = [pl.BlockSpec(memory_space=pltpu.HBM)] * len(self.arrays)
        self.scratch = [pltpu.VMEM(shapes[name], BF16) for name in self.names] + [
            pltpu.SemaphoreType.DMA((len(self.names),))
        ]
        self.bytes = sum(2 * shapes[name][0] * shapes[name][1] for name in self.names)

    def bind(self, refs, scratch, place_ref):
        self.refs = refs
        self.targets = dict(zip(self.names, scratch))
        self.semaphores = {name: scratch[-1].at[i] for i, name in enumerate(self.names)}
        self.place = (place_ref[0], place_ref[1], place_ref[2])
        return self

    def start(self, only=None):
        at = 0
        for source, names in self.wanted:
            count = len(source.operands(names))
            refs = self.refs[at : at + count]
            at += count
            names = [name for name in names if only is None or name in only]
            if names:
                source.start(refs, self.place, names, self.targets, self.semaphores)

    def wait(self, name):
        target = self.targets[name]
        pltpu.make_async_copy(target, target, self.semaphores[name]).wait()


def normed(values, gain, shift):
    centre = values - jnp.mean(values, axis=-1, keepdims=True)
    spread = lax.rsqrt(jnp.mean(centre * centre, axis=-1, keepdims=True) + EPSILON)
    return centre * spread * gain + shift


def norm_back(values, gain, grad):
    centre = values - jnp.mean(values, axis=-1, keepdims=True)
    spread = lax.rsqrt(jnp.mean(centre * centre, axis=-1, keepdims=True) + EPSILON)
    scaled = centre * spread
    grad_gain = jnp.sum(grad * scaled, axis=0, keepdims=True)
    grad_shift = jnp.sum(grad, axis=0, keepdims=True)
    inner = grad * gain
    inner = inner - jnp.mean(inner, axis=-1, keepdims=True) - scaled * jnp.mean(
        inner * scaled, axis=-1, keepdims=True
    )
    return inner * spread, grad_gain, grad_shift


def lane_sides(scale=1.0):
    lane = lax.broadcasted_iota(jnp.int32, (LANES, LANES), 1)
    left = jnp.where(lane < LANES // 2, scale, 0.0)
    return left.astype(BF16), (scale - left).astype(BF16)


def by_head(values, sides):
    return jnp.concatenate([values * sides[0], values * sides[1]], axis=0)


def pair_columns(width, pair):
    return [slice(third * width + pair * LANES, third * width + (pair + 1) * LANES) for third in range(3)]


def head_ones():
    row = lax.broadcasted_iota(jnp.int32, (2 * LANES, LANES), 0)
    lane = lax.broadcasted_iota(jnp.int32, (2 * LANES, LANES), 1)
    return jnp.where((row < LANES) == (lane < LANES // 2), 1.0, 0.0).astype(BF16)


def spread_ones():
    row = lax.broadcasted_iota(jnp.int32, (2 * LANES, 2 * LANES), 0)
    lane = lax.broadcasted_iota(jnp.int32, (2 * LANES, 2 * LANES), 1)
    return jnp.where((row % LANES < LANES // 2) == (lane < LANES), 1.0, 0.0).astype(BF16)


def attention(joined_ref, rows, width, allowed, store):
    sides, key_sides = lane_sides(), lane_sides((width // HEADS) ** -0.5)
    places = [pair_columns(width, pair) for pair in range(width // LANES)]
    scores = [
        dot_nt(joined_ref[rows, one], by_head(joined_ref[rows, two], key_sides))
        for one, two, _ in places
    ]
    weights = []
    for both in scores:
        parts = []
        for head in range(2):
            own = jnp.where(allowed, both[:, head * LANES : (head + 1) * LANES], -1e30)
            raised = jnp.exp(own - jnp.max(own, axis=-1, keepdims=True))
            parts.append(raised * (1.0 / jnp.sum(raised, axis=-1, keepdims=True)))
        weights.append(jnp.concatenate(parts, axis=1).astype(BF16))
    for pair, (low, (_, _, three)) in enumerate(zip(weights, places)):
        store(pair, low, by_head(joined_ref[rows, three], sides))


def gelu_both(values):
    below = 0.5 + 0.5 * lax.erf(values * 0.7071067811865476)
    bell = jnp.exp(values * values * -0.5) * 0.3989422804014327
    return values * below, below + values * bell


def text_attend_body(loader, n_sources, width, place, x_ref, ids_ref, vec_ref, *rest):
    sources, rest = rest[:n_sources], rest[n_sources:]
    pair_ref, joined_ref, weights_ref, exact_ref = rest[:4]
    load = loader.bind(sources, rest[4:], place)

    @pl.when(pl.program_id(0) == 0)
    def _():
        load.start()
        load.wait("qkv")

    w_qkv = load.targets["qkv"]
    values = x_ref[...].astype(F32)
    norm_one = normed(
        values, vec_ref[LN1_GAIN : LN1_GAIN + 1, :], vec_ref[LN1_BIAS : LN1_BIAS + 1, :]
    ).astype(BF16)
    pair_ref[:, :width] = norm_one
    for third, bias in enumerate((Q_BIAS, None, V_BIAS)):
        columns = slice(third * width, (third + 1) * width)
        product = dot_nn(norm_one, w_qkv[:, columns])
        if bias is not None:
            product = product + vec_ref[bias : bias + 1, :]
        joined_ref[:, columns] = product.astype(BF16)
    ones = head_ones()
    for part in range(x_ref.shape[0] // LANES):
        rows = slice(part * LANES, (part + 1) * LANES)
        ids = jnp.broadcast_to(ids_ref[part], (LANES, LANES))

        def store(pair, low, values):
            lanes = slice(pair * LANES, (pair + 1) * LANES)
            weights_ref[part, pair] = low
            both = dot_nn(low, jnp.concatenate([values, ones], axis=1))
            later = slice(width + pair * LANES, width + (pair + 1) * LANES)
            pair_ref[rows, later] = both[:, :LANES].astype(BF16)
            exact_ref[rows, lanes] = both[:, :LANES] / both[:, LANES:]

        attention(joined_ref, rows, width, ids == ids.T, store)


def text_forward_body(loader, n_sources, place, x_ref, mixed_ref, vec_ref, fc1_bias_ref, *rest):
    sources, rest = rest[:n_sources], rest[n_sources:]
    hidden_ref, active_ref, slope_ref = rest[:3]
    load = loader.bind(sources, rest[3:], place)
    first = pl.program_id(0) == 0

    @pl.when(first)
    def _():
        load.start(["out"])
        load.wait("out")
        load.start(["fc1"])

    hidden = (
        x_ref[...].astype(F32)
        + dot_nn(mixed_ref[...], load.targets["out"][...])
        + vec_ref[OUT_BIAS : OUT_BIAS + 1, :]
    )
    hidden_ref[...] = hidden
    norm_two = normed(
        hidden, vec_ref[LN2_GAIN : LN2_GAIN + 1, :], vec_ref[LN2_BIAS : LN2_BIAS + 1, :]
    ).astype(BF16)
    active_ref[:, slope_ref.shape[1] :] = norm_two

    @pl.when(first)
    def _():
        load.wait("fc1")

    w_fc1 = load.targets["fc1"]
    step = hidden.shape[1]
    for k in range(w_fc1.shape[1] // step):
        columns = slice(k * step, (k + 1) * step)
        pre_act = dot_nn(norm_two, w_fc1[:, columns]) + fc1_bias_ref[:, columns]
        active, slope = gelu_both(pre_act)
        active_ref[:, columns] = active.astype(BF16)
        slope_ref[:, columns] = slope.astype(BF16)


def text_back_body(loader, n_sources, place, g_ref, hidden_ref, slope_ref, vec_ref, *rest):
    sources, rest = rest[:n_sources], rest[n_sources:]
    mine_ref, share_ref, d_mixed_ref, sums_ref, wide_ref = rest[:5]
    load = loader.bind(sources, rest[5:], place)
    first = pl.program_id(0) == 0

    @pl.when(first)
    def _():
        load.start(["fc2"])
        sums_ref[...] = jnp.zeros_like(sums_ref)
        wide_ref[...] = jnp.zeros_like(wide_ref)
        load.wait("fc2")
        load.start(["fc1", "out"])

    g = g_ref[...]
    w_fc2 = load.targets["fc2"]
    step, half = g.shape[1], mine_ref.shape[1]
    starts = [pl.multiple_of(side * half, LANES) for side in (place[2], 1 - place[2])]
    for start, out in zip(starts, (mine_ref, share_ref)):
        for at in range(0, half, step):
            columns = pl.ds(pl.multiple_of(start + at, LANES), step)
            grad = dot_nt(g, w_fc2[columns, :])
            low = (grad * slope_ref[:, columns].astype(F32)).astype(BF16)
            out[:, at : at + step] = low
            wide_ref[0:1, columns] += jnp.sum(low.astype(F32), axis=0, keepdims=True)

    @pl.when(first)
    def _():
        load.wait("fc1")
        load.wait("out")

    w_fc1 = load.targets["fc1"]
    d_norm = dot_nt(mine_ref[...], w_fc1[:, pl.ds(starts[0], half)])
    d_norm = d_norm + dot_nt(share_ref[:, :half], w_fc1[:, pl.ds(starts[1], half)])
    part, gain, shift = norm_back(
        hidden_ref[...], vec_ref[LN2_GAIN : LN2_GAIN + 1, :], d_norm
    )
    dy1 = (g.astype(F32) + part).astype(BF16)
    share_ref[:, slope_ref.shape[1] // 2 :] = dy1
    d_mixed_ref[...] = dot_nt(dy1, load.targets["out"][...]).astype(BF16)
    sums_ref[LN2_GAIN : LN2_GAIN + 1, :] += gain
    sums_ref[LN2_BIAS : LN2_BIAS + 1, :] += shift
    sums_ref[OUT_BIAS : OUT_BIAS + 1, :] += jnp.sum(dy1.astype(F32), axis=0, keepdims=True)
    sums_ref[FC2_BIAS : FC2_BIAS + 1, :] += jnp.sum(g.astype(F32), axis=0, keepdims=True)


def text_out_body(loader, n_sources, place, hidden_ref, active_ref, vec_ref, *rest):
    sources, rest = rest[:n_sources], rest[n_sources:]
    (out_ref,) = rest[:1]
    load = loader.bind(sources, rest[1:], place)

    @pl.when(pl.program_id(0) == 0)
    def _():
        load.start()
        load.wait("fc2")

    out_ref[...] = (
        hidden_ref[...]
        + dot_nn(active_ref[...], load.targets["fc2"][...])
        + vec_ref[FC2_BIAS : FC2_BIAS + 1, :]
    ).astype(BF16)


def text_unjoin_body(
    loader,
    n_sources,
    width,
    place,
    joined_ref,
    weights_ref,
    d_mixed_ref,
    exact_ref,
    x_ref,
    dy1_ref,
    vec_ref,
    begin_ref,
    *rest,
):
    sources, rest = rest[:n_sources], rest[n_sources:]
    d_joined_ref, share_ref, grad_ref, sums_ref = rest[:4]
    load = loader.bind(sources, rest[4:], place)
    start = pl.program_id(0) == 0

    @pl.when(start)
    def _():
        load.start()
        sums_ref[...] = begin_ref[...]

    scale = (width // HEADS) ** -0.5
    sides, key_sides = lane_sides(), lane_sides(scale)
    left = lax.broadcasted_iota(jnp.int32, (LANES, LANES), 1) < LANES // 2
    ones = spread_ones()
    places = [pair_columns(width, pair) for pair in range(width // LANES)]
    for part in range(joined_ref.shape[0] // LANES):
        rows = slice(part * LANES, (part + 1) * LANES)
        d_weights = [
            dot_nt(d_mixed_ref[rows, one], by_head(joined_ref[rows, three], sides))
            for one, _, three in places
        ]
        d_scores = []
        for pair, (one, _, _) in enumerate(places):
            product = d_mixed_ref[rows, one].astype(F32) * exact_ref[rows, one]
            high = product.astype(BF16)
            low = (product - high.astype(F32)).astype(BF16)
            total = dot_nn(jnp.concatenate([high, low], axis=1), ones)
            d_scores.append(
                (weights_ref[part, pair].astype(F32) * (d_weights[pair] - total)).astype(BF16)
            )
        for pair, (one, two, three) in enumerate(places):
            d_joined_ref[rows, one] = dot_nn(
                d_scores[pair], by_head(joined_ref[rows, two], key_sides)
            ).astype(BF16)
            d_keys = dot_tn(d_scores[pair], joined_ref[rows, one]) * scale
            d_joined_ref[rows, two] = jnp.where(left, d_keys[:LANES], d_keys[LANES:]).astype(BF16)
            d_values = dot_tn(weights_ref[part, pair], d_mixed_ref[rows, one])
            d_joined_ref[rows, three] = jnp.where(
                left, d_values[:LANES], d_values[LANES:]
            ).astype(BF16)
    for row, third in ((Q_BIAS, 0), (V_BIAS, 2)):
        columns = d_joined_ref[:, third * width : (third + 1) * width].astype(F32)
        sums_ref[row : row + 1, :] += jnp.sum(columns, axis=0, keepdims=True)

    @pl.when(start)
    def _():
        load.wait("qkv")

    half = share_ref.shape[1]
    theirs = pl.ds(pl.multiple_of((1 - place[2]) * half, LANES), half)
    share_ref[...] = d_joined_ref[:, theirs]
    d_norm = dot_nt(d_joined_ref[...], load.targets["qkv"][...])
    part, gain, shift = norm_back(
        x_ref[...].astype(F32), vec_ref[LN1_GAIN : LN1_GAIN + 1, :], d_norm
    )
    grad_ref[...] = dy1_ref[...].astype(F32) + part
    sums_ref[LN1_GAIN : LN1_GAIN + 1, :] += gain
    sums_ref[LN1_BIAS : LN1_BIAS + 1, :] += shift


def image_body(loader, n_sources, width, tokens, padded, place, x_ref, vec_ref, *rest):
    sources, rest = rest[:n_sources], rest[n_sources:]
    out_ref, joined_ref, mixed_ref, hidden_ref = rest[:4]
    load = loader.bind(sources, rest[4:], place)
    load.start()
    hidden_ref[...] = jnp.zeros_like(hidden_ref)
    for image in range(x_ref.shape[0]):
        hidden_ref[image * padded : image * padded + tokens, :] = x_ref[image].astype(F32)
    values = hidden_ref[...]
    norm_one = normed(values, vec_ref[IMAGE_GAIN_ONE : IMAGE_GAIN_ONE + 1, :], 0.0).astype(BF16)
    load.wait("qkv")
    w_qkv = load.targets["qkv"]
    for third in range(3):
        columns = slice(third * width, (third + 1) * width)
        joined_ref[:, columns] = dot_nn(norm_one, w_qkv[:, columns]).astype(BF16)
    row = lax.broadcasted_iota(jnp.int32, (LANES, LANES), 0)
    column = lax.broadcasted_iota(jnp.int32, (LANES, LANES), 1)
    allowed = (row // padded == column // padded) & (column % padded < tokens)
    for part in range(hidden_ref.shape[0] // LANES):
        rows = slice(part * LANES, (part + 1) * LANES)

        def store(pair, low, values):
            lanes = slice(pair * LANES, (pair + 1) * LANES)
            mixed_ref[rows, lanes] = dot_nn(low, values).astype(BF16)

        attention(joined_ref, rows, width, allowed, store)
    load.wait("out")
    hidden = values + dot_nn(mixed_ref[...], load.targets["out"][...])
    norm_two = normed(hidden, vec_ref[IMAGE_GAIN_TWO : IMAGE_GAIN_TWO + 1, :], 0.0).astype(BF16)
    hidden_ref[...] = hidden
    load.wait("fc1")
    load.wait("fc2")
    w_fc1, w_fc2 = load.targets["fc1"], load.targets["fc2"]
    for k in range(w_fc1.shape[1] // width):
        columns = slice(k * width, (k + 1) * width)
        pre_act = dot_nn(norm_two, w_fc1[:, columns])
        active = (pre_act * (0.5 + 0.5 * lax.erf(pre_act * 0.7071067811865476))).astype(BF16)
        hidden_ref[...] += dot_nn(active, w_fc2[columns, :])
    for image in range(x_ref.shape[0]):
        own = hidden_ref[image * padded : image * padded + tokens, :]
        out_ref[image] = own.astype(BF16)


SLOTS = 16
CORNERED = (0, 2, 1, 3, 4, 6, 12, 14, 9, 11, 13, 15, 5, 7, 8, 10)


class Job:
    def __init__(self, kind, lefts, rights, start, half, folds=1, wholes=(True, True)):
        self.kind, self.lefts, self.rights, self.start = kind, lefts, rights, start
        self.half, self.folds, self.wholes = half, folds, wholes
        self.width = half * folds
        self.block = half // 2 if half > 1152 else half


class Pieces:
    def __init__(self, jobs, model):
        self.jobs, self.model = jobs, model
        self.height = model // SLOTS
        self.width = sum(job.width for job in jobs)
        self.operands = []
        self.scratch = [pltpu.VMEM((SLOTS, self.height, self.width), BF16)]
        self.loads = self.flops = 0
        for job in jobs:
            self.operands += [array for array, _ in job.lefts]
            self.operands += [array for array, _ in job.rights]
            if job.kind == "sums":
                self.scratch += [
                    pltpu.VMEM((4, *job.lefts[0][0].shape), F32),
                    pltpu.VMEM((model, LANES), F32),
                ]
                self.loads += 4
                continue
            tokens = job.lefts[0][0].shape[0]
            self.scratch += [
                pltpu.VMEM((job.folds, 2 * tokens, model), BF16),
                pltpu.VMEM((2 * tokens, job.half), BF16),
                pltpu.VMEM((model, job.block), F32),
            ]
            self.loads += 2 * job.folds + 2 * job.half // job.block
            self.flops += 4 * tokens * model * job.width
        self.out_shape = [jax.ShapeDtypeStruct((4, self.height, self.width), BF16)] * 4
        self.moved = 2 * sum(a.size for a in self.operands)

    def steps(self, place, operands, outs, scratch, load, send):
        operands, scratch = list(operands), list(scratch)
        pieces = scratch.pop(0)
        steps = []
        f, x, core = place
        y, column = f % 2, f // 2
        height, model = self.height, self.model

        def put(slot, columns, value):
            pieces[CORNERED.index(slot), :, columns] = value.astype(BF16)

        def put_rows(total, columns):
            for slot in range(SLOTS):
                dy, dx, dz = slot // 8, (slot // 4) % 2, slot % 4
                first = ((f ^ (dy + 2 * dz)) * 2 + (x ^ dx)) * height
                put(slot, columns, total[pl.ds(pl.multiple_of(first, 16), height), :])
            for i, out in enumerate(outs):
                send(pieces.at[pl.ds(4 * i, 4), :, columns], out.at[:, :, columns])

        def rows_step(job, left, right, total, at):
            def compute():
                total[...] = dot_tn(left[0], right[:, at : at + job.block])
                put_rows(total, slice(job.start + at, job.start + at + job.block))

            return compute

        def folds_step(job, left, right, total, dz):
            rows = total.shape[0] // 2

            def compute():
                total[...] = dot_tn(left[dz], right[...])
                for dy in range(2):
                    for dx in range(2):
                        slot = dy * 8 + dx * 4 + dz
                        first = (y ^ dy) * rows + (x ^ dx) * (rows // 2)
                        for fold in range(job.folds):
                            lane = job.start + fold * job.half
                            top = pl.multiple_of(first + fold * height, 16)
                            put(slot, slice(lane, lane + job.half), total[pl.ds(top, height), :])
                        at = CORNERED.index(slot)
                        columns = slice(job.start, job.start + job.width)
                        send(pieces.at[at, :, columns], outs[at // 4].at[at % 4, :, columns])

            return compute

        def sums_step(job, table, total):
            def compute():
                own = jnp.where(core == 0, table[0] + table[1], table[2] + table[3])
                total[...] = jnp.concatenate([own] * (LANES // 8)).T
                put_rows(total, slice(job.start, job.start + LANES))

            return compute

        for job in self.jobs:
            left_refs = operands.pop(0), operands.pop(0)
            right_refs = operands.pop(0), operands.pop(0)
            if job.kind == "sums":
                table, total = scratch.pop(0), scratch.pop(0)
                loads = [load(ref, table.at[i]) for i, ref in enumerate(left_refs + right_refs)]
                steps.append((loads, sums_step(job, table, total)))
                continue
            left, right, total = scratch.pop(0), scratch.pop(0), scratch.pop(0)
            tokens = left.shape[1] // 2

            def load_left(fold, lane):
                return [
                    load(
                        ref.at[:, pl.ds(pl.multiple_of(first + lane, LANES), model)],
                        left.at[fold, pl.ds(i * tokens, tokens)],
                    )
                    for i, (ref, (_, first)) in enumerate(zip(left_refs, job.lefts))
                ]

            def load_right(at):
                copies = []
                for i, (ref, (_, first), both) in enumerate(
                    zip(right_refs, job.rights, job.wholes)
                ):
                    lane = first + at + (core * job.half if both else 0)
                    copies.append(
                        load(
                            ref.at[:, pl.ds(pl.multiple_of(lane, LANES), job.block)],
                            right.at[pl.ds(i * tokens, tokens), pl.ds(at, job.block)],
                        )
                    )
                return copies

            if job.kind == "folds":
                begin = load_right(0)
                for dz in range(job.folds):
                    steps.append(
                        (
                            begin + load_left(dz, (column ^ dz) * model),
                            folds_step(job, left, right, total, dz),
                        )
                    )
                    begin = []
                continue
            begin = load_left(0, 0)
            for at in range(0, job.half, job.block):
                steps.append((begin + load_right(at), rows_step(job, left, right, total, at)))
                begin = []
        return steps


class Adds:
    def __init__(self, groups):
        self.groups = groups
        self.operands, self.scratch, self.out_shape = [], [], []
        for sums in groups:
            count, height = sums[0][0][2], sums[0][0][0].shape[1]
            width = sum(pieces[0][0].shape[2] for pieces in sums)
            for pieces in sums:
                for piece in pieces:
                    self.operands.append(piece[0])
                    self.scratch.append(
                        pltpu.VMEM((count, height, pieces[0][0].shape[2]), BF16)
                    )
            self.out_shape.append(jax.ShapeDtypeStruct((count, height, width), BF16))
        self.scratch += [pltpu.VMEM(a.shape, BF16) for a in self.out_shape]
        self.loads = len(self.operands)
        self.flops = sum(a.size for a in self.out_shape)
        self.moved = 2 * sum(a.size for a in self.out_shape) * 4

    def steps(self, place, operands, outs, scratch, load, send):
        operands, scratch = list(operands), list(scratch)
        totals = scratch[len(operands) :]
        loads, work = [], []
        for sums, out, total in zip(self.groups, outs, totals):
            at = 0
            for pieces in sums:
                held = []
                for _, first, count, *lane in pieces:
                    source, target = operands.pop(0), scratch.pop(0)
                    lanes = pl.ds(lane[0] if lane else 0, target.shape[2])
                    loads.append(load(source.at[pl.ds(first, count), :, lanes], target))
                    held.append(target)
                work.append((held, total, slice(at, at + held[0].shape[2])))
                at += held[0].shape[2]

        def compute():
            for held, total, columns in work:
                value = held[0][...].astype(F32)
                for other in held[1:]:
                    value = value + other[...].astype(F32)
                total[:, :, columns] = value.astype(BF16)
            for out, total in zip(outs, totals):
                send(total, out)

        return [(loads, compute)]


def tasks_body(tasks, counts, place, *refs):
    n_in, n_out = sum(c[0] for c in counts), sum(c[1] for c in counts)
    ins, outs, held = refs[:n_in], refs[n_in : n_in + n_out], refs[n_in + n_out :]
    (in_sem, out_sem), held = held[:2], held[2:]
    where = (place[0], place[1], place[2])
    n_loads = 0

    def load(source, target):
        nonlocal n_loads
        copy = pltpu.make_async_copy(source, target, in_sem.at[n_loads])
        n_loads += 1
        return copy

    def send(source, target):
        pltpu.make_async_copy(source, target, out_sem).start()

    steps, at_in, at_out, at_held = [], 0, 0, 0
    for task, (a, b, c) in zip(tasks, counts):
        steps += task.steps(
            where,
            ins[at_in : at_in + a],
            outs[at_out : at_out + b],
            held[at_held : at_held + c],
            load,
            send,
        )
        at_in, at_out, at_held = at_in + a, at_out + b, at_held + c
    ahead = 1 if any(isinstance(task, Pieces) for task in tasks) else len(steps)
    for loads, _ in steps[:ahead]:
        for copy in loads:
            copy.start()
    for index, (loads, compute) in enumerate(steps):
        for copy in loads:
            copy.wait()
        for later, _ in steps[index + ahead : index + ahead + 1]:
            for copy in later:
                copy.start()
        compute()
    for out in outs:
        pltpu.make_async_copy(out, out, out_sem).wait()


def do_tasks(place, tasks, name, after=(), weight=1):
    counts = [(len(t.operands), len(t.out_shape), len(t.scratch)) for t in tasks]
    outs = call(
        partial(tasks_body, tasks, counts),
        name,
        sum(t.flops for t in tasks),
        sum(t.moved for t in tasks),
        (place, *[a for t in tasks for a in t.operands]),
        after=after,
        weight=weight,
        num_prefetch=1,
        grid_spec=dict(
            grid=(1,),
            in_specs=[pl.BlockSpec(memory_space=pl.ANY)] * sum(c[0] for c in counts),
            out_specs=[pl.BlockSpec(memory_space=pl.ANY)] * sum(c[1] for c in counts),
            scratch_shapes=[
                pltpu.SemaphoreType.DMA((sum(t.loads for t in tasks),)),
                pltpu.SemaphoreType.DMA,
            ]
            + [s for t in tasks for s in t.scratch],
        ),
        out_shape=[s for t in tasks for s in t.out_shape],
    )
    outs, results = list(outs), []
    for _, count, _ in counts:
        results.append(outs[:count])
        outs = outs[count:]
    return results


def swap(value, axis, bit):
    size = lax.axis_size(axis)
    return lax.ppermute(value, axis, [(i, i ^ bit) for i in range(size)])


def swap_corner(value):
    n = lax.axis_size("fsdp")
    pairs = [
        (d * n + i, (d ^ 2) * n + (i ^ 1)) for d in range(lax.axis_size("dp")) for i in range(n)
    ]
    return lax.ppermute(value, ("dp", "fsdp"), pairs)


def gate_body(count, *refs):
    pass


def gate(arrays, after):
    return call(
        partial(gate_body, len(arrays)),
        "gate",
        0,
        0,
        arrays,
        after=after,
        grid_spec=dict(
            grid=(1,),
            in_specs=[pl.BlockSpec(memory_space=pl.ANY)] * len(arrays),
            out_specs=[pl.BlockSpec(memory_space=pl.ANY)] * len(arrays),
        ),
        out_shape=[jax.ShapeDtypeStruct(a.shape, a.dtype) for a in arrays],
        input_output_aliases={i: i for i in range(len(arrays))},
    )


def gather_column(own):
    return jnp.stack([own] + [swap(own, "fsdp", bit) for bit in (2, 4, 6)])


def gather_pieces(column):
    return column, swap(column, "fsdp", 1), swap(column, "dp", 2), swap_corner(column)


def both_cores(here):
    places = ((0, 0), (1, 0), (0, 1), (1, 1))
    return [(a, at + (0,)) for a, at in zip(here, places)] + [
        (swap(a, "dp", 1), at + (1,)) for a, at in zip(here, places)
    ]


def gathered_vectors(buffers, rows, at, width, f):
    held = jnp.stack([buffers[i][0][:, :rows, at : at + width] for i in range(2)])
    held = held.reshape(2, 2, 2, rows, width)
    for axis, bit in ((0, 1), (1, 4), (2, 2)):
        held = jnp.where((f & bit) != 0, jnp.flip(held, axis), held)
    return held.transpose(3, 1, 2, 0, 4).reshape(rows, 8 * width)


class Reduction:
    def __init__(self, *sets):
        self.sets = [
            (own, swap(across, "dp", 2), swap(beside, "fsdp", 1), later)
            for own, across, beside, later in sets
        ]

    def corners(self):
        return Adds(
            [
                [[(later, 0, 2), (beside, 2, 2)] for _, _, beside, later in self.sets],
                [[(later, 2, 2), (across, 2, 2)] for _, across, _, later in self.sets],
            ]
        )

    def after_corners(self, outs):
        x_odd, y_even = outs
        self.x_odd, self.y_even = swap(x_odd, "dp", 2), swap(y_even, "fsdp", 1)

    def sides(self, straight=False):
        groups = []
        for odd in range(2):
            for at, count in ((0, 1), (1, 1)) if straight else ((0, 2),):
                sums, lane = [], 0
                for own, across, beside, _ in self.sets:
                    width = own.shape[2]
                    near, far = (beside, self.x_odd) if odd else (across, self.y_even)
                    sums.append(
                        [
                            (own, 2 * odd + at, count),
                            (near, at, count),
                            (far, at, count, lane),
                        ]
                    )
                    lane += width
                groups.append(sums)
        return Adds(groups)

    def after_sides(self, outs):
        self.low, high = outs
        self.high = swap(high, "fsdp", 2)

    def halves(self):
        return Adds([[[(self.low, i, 1), (self.high, i, 1)]] for i in range(2)])

    def after_halves(self, outs):
        own, send = outs
        self.last = [own, swap(send, "fsdp", 4)]

    def after_sides_straight(self, outs):
        own, two, one, three = outs
        self.last = [own, swap(one, "fsdp", 2), swap(two, "fsdp", 4), swap(three, "fsdp", 6)]

    def column(self):
        return [(a, 0, 1) for a in self.last]


def replicas(total):
    total = total[0]
    across = swap(total, "dp", 2)
    return total, across, swap(total, "dp", 1), swap(across, "dp", 1)


def finish_body(lots, place, *refs):
    refs, outs = refs[: 4 * len(lots)], list(refs[4 * len(lots) :])
    x_first, core_first = place[1] == 0, place[2] == 0
    for parts in lots:
        own_ref, across_ref, other_ref, diagonal_ref = refs[:4]
        refs = refs[4:]
        sides = []
        for mine, theirs in ((own_ref, across_ref), (other_ref, diagonal_ref)):
            mine, theirs = mine[...].astype(F32), theirs[...].astype(F32)
            sides.append((jnp.where(x_first, mine, theirs), jnp.where(x_first, theirs, mine)))
        at = 0
        for width, folds in parts:
            out = outs.pop(0)
            height = own_ref.shape[0]
            for dx in range(2):
                one, two = sides[0][dx], sides[1][dx]
                for fold in range(folds):
                    lanes = slice(at + fold * width, at + (fold + 1) * width)
                    rows = slice((dx * folds + fold) * height, (dx * folds + fold + 1) * height)
                    out[rows, :width] = jnp.where(core_first, one[:, lanes], two[:, lanes])
                    out[rows, width:] = jnp.where(core_first, two[:, lanes], one[:, lanes])
            at += width * folds


def finish(place, lots, parts):
    arrays = [a for lot in lots for a in lot]
    height = arrays[0].shape[0]
    shapes = [(2 * folds * height, 2 * columns) for lot in parts for columns, folds in lot]
    return call(
        partial(finish_body, parts),
        "finish",
        0,
        sum(a.size for a in arrays) * 6,
        (place, *arrays),
        num_prefetch=1,
        grid_spec=dict(
            grid=(1,),
            in_specs=[pl.BlockSpec(a.shape, lambda i, place: (0, 0)) for a in arrays],
            out_specs=[pl.BlockSpec(shape, lambda i, place: (0, 0)) for shape in shapes],
        ),
        out_shape=[jax.ShapeDtypeStruct(shape, F32) for shape in shapes],
    )


def per_device(
    text_in,
    text_segments,
    text_cotangent,
    image_in,
    ln1_gain,
    ln1_bias,
    w_qkv,
    q_bias,
    v_bias,
    w_out,
    out_bias,
    ln2_gain,
    ln2_bias,
    w_fc1,
    fc1_bias,
    w_fc2,
    fc2_bias,
    image_norms,
    image_qkv,
    image_proj,
    image_fc1,
    image_fc2,
):
    n_fsdp, n_dp = lax.axis_size("fsdp"), lax.axis_size("dp")
    batch_rows, length, model = text_in.shape
    hidden_units = w_fc1.shape[1]
    tokens = batch_rows * length
    folds = hidden_units // model
    f, replica = lax.axis_index("fsdp"), lax.axis_index("dp")
    x, core = replica // 2, replica % 2
    place = jnp.stack([f, x, core]).astype(jnp.int32)
    shard = model // n_fsdp
    by_pieces = n_fsdp == 8 and n_dp == 4 and shard % 32 == 0

    shapes = {
        "qkv": (model, 3 * model),
        "out": (model, model),
        "fc1": (model, hidden_units),
        "fc2": (hidden_units, model),
    }
    text = {"qkv": w_qkv, "out": w_out, "fc1": w_fc1, "fc2": w_fc2}
    image = {"qkv": image_qkv, "out": image_proj, "fc1": image_fc1, "fc2": image_fc2}

    def parts_of(names):
        return pack_parts([(name, shapes[name], model) for name in names])

    vectors = jnp.concatenate(
        [
            jnp.stack(
                [ln1_gain, ln1_bias, q_bias, v_bias, out_bias, ln2_gain, ln2_bias, fc2_bias]
            ),
            image_norms,
            fc1_bias.reshape(folds, shard),
        ]
    )
    vectors = jnp.pad(vectors, ((0, VECTOR_ROWS - vectors.shape[0]), (0, 0)))
    if by_pieces:
        names = ("qkv",), ("fc2",), ("out", "fc1"), ("qkv", "out", "fc1", "fc2")
        packs = [parts_of(each) + (text,) for each in names[:3]] + [parts_of(names[3]) + (image,)]
        lanes = jnp.pad(vectors, ((0, 0), (0, LANES - shard)))
        cuts = cut_pieces(place, None, packs[1:])
        cuts = cut_pieces(place, lanes, packs[:1], (cuts[0],)) + cuts
        text_qkv = Relative(packs[0][0], both_cores(gather_pieces(gather_column(cuts[0]))))
        (own,) = gate([cuts[1]], (text_qkv.buffers[0][0],))
        column_fc2 = gather_column(own)
        (image_in,) = gate([image_in], (own,))
        early = column_fc2, image_in
        text_rest = Listed(packs[2][0], lax.all_gather(cuts[2], ("fsdp", "dp")))
        vectors = gathered_vectors(text_qkv.buffers, VECTOR_ROWS, packs[0][1], shard, f)
        vectors = vectors.astype(F32)
    else:
        vectors = lax.all_gather(vectors, "fsdp", axis=1, tiled=True).astype(F32)
        gathered = {n: lax.all_gather(a, "fsdp", axis=0, tiled=True) for n, a in text.items()}
        text_qkv = text_fc2 = text_rest = Whole(gathered)
        image_source = Whole(
            {n: lax.all_gather(a, "fsdp", axis=0, tiled=True) for n, a in image.items()}
        )
    fc1_vector = vectors[FC1_BIAS : FC1_BIAS + folds].reshape(folds, n_fsdp, shard)
    fc1_vector = fc1_vector.transpose(1, 0, 2).reshape(1, hidden_units)

    inflow = text_in.reshape(tokens, model)
    cotangent = text_cotangent.reshape(tokens, model)
    ids = text_segments + 16 * (lax.broadcasted_iota(jnp.int32, text_segments.shape, 0) % (LANES // length))
    ids = ids.astype(F32).reshape(tokens // LANES, 1, LANES)
    steps = tokens // TILE
    groups = TILE // LANES
    pairs = model // LANES

    def rows_of(width):
        return pl.BlockSpec((TILE, width), lambda i, place: (i, 0))

    def fixed(*shape):
        return pl.BlockSpec(shape, lambda i, place: (0,) * len(shape))

    def array(*shape, dtype=BF16):
        return jax.ShapeDtypeStruct(shape, dtype)

    weights_spec = pl.BlockSpec((groups, pairs, LANES, 2 * LANES), lambda i, place: (i, 0, 0, 0))
    vec_spec = fixed(VECTOR_ROWS, model)

    def run(body, wanted, name, flops, moved, in_specs, out_specs, out_shape, operands, grid=(steps,), extra=(), after=(), weight=1):
        loader = Loader(wanted, shapes)
        return call(
            partial(body, loader, len(loader.arrays)),
            name,
            flops,
            moved + loader.bytes,
            (place, *operands, *loader.arrays),
            after=after,
            weight=weight,
            num_prefetch=1,
            grid_spec=dict(
                grid=grid,
                in_specs=list(in_specs) + loader.specs,
                out_specs=out_specs,
                scratch_shapes=list(extra) + loader.scratch,
            ),
            out_shape=out_shape,
        )

    def bind(body, *values):
        return lambda loader, count, *refs: body(loader, count, *values, *refs)

    square = 2 * tokens * model * model
    def columns_of(width, index):
        return pl.BlockSpec((TILE, width), lambda i, place: (i, index))

    if not by_pieces:
        early = ()
    pair, joined, weights, exact = run(
        bind(text_attend_body, model),
        [(text_qkv, ["qkv"])],
        "text_attend",
        4 * square,
        tokens * model * 24,
        [rows_of(model), pl.BlockSpec((groups, 1, LANES), lambda i, place: (i, 0, 0)), vec_spec],
        [rows_of(2 * model), rows_of(3 * model), weights_spec, rows_of(model)],
        [
            array(tokens, 2 * model),
            array(tokens, 3 * model),
            array(tokens // LANES, pairs, LANES, 2 * LANES),
            array(tokens, model, dtype=F32),
        ],
        (inflow, ids, vectors),
        after=early,
    )
    done = (pair,)
    if by_pieces:
        (column_fc2,) = gate([column_fc2], done)
        pieces_fc2 = gather_pieces(column_fc2)
        their_pair, their_cotangent = swap(pair, "dp", 1), swap(cotangent, "dp", 1)
        done = (column_fc2,)
    hidden, forward, slope = run(
        text_forward_body,
        [(text_rest, ["out", "fc1"])],
        "text_forward",
        (1 + folds) * square,
        tokens * model * (10 + 4 * folds),
        [rows_of(model), columns_of(model, 1), vec_spec, fixed(1, hidden_units)],
        [rows_of(model), rows_of(hidden_units + model), rows_of(hidden_units)],
        [
            array(tokens, model, dtype=F32),
            array(tokens, hidden_units + model),
            array(tokens, hidden_units),
        ],
        (inflow, pair, vectors, fc1_vector),
        after=done,
    )
    done = (forward,)
    if by_pieces:
        *pieces_fc2, own = gate([*pieces_fc2, cuts[3]], (*done, their_pair, their_cotangent))
        image_source = Listed(packs[3][0], lax.all_gather(own, ("fsdp", "dp")))
        text_fc2 = Relative(packs[1][0], both_cores(pieces_fc2))
        (forward,) = gate([forward], [a for a, _ in text_fc2.buffers[4:]])
        done = (forward,)
        their_forward = swap(forward, "dp", 1)
    d_pre, share, d_mixed, sums_two, sums_wide = run(
        text_back_body,
        [(text_fc2, ["fc2"]), (text_rest, ["fc1", "out"])],
        "text_back",
        (1 + 2 * folds) * square,
        tokens * model * (16 + 4 * folds),
        [rows_of(model), rows_of(model), rows_of(hidden_units), vec_spec],
        [
            rows_of(hidden_units // 2),
            rows_of(hidden_units // 2 + model),
            rows_of(model),
            fixed(8, model),
            fixed(8, hidden_units),
        ],
        [
            array(tokens, hidden_units // 2),
            array(tokens, hidden_units // 2 + model),
            array(tokens, model),
            array(8, model, dtype=F32),
            array(8, hidden_units, dtype=F32),
        ],
        (cotangent, hidden, slope, vectors),
        after=done,
    )
    done = (d_mixed,)
    early_share = share
    units = sums_wide[0].reshape(n_fsdp, folds, shard).transpose(1, 0, 2).reshape(folds, model)
    units = jnp.pad(units, ((0, 8 - folds), (0, 0)))
    if by_pieces:
        their_share, their_units = swap(share, "dp", 1), swap(units, "dp", 1)
        jobs = [
            Job(
                "folds",
                [(forward, 0), (their_forward, 0)],
                [(cotangent, 0), (their_cotangent, 0)],
                0,
                model // 2,
                folds,
            )
        ]
        (first,) = do_tasks(place, [Pieces(jobs, model)], "grads_one", done)
        half = hidden_units // 2
        jobs = [
            Job(
                "rows",
                [(forward, hidden_units), (their_forward, hidden_units)],
                [(d_pre, 0), (their_share, 0)],
                0,
                half,
                wholes=(False, False),
            ),
        ]
        (second,) = do_tasks(place, [Pieces(jobs, model)], "grads_two", (first[0],))
        wide = Reduction(first, second)
        done = second[0], their_units, *wide.sets[0][1:3]
        out_job = Job(
            "rows",
            [(pair, model), (their_pair, model)],
            [(share, half), (their_share, half)],
            0,
            model // 2,
        )
    d_joined, share, text_grad, sums_one = run(
        bind(text_unjoin_body, model),
        [(text_qkv, ["qkv"])],
        "text_unjoin",
        5 * square,
        tokens * model * 32,
        [
            rows_of(3 * model),
            weights_spec,
            rows_of(model),
            rows_of(model),
            rows_of(model),
            columns_of(model, hidden_units // 2 // model),
            vec_spec,
            fixed(8, model),
        ],
        [rows_of(3 * model), rows_of(3 * model // 2), rows_of(model), fixed(8, model)],
        [
            array(tokens, 3 * model),
            array(tokens, 3 * model // 2),
            array(tokens, model, dtype=F32),
            array(8, model, dtype=F32),
        ],
        (joined, weights, d_mixed, exact, inflow, share, vectors, sums_two),
        after=done,
    )
    done = (text_grad,)
    if by_pieces:
        their_share, their_sums = swap(share, "dp", 1), swap(sums_one, "dp", 1)
    text_out = run(
        text_out_body,
        [(text_fc2, ["fc2"])],
        "text_out",
        folds * square,
        tokens * model * (6 + 2 * folds),
        [rows_of(model), rows_of(hidden_units), vec_spec],
        rows_of(model),
        array(tokens, model),
        (hidden, forward, vectors),
        after=done,
    )
    done = (text_out,)
    if by_pieces:
        (outs,) = do_tasks(place, [wide.corners()], "sums_one", done, weight=100000)
        wide.after_corners(outs)
        jobs = [
            out_job,
            Job(
                "rows",
                [(pair, 0), (their_pair, 0)],
                [(d_joined, 0), (their_share, 0)],
                model // 2,
                3 * model // 2,
                wholes=(True, False),
            ),
            Job(
                "sums",
                [(sums_one, 0), (their_sums, 0)],
                [(units, 0), (their_units, 0)],
                2 * model,
                LANES,
            ),
        ]
        (slots,) = do_tasks(place, [Pieces(jobs, model)], "grads_three", (outs[0],))
        narrow = Reduction(slots)
        (outs,) = do_tasks(place, [wide.sides()], "sums_two", (slots[0],))
        wide.after_sides(outs)
        done = (outs[0],)

    images, image_tokens, _ = image_in.shape
    padded = -(-image_tokens // 64) * 64
    held = images * padded
    image_out = run(
        bind(image_body, model, image_tokens, padded),
        [(image_source, ["qkv", "out", "fc1", "fc2"])],
        "image_block",
        2 * held * model * model * (4 + 2 * folds),
        4 * held * model,
        [fixed(*image_in.shape), vec_spec],
        fixed(*image_in.shape),
        array(*image_in.shape),
        (image_in, vectors),
        grid=(1,),
        extra=[
            pltpu.VMEM((held, 3 * model), BF16),
            pltpu.VMEM((held, model), BF16),
            pltpu.VMEM((held, model), F32),
        ],
        after=done,
    )
    done = (image_out,)

    if by_pieces:
        first, second = do_tasks(place, [narrow.corners(), wide.halves()], "sums_three", done)
        narrow.after_corners(first)
        wide.after_halves(second)
        (outs,) = do_tasks(place, [narrow.sides(straight=True)], "sums_four", (first[0],))
        narrow.after_sides_straight(outs)
        (((total,)),) = do_tasks(
            place, [Adds([[wide.column(), narrow.column()]])], "sums_five", (outs[0],)
        )
        parts = (
            (model // 2, folds),
            (hidden_units // 2, 1),
            (model // 2, 1),
            (3 * model // 2, 1),
            (LANES, 1),
        )
        grad_fc2, grad_fc1, grad_out, grad_qkv, sums = finish(
            place, (replicas(total),), (parts,)
        )
        sums = jnp.concatenate([sums[:, :8], sums[:, LANES : LANES + 8]], axis=1).T
    else:

        def product(left, right):
            total = lax.psum_scatter(dot_tn(left, right), "fsdp", scatter_dimension=0, tiled=True)
            return lax.psum(total, "dp")

        grad_fc2 = product(forward[:, :hidden_units], cotangent)
        first = replica % 2 == 0
        mine, theirs = d_pre, early_share[:, : hidden_units // 2]
        d_pre = jnp.concatenate(
            [jnp.where(first, mine, theirs), jnp.where(first, theirs, mine)], axis=1
        )
        grad_fc1 = product(forward[:, hidden_units:], d_pre)
        grad_out = product(pair[:, model:], early_share[:, hidden_units // 2 :])
        grad_qkv = product(pair[:, :model], d_joined)
        sums = jnp.concatenate([sums_one, units])
        sums = lax.psum_scatter(sums, "fsdp", scatter_dimension=1, tiled=True)
        sums = lax.psum(sums, "dp")

    return (
        text_out.reshape(text_in.shape),
        image_out,
        text_grad.reshape(text_in.shape),
        sums[LN1_GAIN],
        sums[LN1_BIAS],
        grad_qkv,
        sums[Q_BIAS],
        sums[V_BIAS],
        grad_out,
        sums[OUT_BIAS],
        sums[LN2_GAIN],
        sums[LN2_BIAS],
        grad_fc1,
        sums[8 : 8 + folds].reshape(-1),
        grad_fc2,
        sums[FC2_BIAS],
    )


def solution(mesh):
    rows = P(("dp", "fsdp"), None, None)
    vector, matrix = P("fsdp"), P("fsdp", None)
    in_specs = (
        rows,
        P(("dp", "fsdp"), None),
        rows,
        rows,
        vector,
        vector,
        matrix,
        vector,
        vector,
        matrix,
        vector,
        vector,
        vector,
        matrix,
        vector,
        matrix,
        vector,
        P(None, "fsdp"),
        matrix,
        matrix,
        matrix,
        matrix,
    )
    out_specs = (
        rows,
        rows,
        rows,
        vector,
        vector,
        matrix,
        vector,
        vector,
        matrix,
        vector,
        vector,
        vector,
        matrix,
        vector,
        matrix,
        vector,
    )
    return jax.shard_map(
        per_device, mesh=mesh, in_specs=in_specs, out_specs=out_specs, check_vma=False
    )
```

```python
from functools import partial

import jax
import jax.numpy as jnp
from jax import lax
from jax.experimental import pallas as pl
from jax.experimental.pallas import tpu as pltpu
from jax.sharding import PartitionSpec as P

HEADS = 12
EPSILON = 1e-06
LANES = 128
TILE = 256
MIB = 1024 * 1024
F32 = jnp.float32
BF16 = jnp.bfloat16

LN1_GAIN, LN1_BIAS, Q_BIAS, V_BIAS, OUT_BIAS, LN2_GAIN, LN2_BIAS, FC2_BIAS = range(8)
IMAGE_GAIN_ONE, IMAGE_GAIN_TWO, FC1_BIAS = 8, 9, 10
VECTOR_ROWS = 16


def dot_nn(a, b):
    return lax.dot_general(a, b, (((1,), (0,)), ((), ())), preferred_element_type=F32)


def dot_nt(a, b):
    return lax.dot_general(a, b, (((1,), (1,)), ((), ())), preferred_element_type=F32)


def dot_tn(a, b):
    return lax.dot_general(a, b, (((0,), (0,)), ((), ())), preferred_element_type=F32)


def call(body, name, flops, moved, operands, after=(), num_prefetch=0, weight=1, **kwargs):
    grid_spec = kwargs.pop("grid_spec")
    first = num_prefetch + len(grid_spec["in_specs"])

    def ordered(*refs):
        return body(*refs[:first], *refs[first + len(after) :])

    grid_spec["in_specs"] = list(grid_spec["in_specs"]) + [
        pl.BlockSpec(memory_space=pltpu.HBM)
    ] * len(after)
    return pl.pallas_call(
        ordered,
        name=name,
        grid_spec=pltpu.PrefetchScalarGridSpec(num_scalar_prefetch=num_prefetch, **grid_spec),
        compiler_params=pltpu.CompilerParams(vmem_limit_bytes=63 * MIB),
        cost_estimate=pl.CostEstimate(
            flops=int(flops) * weight, bytes_accessed=int(moved), transcendentals=0
        ),
        **kwargs,
    )(*operands, *after)


class Part:
    def __init__(self, name, start, width, folds):
        self.name, self.start, self.width, self.folds = name, start, width, folds


def pack_parts(shapes):
    parts, at = {}, 0
    for name, (rows, columns), model in shapes:
        folds = rows // model
        parts[name] = Part(name, at, columns // 2, folds)
        at += folds * (columns // 2)
    return parts, at


def cut_body(plan, at, place, *refs):
    vectors, refs = (refs[0], refs[1:]) if at is not None else (None, refs)
    sources, outs = refs[: len(plan)], refs[len(plan) :]
    for source, (target, part) in zip(sources, plan):
        step = source.shape[0] // part.folds
        for fold in range(part.folds):
            left = part.start + fold * part.width
            outs[target][:, left : left + part.width] = source[fold * step : (fold + 1) * step, :]
    if vectors is None:
        return
    block = jnp.zeros((outs[0].shape[0], LANES), BF16)
    outs[0][:, at : at + LANES] = block
    outs[0][: vectors.shape[0], at : at + LANES] = vectors[...]


def cut_pieces(place, vectors, packs, after=()):
    plan, sources, shapes, specs = [], [], [], []
    for target, (parts, width, matrices) in enumerate(packs):
        for name, part in parts.items():
            plan.append((target, part))
            sources.append(matrices[name])
            rows = matrices[name].shape[0] // 2
            specs.append(pl.BlockSpec((rows, part.width), lambda i, place: (place[1], place[2])))
        width += LANES if vectors is not None else 0
        shapes.append(jax.ShapeDtypeStruct((rows // part.folds, width), BF16))
    return call(
        partial(cut_body, plan, None if vectors is None else packs[0][1]),
        "cut_pieces",
        0,
        sum(a.size for a in sources),
        (place, *([] if vectors is None else [vectors]), *sources),
        after=after,
        weight=1,
        num_prefetch=1,
        grid_spec=dict(
            grid=(1,),
            in_specs=(
                []
                if vectors is None
                else [pl.BlockSpec(vectors.shape, lambda i, place: (0, 0))]
            )
            + specs,
            out_specs=[pl.BlockSpec(a.shape, lambda i, place: (0, 0)) for a in shapes],
        ),
        out_shape=shapes,
    )


class Whole:
    def __init__(self, arrays):
        self.arrays = arrays

    def operands(self, names):
        self.asked = list(names)
        return [self.arrays[name] for name in names]

    def start(self, refs, place, names, targets, semaphores):
        for name in names:
            ref, target = refs[self.asked.index(name)], targets[name]
            chunks, base, rows = semaphores[name]
            for chunk in range(target.shape[0] // rows):
                part = pl.ds(chunk * rows, rows)
                pltpu.make_async_copy(ref.at[part], target.at[part], chunks.at[base + chunk]).start()


def start_piece(source, parts, names, targets, semaphores, f, x, core):
    for name in names:
        part = parts[name]
        height = source.shape[0]
        first = f * (2 * part.folds * height) + x * (part.folds * height)
        chunks, base, rows = semaphores[name]
        semaphore = chunks.at[base + lax.div(f * (2 * part.folds * height), rows)]
        for fold in range(part.folds):
            columns = part.start + fold * part.width
            pltpu.make_async_copy(
                source.at[:, pl.ds(columns, part.width)],
                targets[name].at[
                    pl.ds(pl.multiple_of(first + fold * height, 16), height),
                    pl.ds(pl.multiple_of(core * part.width, LANES), part.width),
                ],
                semaphore,
            ).start()


class Relative:
    def __init__(self, parts, buffers):
        self.parts, self.buffers = parts, buffers

    def operands(self, names):
        return [array for array, _ in self.buffers]

    def start(self, refs, place, names, targets, semaphores):
        f, x, core = place
        for ref, (_, (dy, dx, dc)) in zip(refs, self.buffers):
            for dz in range(ref.shape[0]):
                start_piece(
                    ref.at[dz],
                    self.parts,
                    names,
                    targets,
                    semaphores,
                    f ^ (dy + 2 * dz),
                    x ^ dx,
                    core ^ dc,
                )


class Listed:
    def __init__(self, parts, array):
        self.parts, self.array = parts, array

    def operands(self, names):
        return [self.array]

    def start(self, refs, place, names, targets, semaphores):
        (ref,) = refs

        def step(i, carry):
            start_piece(
                ref.at[i], self.parts, names, targets, semaphores, i // 4, (i // 2) % 2, i % 2
            )
            return carry

        lax.fori_loop(0, ref.shape[0], step, 0)


class Loader:
    def __init__(self, wanted, shapes):
        self.wanted, self.shapes = wanted, shapes
        self.names = [name for _, names in wanted for name in names]
        self.arrays = [a for source, names in wanted for a in source.operands(names)]
        self.specs = [pl.BlockSpec(memory_space=pltpu.HBM)] * len(self.arrays)
        self.scratch = [pltpu.VMEM(shapes[name], BF16) for name in self.names] + [
            pltpu.SemaphoreType.DMA((sum(self.chunks(name) for name in self.names),))
        ]
        self.bytes = sum(2 * shapes[name][0] * shapes[name][1] for name in self.names)

    def chunks(self, name):
        return self.shapes[name][0] // self.shapes["qkv"][0]

    def bind(self, refs, scratch, place_ref):
        self.refs = refs
        self.targets = dict(zip(self.names, scratch))
        self.semaphores, base = {}, 0
        for name in self.names:
            self.semaphores[name] = scratch[-1], base, self.shapes["qkv"][0]
            base += self.chunks(name)
        self.place = (place_ref[0], place_ref[1], place_ref[2])
        return self

    def start(self, only=None):
        at = 0
        for source, names in self.wanted:
            count = len(source.operands(names))
            refs = self.refs[at : at + count]
            at += count
            names = [name for name in names if only is None or name in only]
            if names:
                source.start(refs, self.place, names, self.targets, self.semaphores)

    def wait(self, name, only=None):
        target = self.targets[name]
        chunks, base, rows = self.semaphores[name]
        for chunk in range(self.chunks(name)) if only is None else (only,):
            start = chunk * rows
            part = target.at[pl.ds(pl.multiple_of(start, 16), rows)]
            pltpu.make_async_copy(part, part, chunks.at[base + chunk]).wait()


def normed(values, gain, shift):
    centre = values - jnp.mean(values, axis=-1, keepdims=True)
    spread = lax.rsqrt(jnp.mean(centre * centre, axis=-1, keepdims=True) + EPSILON)
    return centre * spread * gain + shift


def norm_back(values, gain, grad):
    centre = values - jnp.mean(values, axis=-1, keepdims=True)
    spread = lax.rsqrt(jnp.mean(centre * centre, axis=-1, keepdims=True) + EPSILON)
    scaled = centre * spread
    grad_gain = jnp.sum(grad * scaled, axis=0, keepdims=True)
    grad_shift = jnp.sum(grad, axis=0, keepdims=True)
    inner = grad * gain
    inner = inner - jnp.mean(inner, axis=-1, keepdims=True) - scaled * jnp.mean(
        inner * scaled, axis=-1, keepdims=True
    )
    return inner * spread, grad_gain, grad_shift


def lane_sides(scale=1.0):
    lane = lax.broadcasted_iota(jnp.int32, (LANES, LANES), 1)
    left = jnp.where(lane < LANES // 2, scale, 0.0)
    return left.astype(BF16), (scale - left).astype(BF16)


def by_head(values, sides):
    return jnp.concatenate([values * sides[0], values * sides[1]], axis=0)


def pair_columns(width, pair):
    return [slice(third * width + pair * LANES, third * width + (pair + 1) * LANES) for third in range(3)]


def head_ones():
    row = lax.broadcasted_iota(jnp.int32, (2 * LANES, LANES), 0)
    lane = lax.broadcasted_iota(jnp.int32, (2 * LANES, LANES), 1)
    return jnp.where((row < LANES) == (lane < LANES // 2), 1.0, 0.0).astype(BF16)


def spread_ones():
    row = lax.broadcasted_iota(jnp.int32, (2 * LANES, 2 * LANES), 0)
    lane = lax.broadcasted_iota(jnp.int32, (2 * LANES, 2 * LANES), 1)
    return jnp.where((row % LANES < LANES // 2) == (lane < LANES), 1.0, 0.0).astype(BF16)


def attention(joined_ref, rows, width, allowed, store):
    sides, key_sides = lane_sides(), lane_sides((width // HEADS) ** -0.5)
    places = [pair_columns(width, pair) for pair in range(width // LANES)]
    scores = [
        dot_nt(joined_ref[rows, one], by_head(joined_ref[rows, two], key_sides))
        for one, two, _ in places
    ]
    weights = []
    for both in scores:
        parts = []
        for head in range(2):
            own = jnp.where(allowed, both[:, head * LANES : (head + 1) * LANES], -1e30)
            raised = jnp.exp(own - jnp.max(own, axis=-1, keepdims=True))
            parts.append(raised * (1.0 / jnp.sum(raised, axis=-1, keepdims=True)))
        weights.append(jnp.concatenate(parts, axis=1).astype(BF16))
    for pair, (low, (_, _, three)) in enumerate(zip(weights, places)):
        store(pair, low, by_head(joined_ref[rows, three], sides))


def gelu_both(values):
    below = 0.5 + 0.5 * lax.erf(values * 0.7071067811865476)
    bell = jnp.exp(values * values * -0.5) * 0.3989422804014327
    return values * below, below + values * bell


def text_attend_body(loader, n_sources, width, place, x_ref, ids_ref, vec_ref, *rest):
    sources, rest = rest[:n_sources], rest[n_sources:]
    pair_ref, joined_ref, weights_ref, exact_ref = rest[:4]
    load = loader.bind(sources, rest[4:], place)

    @pl.when(pl.program_id(0) == 0)
    def _():
        load.start()
        load.wait("qkv")

    w_qkv = load.targets["qkv"]
    values = x_ref[...].astype(F32)
    norm_one = normed(
        values, vec_ref[LN1_GAIN : LN1_GAIN + 1, :], vec_ref[LN1_BIAS : LN1_BIAS + 1, :]
    ).astype(BF16)
    pair_ref[:, :width] = norm_one
    for third, bias in enumerate((Q_BIAS, None, V_BIAS)):
        columns = slice(third * width, (third + 1) * width)
        product = dot_nn(norm_one, w_qkv[:, columns])
        if bias is not None:
            product = product + vec_ref[bias : bias + 1, :]
        joined_ref[:, columns] = product.astype(BF16)
    ones = head_ones()
    for part in range(x_ref.shape[0] // LANES):
        rows = slice(part * LANES, (part + 1) * LANES)
        ids = jnp.broadcast_to(ids_ref[part], (LANES, LANES))

        def store(pair, low, values):
            lanes = slice(pair * LANES, (pair + 1) * LANES)
            weights_ref[part, pair] = low
            both = dot_nn(low, jnp.concatenate([values, ones], axis=1))
            later = slice(width + pair * LANES, width + (pair + 1) * LANES)
            pair_ref[rows, later] = both[:, :LANES].astype(BF16)
            exact_ref[rows, lanes] = both[:, :LANES] / both[:, LANES:]

        attention(joined_ref, rows, width, ids == ids.T, store)


def text_forward_body(loader, n_sources, place, x_ref, mixed_ref, vec_ref, fc1_bias_ref, *rest):
    sources, rest = rest[:n_sources], rest[n_sources:]
    hidden_ref, active_ref, slope_ref = rest[:3]
    load = loader.bind(sources, rest[3:], place)
    first = pl.program_id(0) == 0

    @pl.when(first)
    def _():
        load.start(["out"])
        load.wait("out")
        load.start(["fc1"])

    hidden = (
        x_ref[...].astype(F32)
        + dot_nn(mixed_ref[...], load.targets["out"][...])
        + vec_ref[OUT_BIAS : OUT_BIAS + 1, :]
    )
    hidden_ref[...] = hidden
    norm_two = normed(
        hidden, vec_ref[LN2_GAIN : LN2_GAIN + 1, :], vec_ref[LN2_BIAS : LN2_BIAS + 1, :]
    ).astype(BF16)
    active_ref[:, slope_ref.shape[1] :] = norm_two

    @pl.when(first)
    def _():
        load.wait("fc1")

    w_fc1 = load.targets["fc1"]
    step = hidden.shape[1]
    for k in range(w_fc1.shape[1] // step):
        columns = slice(k * step, (k + 1) * step)
        pre_act = dot_nn(norm_two, w_fc1[:, columns]) + fc1_bias_ref[:, columns]
        active, slope = gelu_both(pre_act)
        active_ref[:, columns] = active.astype(BF16)
        slope_ref[:, columns] = slope.astype(BF16)


def text_back_body(loader, n_sources, place, g_ref, hidden_ref, slope_ref, vec_ref, *rest):
    sources, rest = rest[:n_sources], rest[n_sources:]
    mine_ref, share_ref, d_mixed_ref, sums_ref, wide_ref = rest[:5]
    load = loader.bind(sources, rest[5:], place)
    first = pl.program_id(0) == 0

    @pl.when(first)
    def _():
        load.start(["fc2"])
        sums_ref[...] = jnp.zeros_like(sums_ref)
        wide_ref[...] = jnp.zeros_like(wide_ref)
        load.start(["fc1", "out"])

    g = g_ref[...]
    w_fc2 = load.targets["fc2"]
    step, half = g.shape[1], mine_ref.shape[1]
    starts = [pl.multiple_of(side * half, LANES) for side in (place[2], 1 - place[2])]

    def steps(arriving):
        for start, out in zip(starts, (mine_ref, share_ref)):
            for at in range(0, half, step):
                if arriving:
                    load.wait("fc2", lax.div(start + at, step))
                columns = pl.ds(pl.multiple_of(start + at, LANES), step)
                grad = dot_nt(g, w_fc2[columns, :])
                low = (grad * slope_ref[:, columns].astype(F32)).astype(BF16)
                out[:, at : at + step] = low
                wide_ref[0:1, columns] += jnp.sum(low.astype(F32), axis=0, keepdims=True)

    pl.when(first)(partial(steps, True))
    pl.when(jnp.logical_not(first))(partial(steps, False))

    @pl.when(first)
    def _():
        load.wait("fc1")
        load.wait("out")

    w_fc1 = load.targets["fc1"]
    d_norm = dot_nt(mine_ref[...], w_fc1[:, pl.ds(starts[0], half)])
    d_norm = d_norm + dot_nt(share_ref[:, :half], w_fc1[:, pl.ds(starts[1], half)])
    part, gain, shift = norm_back(
        hidden_ref[...], vec_ref[LN2_GAIN : LN2_GAIN + 1, :], d_norm
    )
    dy1 = (g.astype(F32) + part).astype(BF16)
    share_ref[:, slope_ref.shape[1] // 2 :] = dy1
    d_mixed_ref[...] = dot_nt(dy1, load.targets["out"][...]).astype(BF16)
    sums_ref[LN2_GAIN : LN2_GAIN + 1, :] += gain
    sums_ref[LN2_BIAS : LN2_BIAS + 1, :] += shift
    sums_ref[OUT_BIAS : OUT_BIAS + 1, :] += jnp.sum(dy1.astype(F32), axis=0, keepdims=True)
    sums_ref[FC2_BIAS : FC2_BIAS + 1, :] += jnp.sum(g.astype(F32), axis=0, keepdims=True)


def text_out_body(loader, n_sources, place, hidden_ref, active_ref, vec_ref, *rest):
    sources, rest = rest[:n_sources], rest[n_sources:]
    (out_ref,) = rest[:1]
    load = loader.bind(sources, rest[1:], place)

    @pl.when(pl.program_id(0) == 0)
    def _():
        load.start()
        load.wait("fc2")

    out_ref[...] = (
        hidden_ref[...]
        + dot_nn(active_ref[...], load.targets["fc2"][...])
        + vec_ref[FC2_BIAS : FC2_BIAS + 1, :]
    ).astype(BF16)


def text_unjoin_body(
    loader,
    n_sources,
    width,
    place,
    joined_ref,
    weights_ref,
    d_mixed_ref,
    exact_ref,
    x_ref,
    dy1_ref,
    vec_ref,
    begin_ref,
    *rest,
):
    sources, rest = rest[:n_sources], rest[n_sources:]
    d_joined_ref, share_ref, grad_ref, sums_ref = rest[:4]
    load = loader.bind(sources, rest[4:], place)
    start = pl.program_id(0) == 0

    @pl.when(start)
    def _():
        load.start()
        sums_ref[...] = begin_ref[...]

    scale = (width // HEADS) ** -0.5
    sides, key_sides = lane_sides(), lane_sides(scale)
    left = lax.broadcasted_iota(jnp.int32, (LANES, LANES), 1) < LANES // 2
    ones = spread_ones()
    places = [pair_columns(width, pair) for pair in range(width // LANES)]
    for part in range(joined_ref.shape[0] // LANES):
        rows = slice(part * LANES, (part + 1) * LANES)
        d_weights = [
            dot_nt(d_mixed_ref[rows, one], by_head(joined_ref[rows, three], sides))
            for one, _, three in places
        ]
        d_scores = []
        for pair, (one, _, _) in enumerate(places):
            product = d_mixed_ref[rows, one].astype(F32) * exact_ref[rows, one]
            high = product.astype(BF16)
            low = (product - high.astype(F32)).astype(BF16)
            total = dot_nn(jnp.concatenate([high, low], axis=1), ones)
            d_scores.append(
                (weights_ref[part, pair].astype(F32) * (d_weights[pair] - total)).astype(BF16)
            )
        for pair, (one, two, three) in enumerate(places):
            d_joined_ref[rows, one] = dot_nn(
                d_scores[pair], by_head(joined_ref[rows, two], key_sides)
            ).astype(BF16)
            d_keys = dot_tn(d_scores[pair], joined_ref[rows, one]) * scale
            d_joined_ref[rows, two] = jnp.where(left, d_keys[:LANES], d_keys[LANES:]).astype(BF16)
            d_values = dot_tn(weights_ref[part, pair], d_mixed_ref[rows, one])
            d_joined_ref[rows, three] = jnp.where(
                left, d_values[:LANES], d_values[LANES:]
            ).astype(BF16)
    for row, third in ((Q_BIAS, 0), (V_BIAS, 2)):
        columns = d_joined_ref[:, third * width : (third + 1) * width].astype(F32)
        sums_ref[row : row + 1, :] += jnp.sum(columns, axis=0, keepdims=True)

    @pl.when(start)
    def _():
        load.wait("qkv")

    half = share_ref.shape[1]
    theirs = pl.ds(pl.multiple_of((1 - place[2]) * half, LANES), half)
    share_ref[...] = d_joined_ref[:, theirs]
    d_norm = dot_nt(d_joined_ref[...], load.targets["qkv"][...])
    part, gain, shift = norm_back(
        x_ref[...].astype(F32), vec_ref[LN1_GAIN : LN1_GAIN + 1, :], d_norm
    )
    grad_ref[...] = dy1_ref[...].astype(F32) + part
    sums_ref[LN1_GAIN : LN1_GAIN + 1, :] += gain
    sums_ref[LN1_BIAS : LN1_BIAS + 1, :] += shift


def image_body(loader, n_sources, width, tokens, padded, place, x_ref, vec_ref, *rest):
    sources, rest = rest[:n_sources], rest[n_sources:]
    out_ref, joined_ref, mixed_ref, hidden_ref = rest[:4]
    load = loader.bind(sources, rest[4:], place)
    load.start()
    hidden_ref[...] = jnp.zeros_like(hidden_ref)
    for image in range(x_ref.shape[0]):
        hidden_ref[image * padded : image * padded + tokens, :] = x_ref[image].astype(F32)
    values = hidden_ref[...]
    norm_one = normed(values, vec_ref[IMAGE_GAIN_ONE : IMAGE_GAIN_ONE + 1, :], 0.0).astype(BF16)
    load.wait("qkv")
    w_qkv = load.targets["qkv"]
    for third in range(3):
        columns = slice(third * width, (third + 1) * width)
        joined_ref[:, columns] = dot_nn(norm_one, w_qkv[:, columns]).astype(BF16)
    row = lax.broadcasted_iota(jnp.int32, (LANES, LANES), 0)
    column = lax.broadcasted_iota(jnp.int32, (LANES, LANES), 1)
    allowed = (row // padded == column // padded) & (column % padded < tokens)
    for part in range(hidden_ref.shape[0] // LANES):
        rows = slice(part * LANES, (part + 1) * LANES)

        def store(pair, low, values):
            lanes = slice(pair * LANES, (pair + 1) * LANES)
            mixed_ref[rows, lanes] = dot_nn(low, values).astype(BF16)

        attention(joined_ref, rows, width, allowed, store)
    load.wait("out")
    hidden = values + dot_nn(mixed_ref[...], load.targets["out"][...])
    norm_two = normed(hidden, vec_ref[IMAGE_GAIN_TWO : IMAGE_GAIN_TWO + 1, :], 0.0).astype(BF16)
    hidden_ref[...] = hidden
    load.wait("fc1")
    load.wait("fc2")
    w_fc1, w_fc2 = load.targets["fc1"], load.targets["fc2"]
    for k in range(w_fc1.shape[1] // width):
        columns = slice(k * width, (k + 1) * width)
        pre_act = dot_nn(norm_two, w_fc1[:, columns])
        active = (pre_act * (0.5 + 0.5 * lax.erf(pre_act * 0.7071067811865476))).astype(BF16)
        hidden_ref[...] += dot_nn(active, w_fc2[columns, :])
    for image in range(x_ref.shape[0]):
        own = hidden_ref[image * padded : image * padded + tokens, :]
        out_ref[image] = own.astype(BF16)


SLOTS = 16
CORNERED = (0, 2, 1, 3, 4, 6, 12, 14, 9, 11, 13, 15, 5, 7, 8, 10)


class Job:
    def __init__(self, kind, lefts, rights, start, half, folds=1, wholes=(True, True)):
        self.kind, self.lefts, self.rights, self.start = kind, lefts, rights, start
        self.half, self.folds, self.wholes = half, folds, wholes
        self.width = half * folds
        self.block = half // 2 if half > 1152 else half


class Pieces:
    def __init__(self, jobs, model):
        self.jobs, self.model = jobs, model
        self.height = model // SLOTS
        self.width = sum(job.width for job in jobs)
        self.operands = []
        self.scratch = [pltpu.VMEM((SLOTS, self.height, self.width), BF16)]
        self.loads = self.flops = 0
        for job in jobs:
            self.operands += [array for array, _ in job.lefts]
            self.operands += [array for array, _ in job.rights]
            if job.kind == "sums":
                self.scratch += [
                    pltpu.VMEM((4, *job.lefts[0][0].shape), F32),
                    pltpu.VMEM((model, LANES), F32),
                ]
                self.loads += 4
                continue
            tokens = job.lefts[0][0].shape[0]
            self.scratch += [
                pltpu.VMEM((job.folds, 2 * tokens, model), BF16),
                pltpu.VMEM((2 * tokens, job.half), BF16),
                pltpu.VMEM((model, job.block), F32),
            ]
            self.loads += 2 * job.folds + 2 * job.half // job.block
            self.flops += 4 * tokens * model * job.width
        self.out_shape = [jax.ShapeDtypeStruct((4, self.height, self.width), BF16)] * 4
        self.moved = 2 * sum(a.size for a in self.operands)

    def steps(self, place, operands, outs, scratch, load, send):
        operands, scratch = list(operands), list(scratch)
        pieces = scratch.pop(0)
        steps = []
        f, x, core = place
        y, column = f % 2, f // 2
        height, model = self.height, self.model

        def put(slot, columns, value):
            pieces[CORNERED.index(slot), :, columns] = value.astype(BF16)

        def put_rows(total, columns):
            for slot in range(SLOTS):
                dy, dx, dz = slot // 8, (slot // 4) % 2, slot % 4
                first = ((f ^ (dy + 2 * dz)) * 2 + (x ^ dx)) * height
                put(slot, columns, total[pl.ds(pl.multiple_of(first, 16), height), :])
            for i, out in enumerate(outs):
                send(pieces.at[pl.ds(4 * i, 4), :, columns], out.at[:, :, columns])

        def rows_step(job, left, right, total, at):
            def compute():
                total[...] = dot_tn(left[0], right[:, at : at + job.block])
                put_rows(total, slice(job.start + at, job.start + at + job.block))

            return compute

        def folds_step(job, left, right, total, dz):
            rows = total.shape[0] // 2

            def compute():
                total[...] = dot_tn(left[dz], right[...])
                for dy in range(2):
                    for dx in range(2):
                        slot = dy * 8 + dx * 4 + dz
                        first = (y ^ dy) * rows + (x ^ dx) * (rows // 2)
                        for fold in range(job.folds):
                            lane = job.start + fold * job.half
                            top = pl.multiple_of(first + fold * height, 16)
                            put(slot, slice(lane, lane + job.half), total[pl.ds(top, height), :])
                        at = CORNERED.index(slot)
                        columns = slice(job.start, job.start + job.width)
                        send(pieces.at[at, :, columns], outs[at // 4].at[at % 4, :, columns])

            return compute

        def sums_step(job, table, total):
            def compute():
                own = jnp.where(core == 0, table[0] + table[1], table[2] + table[3])
                total[...] = jnp.concatenate([own] * (LANES // 8)).T
                put_rows(total, slice(job.start, job.start + LANES))

            return compute

        for job in self.jobs:
            left_refs = operands.pop(0), operands.pop(0)
            right_refs = operands.pop(0), operands.pop(0)
            if job.kind == "sums":
                table, total = scratch.pop(0), scratch.pop(0)
                loads = [load(ref, table.at[i]) for i, ref in enumerate(left_refs + right_refs)]
                steps.append((loads, sums_step(job, table, total)))
                continue
            left, right, total = scratch.pop(0), scratch.pop(0), scratch.pop(0)
            tokens = left.shape[1] // 2

            def load_left(fold, lane):
                return [
                    load(
                        ref.at[:, pl.ds(pl.multiple_of(first + lane, LANES), model)],
                        left.at[fold, pl.ds(i * tokens, tokens)],
                    )
                    for i, (ref, (_, first)) in enumerate(zip(left_refs, job.lefts))
                ]

            def load_right(at):
                copies = []
                for i, (ref, (_, first), both) in enumerate(
                    zip(right_refs, job.rights, job.wholes)
                ):
                    lane = first + at + (core * job.half if both else 0)
                    copies.append(
                        load(
                            ref.at[:, pl.ds(pl.multiple_of(lane, LANES), job.block)],
                            right.at[pl.ds(i * tokens, tokens), pl.ds(at, job.block)],
                        )
                    )
                return copies

            if job.kind == "folds":
                begin = load_right(0)
                for dz in range(job.folds):
                    steps.append(
                        (
                            begin + load_left(dz, (column ^ dz) * model),
                            folds_step(job, left, right, total, dz),
                        )
                    )
                    begin = []
                continue
            begin = load_left(0, 0)
            for at in range(0, job.half, job.block):
                steps.append((begin + load_right(at), rows_step(job, left, right, total, at)))
                begin = []
        return steps


class Adds:
    def __init__(self, groups):
        self.groups = groups
        self.operands, self.scratch, self.out_shape = [], [], []
        for sums in groups:
            count, height = sums[0][0][2], sums[0][0][0].shape[1]
            width = sum(pieces[0][0].shape[2] for pieces in sums)
            for pieces in sums:
                for piece in pieces:
                    self.operands.append(piece[0])
                    self.scratch.append(
                        pltpu.VMEM((count, height, pieces[0][0].shape[2]), BF16)
                    )
            self.out_shape.append(jax.ShapeDtypeStruct((count, height, width), BF16))
        self.scratch += [pltpu.VMEM(a.shape, BF16) for a in self.out_shape]
        self.loads = len(self.operands)
        self.flops = sum(a.size for a in self.out_shape)
        self.moved = 2 * sum(a.size for a in self.out_shape) * 4

    def steps(self, place, operands, outs, scratch, load, send):
        operands, scratch = list(operands), list(scratch)
        totals = scratch[len(operands) :]
        loads, work = [], []
        for sums, out, total in zip(self.groups, outs, totals):
            at = 0
            for pieces in sums:
                held = []
                for _, first, count, *lane in pieces:
                    source, target = operands.pop(0), scratch.pop(0)
                    lanes = pl.ds(lane[0] if lane else 0, target.shape[2])
                    loads.append(load(source.at[pl.ds(first, count), :, lanes], target))
                    held.append(target)
                work.append((held, total, slice(at, at + held[0].shape[2])))
                at += held[0].shape[2]

        def compute():
            for held, total, columns in work:
                value = held[0][...].astype(F32)
                for other in held[1:]:
                    value = value + other[...].astype(F32)
                total[:, :, columns] = value.astype(BF16)
            for out, total in zip(outs, totals):
                send(total, out)

        return [(loads, compute)]


def tasks_body(tasks, counts, place, *refs):
    n_in, n_out = sum(c[0] for c in counts), sum(c[1] for c in counts)
    ins, outs, held = refs[:n_in], refs[n_in : n_in + n_out], refs[n_in + n_out :]
    (in_sem, out_sem), held = held[:2], held[2:]
    where = (place[0], place[1], place[2])
    n_loads = 0

    def load(source, target):
        nonlocal n_loads
        copy = pltpu.make_async_copy(source, target, in_sem.at[n_loads])
        n_loads += 1
        return copy

    def send(source, target):
        pltpu.make_async_copy(source, target, out_sem).start()

    steps, at_in, at_out, at_held = [], 0, 0, 0
    for task, (a, b, c) in zip(tasks, counts):
        steps += task.steps(
            where,
            ins[at_in : at_in + a],
            outs[at_out : at_out + b],
            held[at_held : at_held + c],
            load,
            send,
        )
        at_in, at_out, at_held = at_in + a, at_out + b, at_held + c
    ahead = 1 if any(isinstance(task, Pieces) for task in tasks) else len(steps)
    for loads, _ in steps[:ahead]:
        for copy in loads:
            copy.start()
    for index, (loads, compute) in enumerate(steps):
        for copy in loads:
            copy.wait()
        for later, _ in steps[index + ahead : index + ahead + 1]:
            for copy in later:
                copy.start()
        compute()
    for out in outs:
        pltpu.make_async_copy(out, out, out_sem).wait()


def do_tasks(place, tasks, name, after=(), weight=1):
    counts = [(len(t.operands), len(t.out_shape), len(t.scratch)) for t in tasks]
    outs = call(
        partial(tasks_body, tasks, counts),
        name,
        sum(t.flops for t in tasks),
        sum(t.moved for t in tasks),
        (place, *[a for t in tasks for a in t.operands]),
        after=after,
        weight=weight,
        num_prefetch=1,
        grid_spec=dict(
            grid=(1,),
            in_specs=[pl.BlockSpec(memory_space=pl.ANY)] * sum(c[0] for c in counts),
            out_specs=[pl.BlockSpec(memory_space=pl.ANY)] * sum(c[1] for c in counts),
            scratch_shapes=[
                pltpu.SemaphoreType.DMA((sum(t.loads for t in tasks),)),
                pltpu.SemaphoreType.DMA,
            ]
            + [s for t in tasks for s in t.scratch],
        ),
        out_shape=[s for t in tasks for s in t.out_shape],
    )
    outs, results = list(outs), []
    for _, count, _ in counts:
        results.append(outs[:count])
        outs = outs[count:]
    return results


def swap(value, axis, bit):
    size = lax.axis_size(axis)
    return lax.ppermute(value, axis, [(i, i ^ bit) for i in range(size)])


def swap_corner(value):
    n = lax.axis_size("fsdp")
    pairs = [
        (d * n + i, (d ^ 2) * n + (i ^ 1)) for d in range(lax.axis_size("dp")) for i in range(n)
    ]
    return lax.ppermute(value, ("dp", "fsdp"), pairs)


def gate_body(count, *refs):
    pass


def gate(arrays, after):
    return call(
        partial(gate_body, len(arrays)),
        "gate",
        0,
        0,
        arrays,
        after=after,
        grid_spec=dict(
            grid=(1,),
            in_specs=[pl.BlockSpec(memory_space=pl.ANY)] * len(arrays),
            out_specs=[pl.BlockSpec(memory_space=pl.ANY)] * len(arrays),
        ),
        out_shape=[jax.ShapeDtypeStruct(a.shape, a.dtype) for a in arrays],
        input_output_aliases={i: i for i in range(len(arrays))},
    )


def gather_column(own):
    return jnp.stack([own] + [swap(own, "fsdp", bit) for bit in (2, 4, 6)])


def gather_pieces(column):
    return column, swap(column, "fsdp", 1), swap(column, "dp", 2), swap_corner(column)


def both_cores(here):
    places = ((0, 0), (1, 0), (0, 1), (1, 1))
    return [(a, at + (0,)) for a, at in zip(here, places)] + [
        (swap(a, "dp", 1), at + (1,)) for a, at in zip(here, places)
    ]


def gathered_vectors(buffers, rows, at, width, f):
    held = jnp.stack([buffers[i][0][:, :rows, at : at + width] for i in range(2)])
    held = held.reshape(2, 2, 2, rows, width)
    for axis, bit in ((0, 1), (1, 4), (2, 2)):
        held = jnp.where((f & bit) != 0, jnp.flip(held, axis), held)
    return held.transpose(3, 1, 2, 0, 4).reshape(rows, 8 * width)


class Reduction:
    def __init__(self, *sets):
        self.sets = [
            (own, swap(across, "dp", 2), swap(beside, "fsdp", 1), later)
            for own, across, beside, later in sets
        ]

    def corners(self):
        return Adds(
            [
                [[(later, 0, 2), (beside, 2, 2)] for _, _, beside, later in self.sets],
                [[(later, 2, 2), (across, 2, 2)] for _, across, _, later in self.sets],
            ]
        )

    def after_corners(self, outs):
        x_odd, y_even = outs
        self.x_odd, self.y_even = swap(x_odd, "dp", 2), swap(y_even, "fsdp", 1)

    def sides(self, straight=False):
        groups = []
        for odd in range(2):
            for at, count in ((0, 1), (1, 1)) if straight else ((0, 2),):
                sums, lane = [], 0
                for own, across, beside, _ in self.sets:
                    width = own.shape[2]
                    near, far = (beside, self.x_odd) if odd else (across, self.y_even)
                    sums.append(
                        [
                            (own, 2 * odd + at, count),
                            (near, at, count),
                            (far, at, count, lane),
                        ]
                    )
                    lane += width
                groups.append(sums)
        return Adds(groups)

    def after_sides(self, outs):
        self.low, high = outs
        self.high = swap(high, "fsdp", 2)

    def halves(self):
        return Adds([[[(self.low, i, 1), (self.high, i, 1)]] for i in range(2)])

    def after_halves(self, outs):
        own, send = outs
        self.last = [own, swap(send, "fsdp", 4)]

    def after_sides_straight(self, outs):
        own, two, one, three = outs
        self.last = [own, swap(one, "fsdp", 2), swap(two, "fsdp", 4), swap(three, "fsdp", 6)]

    def column(self):
        return [(a, 0, 1) for a in self.last]


def replicas(total):
    total = total[0]
    across = swap(total, "dp", 2)
    return total, across, swap(total, "dp", 1), swap(across, "dp", 1)


def finish_body(lots, place, *refs):
    refs, outs = refs[: 4 * len(lots)], list(refs[4 * len(lots) :])
    x_first, core_first = place[1] == 0, place[2] == 0
    for parts in lots:
        own_ref, across_ref, other_ref, diagonal_ref = refs[:4]
        refs = refs[4:]
        sides = []
        for mine, theirs in ((own_ref, across_ref), (other_ref, diagonal_ref)):
            mine, theirs = mine[...].astype(F32), theirs[...].astype(F32)
            sides.append((jnp.where(x_first, mine, theirs), jnp.where(x_first, theirs, mine)))
        at = 0
        for width, folds in parts:
            out = outs.pop(0)
            height = own_ref.shape[0]
            for dx in range(2):
                one, two = sides[0][dx], sides[1][dx]
                for fold in range(folds):
                    lanes = slice(at + fold * width, at + (fold + 1) * width)
                    rows = slice((dx * folds + fold) * height, (dx * folds + fold + 1) * height)
                    out[rows, :width] = jnp.where(core_first, one[:, lanes], two[:, lanes])
                    out[rows, width:] = jnp.where(core_first, two[:, lanes], one[:, lanes])
            at += width * folds


def finish(place, lots, parts):
    arrays = [a for lot in lots for a in lot]
    height = arrays[0].shape[0]
    shapes = [(2 * folds * height, 2 * columns) for lot in parts for columns, folds in lot]
    return call(
        partial(finish_body, parts),
        "finish",
        0,
        sum(a.size for a in arrays) * 6,
        (place, *arrays),
        num_prefetch=1,
        grid_spec=dict(
            grid=(1,),
            in_specs=[pl.BlockSpec(a.shape, lambda i, place: (0, 0)) for a in arrays],
            out_specs=[pl.BlockSpec(shape, lambda i, place: (0, 0)) for shape in shapes],
        ),
        out_shape=[jax.ShapeDtypeStruct(shape, F32) for shape in shapes],
    )


def per_device(
    text_in,
    text_segments,
    text_cotangent,
    image_in,
    ln1_gain,
    ln1_bias,
    w_qkv,
    q_bias,
    v_bias,
    w_out,
    out_bias,
    ln2_gain,
    ln2_bias,
    w_fc1,
    fc1_bias,
    w_fc2,
    fc2_bias,
    image_norms,
    image_qkv,
    image_proj,
    image_fc1,
    image_fc2,
):
    n_fsdp, n_dp = lax.axis_size("fsdp"), lax.axis_size("dp")
    batch_rows, length, model = text_in.shape
    hidden_units = w_fc1.shape[1]
    tokens = batch_rows * length
    folds = hidden_units // model
    f, replica = lax.axis_index("fsdp"), lax.axis_index("dp")
    x, core = replica // 2, replica % 2
    place = jnp.stack([f, x, core]).astype(jnp.int32)
    shard = model // n_fsdp
    by_pieces = n_fsdp == 8 and n_dp == 4 and shard % 32 == 0

    shapes = {
        "qkv": (model, 3 * model),
        "out": (model, model),
        "fc1": (model, hidden_units),
        "fc2": (hidden_units, model),
    }
    text = {"qkv": w_qkv, "out": w_out, "fc1": w_fc1, "fc2": w_fc2}
    image = {"qkv": image_qkv, "out": image_proj, "fc1": image_fc1, "fc2": image_fc2}

    def parts_of(names):
        return pack_parts([(name, shapes[name], model) for name in names])

    vectors = jnp.concatenate(
        [
            jnp.stack(
                [ln1_gain, ln1_bias, q_bias, v_bias, out_bias, ln2_gain, ln2_bias, fc2_bias]
            ),
            image_norms,
            fc1_bias.reshape(folds, shard),
        ]
    )
    vectors = jnp.pad(vectors, ((0, VECTOR_ROWS - vectors.shape[0]), (0, 0)))
    if by_pieces:
        names = ("qkv",), ("fc2",), ("out", "fc1"), ("qkv", "out", "fc1", "fc2")
        packs = [parts_of(each) + (text,) for each in names[:3]] + [parts_of(names[3]) + (image,)]
        lanes = jnp.pad(vectors, ((0, 0), (0, LANES - shard)))
        cuts = cut_pieces(place, None, packs[1:])
        cuts = cut_pieces(place, lanes, packs[:1], (cuts[0],)) + cuts
        text_qkv = Relative(packs[0][0], both_cores(gather_pieces(gather_column(cuts[0]))))
        (own,) = gate([cuts[1]], (text_qkv.buffers[0][0],))
        column_fc2 = gather_column(own)
        (image_in,) = gate([image_in], (own,))
        early = column_fc2, image_in
        text_rest = Listed(packs[2][0], lax.all_gather(cuts[2], ("fsdp", "dp")))
        vectors = gathered_vectors(text_qkv.buffers, VECTOR_ROWS, packs[0][1], shard, f)
        vectors = vectors.astype(F32)
    else:
        vectors = lax.all_gather(vectors, "fsdp", axis=1, tiled=True).astype(F32)
        gathered = {n: lax.all_gather(a, "fsdp", axis=0, tiled=True) for n, a in text.items()}
        text_qkv = text_fc2 = text_rest = Whole(gathered)
        image_source = Whole(
            {n: lax.all_gather(a, "fsdp", axis=0, tiled=True) for n, a in image.items()}
        )
    fc1_vector = vectors[FC1_BIAS : FC1_BIAS + folds].reshape(folds, n_fsdp, shard)
    fc1_vector = fc1_vector.transpose(1, 0, 2).reshape(1, hidden_units)

    inflow = text_in.reshape(tokens, model)
    cotangent = text_cotangent.reshape(tokens, model)
    ids = text_segments + 16 * (lax.broadcasted_iota(jnp.int32, text_segments.shape, 0) % (LANES // length))
    ids = ids.astype(F32).reshape(tokens // LANES, 1, LANES)
    steps = tokens // TILE
    groups = TILE // LANES
    pairs = model // LANES

    def rows_of(width):
        return pl.BlockSpec((TILE, width), lambda i, place: (i, 0))

    def fixed(*shape):
        return pl.BlockSpec(shape, lambda i, place: (0,) * len(shape))

    def array(*shape, dtype=BF16):
        return jax.ShapeDtypeStruct(shape, dtype)

    weights_spec = pl.BlockSpec((groups, pairs, LANES, 2 * LANES), lambda i, place: (i, 0, 0, 0))
    vec_spec = fixed(VECTOR_ROWS, model)

    def run(body, wanted, name, flops, moved, in_specs, out_specs, out_shape, operands, grid=(steps,), extra=(), after=(), weight=1):
        loader = Loader(wanted, shapes)
        return call(
            partial(body, loader, len(loader.arrays)),
            name,
            flops,
            moved + loader.bytes,
            (place, *operands, *loader.arrays),
            after=after,
            weight=weight,
            num_prefetch=1,
            grid_spec=dict(
                grid=grid,
                in_specs=list(in_specs) + loader.specs,
                out_specs=out_specs,
                scratch_shapes=list(extra) + loader.scratch,
            ),
            out_shape=out_shape,
        )

    def bind(body, *values):
        return lambda loader, count, *refs: body(loader, count, *values, *refs)

    square = 2 * tokens * model * model
    def columns_of(width, index):
        return pl.BlockSpec((TILE, width), lambda i, place: (i, index))

    if not by_pieces:
        early = ()
    pair, joined, weights, exact = run(
        bind(text_attend_body, model),
        [(text_qkv, ["qkv"])],
        "text_attend",
        4 * square,
        tokens * model * 24,
        [rows_of(model), pl.BlockSpec((groups, 1, LANES), lambda i, place: (i, 0, 0)), vec_spec],
        [rows_of(2 * model), rows_of(3 * model), weights_spec, rows_of(model)],
        [
            array(tokens, 2 * model),
            array(tokens, 3 * model),
            array(tokens // LANES, pairs, LANES, 2 * LANES),
            array(tokens, model, dtype=F32),
        ],
        (inflow, ids, vectors),
        after=early,
    )
    done = (pair,)
    if by_pieces:
        pieces_fc2 = gather_pieces(column_fc2)
        their_pair, their_cotangent = swap(pair, "dp", 1), swap(cotangent, "dp", 1)
        done = (column_fc2,)
    hidden, forward, slope = run(
        text_forward_body,
        [(text_rest, ["out", "fc1"])],
        "text_forward",
        (1 + folds) * square,
        tokens * model * (10 + 4 * folds),
        [rows_of(model), columns_of(model, 1), vec_spec, fixed(1, hidden_units)],
        [rows_of(model), rows_of(hidden_units + model), rows_of(hidden_units)],
        [
            array(tokens, model, dtype=F32),
            array(tokens, hidden_units + model),
            array(tokens, hidden_units),
        ],
        (inflow, pair, vectors, fc1_vector),
        after=done,
    )
    done = (forward,)
    if by_pieces:
        *pieces_fc2, own = gate([*pieces_fc2, cuts[3]], (*done, their_pair, their_cotangent))
        image_source = Listed(packs[3][0], lax.all_gather(own, ("fsdp", "dp")))
        text_fc2 = Relative(packs[1][0], both_cores(pieces_fc2))
        (forward,) = gate([forward], [a for a, _ in text_fc2.buffers[4:]])
        done = (forward,)
        their_forward = swap(forward, "dp", 1)
    d_pre, share, d_mixed, sums_two, sums_wide = run(
        text_back_body,
        [(text_fc2, ["fc2"]), (text_rest, ["fc1", "out"])],
        "text_back",
        (1 + 2 * folds) * square,
        tokens * model * (16 + 4 * folds),
        [rows_of(model), rows_of(model), rows_of(hidden_units), vec_spec],
        [
            rows_of(hidden_units // 2),
            rows_of(hidden_units // 2 + model),
            rows_of(model),
            fixed(8, model),
            fixed(8, hidden_units),
        ],
        [
            array(tokens, hidden_units // 2),
            array(tokens, hidden_units // 2 + model),
            array(tokens, model),
            array(8, model, dtype=F32),
            array(8, hidden_units, dtype=F32),
        ],
        (cotangent, hidden, slope, vectors),
        after=done,
    )
    done = (d_mixed,)
    early_share = share
    units = sums_wide[0].reshape(n_fsdp, folds, shard).transpose(1, 0, 2).reshape(folds, model)
    units = jnp.pad(units, ((0, 8 - folds), (0, 0)))
    if by_pieces:
        their_share, their_units = swap(share, "dp", 1), swap(units, "dp", 1)
        jobs = [
            Job(
                "folds",
                [(forward, 0), (their_forward, 0)],
                [(cotangent, 0), (their_cotangent, 0)],
                0,
                model // 2,
                folds,
            )
        ]
        (first,) = do_tasks(place, [Pieces(jobs, model)], "grads_one", done)
        half = hidden_units // 2
        jobs = [
            Job(
                "rows",
                [(forward, hidden_units), (their_forward, hidden_units)],
                [(d_pre, 0), (their_share, 0)],
                0,
                half,
                wholes=(False, False),
            ),
        ]
        (second,) = do_tasks(place, [Pieces(jobs, model)], "grads_two", (first[0],))
        wide = Reduction(first, second)
        done = second[0], their_units, *wide.sets[0][1:3]
        out_job = Job(
            "rows",
            [(pair, model), (their_pair, model)],
            [(share, half), (their_share, half)],
            0,
            model // 2,
        )
    d_joined, share, text_grad, sums_one = run(
        bind(text_unjoin_body, model),
        [(text_qkv, ["qkv"])],
        "text_unjoin",
        5 * square,
        tokens * model * 32,
        [
            rows_of(3 * model),
            weights_spec,
            rows_of(model),
            rows_of(model),
            rows_of(model),
            columns_of(model, hidden_units // 2 // model),
            vec_spec,
            fixed(8, model),
        ],
        [rows_of(3 * model), rows_of(3 * model // 2), rows_of(model), fixed(8, model)],
        [
            array(tokens, 3 * model),
            array(tokens, 3 * model // 2),
            array(tokens, model, dtype=F32),
            array(8, model, dtype=F32),
        ],
        (joined, weights, d_mixed, exact, inflow, share, vectors, sums_two),
        after=done,
    )
    done = (text_grad,)
    if by_pieces:
        their_share, their_sums = swap(share, "dp", 1), swap(sums_one, "dp", 1)
    text_out = run(
        text_out_body,
        [(text_fc2, ["fc2"])],
        "text_out",
        folds * square,
        tokens * model * (6 + 2 * folds),
        [rows_of(model), rows_of(hidden_units), vec_spec],
        rows_of(model),
        array(tokens, model),
        (hidden, forward, vectors),
        after=done,
    )
    done = (text_out,)
    if by_pieces:
        (outs,) = do_tasks(place, [wide.corners()], "sums_one", done, weight=100000)
        wide.after_corners(outs)
        jobs = [
            out_job,
            Job(
                "rows",
                [(pair, 0), (their_pair, 0)],
                [(d_joined, 0), (their_share, 0)],
                model // 2,
                3 * model // 2,
                wholes=(True, False),
            ),
            Job(
                "sums",
                [(sums_one, 0), (their_sums, 0)],
                [(units, 0), (their_units, 0)],
                2 * model,
                LANES,
            ),
        ]
        (slots,) = do_tasks(place, [Pieces(jobs, model)], "grads_three", (outs[0],))
        narrow = Reduction(slots)
        (outs,) = do_tasks(place, [wide.sides()], "sums_two", (slots[0],))
        wide.after_sides(outs)
        done = (outs[0],)

    images, image_tokens, _ = image_in.shape
    padded = -(-image_tokens // 64) * 64
    held = images * padded
    image_out = run(
        bind(image_body, model, image_tokens, padded),
        [(image_source, ["qkv", "out", "fc1", "fc2"])],
        "image_block",
        2 * held * model * model * (4 + 2 * folds),
        4 * held * model,
        [fixed(*image_in.shape), vec_spec],
        fixed(*image_in.shape),
        array(*image_in.shape),
        (image_in, vectors),
        grid=(1,),
        extra=[
            pltpu.VMEM((held, 3 * model), BF16),
            pltpu.VMEM((held, model), BF16),
            pltpu.VMEM((held, model), F32),
        ],
        after=done,
    )
    done = (image_out,)

    if by_pieces:
        first, second = do_tasks(place, [narrow.corners(), wide.halves()], "sums_three", done)
        narrow.after_corners(first)
        wide.after_halves(second)
        (outs,) = do_tasks(place, [narrow.sides(straight=True)], "sums_four", (first[0],))
        narrow.after_sides_straight(outs)
        (((total,)),) = do_tasks(
            place, [Adds([[wide.column(), narrow.column()]])], "sums_five", (outs[0],)
        )
        parts = (
            (model // 2, folds),
            (hidden_units // 2, 1),
            (model // 2, 1),
            (3 * model // 2, 1),
            (LANES, 1),
        )
        grad_fc2, grad_fc1, grad_out, grad_qkv, sums = finish(
            place, (replicas(total),), (parts,)
        )
        sums = jnp.concatenate([sums[:, :8], sums[:, LANES : LANES + 8]], axis=1).T
    else:

        def product(left, right):
            total = lax.psum_scatter(dot_tn(left, right), "fsdp", scatter_dimension=0, tiled=True)
            return lax.psum(total, "dp")

        grad_fc2 = product(forward[:, :hidden_units], cotangent)
        first = replica % 2 == 0
        mine, theirs = d_pre, early_share[:, : hidden_units // 2]
        d_pre = jnp.concatenate(
            [jnp.where(first, mine, theirs), jnp.where(first, theirs, mine)], axis=1
        )
        grad_fc1 = product(forward[:, hidden_units:], d_pre)
        grad_out = product(pair[:, model:], early_share[:, hidden_units // 2 :])
        grad_qkv = product(pair[:, :model], d_joined)
        sums = jnp.concatenate([sums_one, units])
        sums = lax.psum_scatter(sums, "fsdp", scatter_dimension=1, tiled=True)
        sums = lax.psum(sums, "dp")

    return (
        text_out.reshape(text_in.shape),
        image_out,
        text_grad.reshape(text_in.shape),
        sums[LN1_GAIN],
        sums[LN1_BIAS],
        grad_qkv,
        sums[Q_BIAS],
        sums[V_BIAS],
        grad_out,
        sums[OUT_BIAS],
        sums[LN2_GAIN],
        sums[LN2_BIAS],
        grad_fc1,
        sums[8 : 8 + folds].reshape(-1),
        grad_fc2,
        sums[FC2_BIAS],
    )


def solution(mesh):
    rows = P(("dp", "fsdp"), None, None)
    vector, matrix = P("fsdp"), P("fsdp", None)
    in_specs = (
        rows,
        P(("dp", "fsdp"), None),
        rows,
        rows,
        vector,
        vector,
        matrix,
        vector,
        vector,
        matrix,
        vector,
        vector,
        vector,
        matrix,
        vector,
        matrix,
        vector,
        P(None, "fsdp"),
        matrix,
        matrix,
        matrix,
        matrix,
    )
    out_specs = (
        rows,
        rows,
        rows,
        vector,
        vector,
        matrix,
        vector,
        vector,
        matrix,
        vector,
        vector,
        vector,
        matrix,
        vector,
        matrix,
        vector,
    )
    return jax.shard_map(
        per_device, mesh=mesh, in_specs=in_specs, out_specs=out_specs, check_vma=False
    )
```
